32 devices in a mesh: sec: 4 (over y, core), dp: 8 (over z, x), mp: 1.
Axes of the slice: x: 2, y: 2, z: 4, core: 2. Of those that a mesh axis runs over, the one named last changes fastest.
Arguments:
- patches: bfloat16 [320, 5120], P('dp'), may hold values from -6 to 6
- ln_gain: bfloat16 [1280], replicated, may hold values from 0.099609375 to 1.8984375
- ln_shift: bfloat16 [1280], replicated, may hold values from -3 to 3
- w_in: bfloat16 [5120, 5120], P('dp', ('sec', 'mp')), may hold values from -0.078125 to 0.078125
- b_in: bfloat16 [5120], P(('sec', 'mp')), may hold values from -3 to 3
- w_out: bfloat16 [5120, 8192], P(('sec', 'mp'), 'dp'), may hold values from -0.125 to 0.125
- b_out: bfloat16 [8192], P(('sec', 'mp')), may hold values from -3 to 3
- place: int32 [320], P('dp'), may hold values from 0 to 255, as said below
- image_counts: int32 [8], P('dp'), may hold values from 1 to 40, 128 in all
- text_rows: bfloat16 [2048, 8192], P('dp', ('sec', 'mp')), may hold values from -6 to 6
- segments: int32 [8, 256], P('dp'), may hold values from 0 to 3, never falling along the last dimension, each value on 1 to 128 neighbouring positions
- norm_gain: bfloat16 [2, 8192], replicated, may hold values from 0.099609375 to 1.8984375
- q_weight: bfloat16 [2, 8192, 4096], P(None, None, ('sec', 'mp'))
- kv_weight: bfloat16 [2, 2, 512, 8192], P(None, None, ('sec', 'mp'))
- o_weight: bfloat16 [2, 4096, 8192], P(None, ('sec', 'mp')), may hold values from -0.125 to 0.125
- grad_rows: bfloat16 [320, 8192], P('dp'), may hold values from -6 to 6
Outputs:
- final_rows: float32 [2048, 8192], P('dp', ('sec', 'mp'))
- patch_grads: float32 [320, 5120], P('dp')
The draws below stay inside these ranges and needn't reach their ends.
Inputs may be any that keep to these rules, and one draw needn't show every extreme that they name: `place`: each owner's 40 entries are distinct token positions of its own packed sequence; only an owner's first image_counts entries are used. `image_counts`: the counts sum to 8 * (16) over all owners.
All inputs are finite; a program needn't handle non-finite values. No bound on the sum of `image_counts` on one device may be relied on, other than what follows from the above.
Results may differ from the reference program's by a relative error of at most 0.0055.
Values may be sent and summed in bfloat16 or wider, within the bound.
No kernel may reach another device: no remote copies, remote signals or barrier semaphores. Data moves between devices by JAX's collectives and lax.ppermute only.
A program may use at most 256 MiB of HBM per device.

```python
import math
import jax
import jax.numpy as jnp
import numpy as np
from jax import lax

D = 8192
HEADS = 32
KV_HEADS = 4
HEAD_DIM = 128
VIT = 1280
MHID = 5120
LAYERS = 2
DOCS = 4
TOK = 256
MERGE_IN = 5120
CAP = 40
SLOTS = 320
TOKENS = 2048
N_SEC = 4
N_DP = 8
N_MP = 1


def attention_tables(key):
    base = jax.random.fold_in(key, 11)
    key_query, key_keys, key_values = jax.random.split(base, 3)
    fan_scale = D ** (-0.5)
    key_table = jax.random.normal(key_keys, (LAYERS, KV_HEADS * HEAD_DIM, D), jnp.float32) * fan_scale
    value_table = jax.random.normal(key_values, (LAYERS, KV_HEADS * HEAD_DIM, D), jnp.float32) * fan_scale
    query_table = jax.random.normal(key_query, (LAYERS, D, HEADS, HEAD_DIM), jnp.float32) * fan_scale
    return (query_table.reshape(LAYERS, D, HEADS * HEAD_DIM), jnp.stack([key_table, value_table], axis=1))


def draw_q_weight(key, part):
    return attention_tables(key)[0].astype(jnp.bfloat16)


def draw_kv_weight(key, part):
    return attention_tables(key)[1].astype(jnp.bfloat16)


def draw_place(key, part):
    owner_keys = jax.random.split(jax.random.fold_in(key, 23), N_DP)

    def one_owner(owner_key):
        inner = jax.random.permutation(owner_key, TOK - 2)[:CAP - 2] + 1
        edges = jnp.array([0, TOK - 1], dtype=jnp.int32)
        listed = jnp.concatenate([edges, inner.astype(jnp.int32)])
        return jax.random.permutation(jax.random.fold_in(owner_key, 5), listed)
    return jax.vmap(one_owner)(owner_keys).reshape(N_DP * CAP).astype(jnp.int32)


def spiked(values, rng, source, target, blocks, factor):
    def block_of(position):
        return (jnp.arange(values.shape[position]) // (values.shape[position] // blocks)).reshape((-1,) + (1,) * (values.ndim - 1 - position))

    near = jax.random.permutation(rng, blocks)[block_of(target)]
    second = (block_of(target) + blocks // 2) % blocks
    return jnp.where((block_of(source) == near) | (block_of(source) == second), factor * values, values)


def block_levels(key, shape, shards, low, largest):
    level = 1.0
    for position, parts in shards:
        steps = jax.random.uniform(jax.random.fold_in(jax.random.fold_in(key, 6), position), (parts,), jnp.float32, low / len(shards), largest / len(shards))
        level = level * jnp.repeat(jnp.exp(steps), shape[position] // parts).reshape((-1,) + (1,) * (len(shape) - 1 - position))
    return level


def profile(count, total, most, skew):
    portions = [(1 << 20) // math.isqrt(standing ** skew) + 1 for standing in range(2, count + 1)]
    surplus, given = total - most - (count - 1), [1] * (count - 1)
    while surplus > 0:
        candidates = [i for i in range(count - 1) if given[i] < most]
        pool, budget = sum([portions[i] for i in candidates]), surplus
        for i in candidates:
            extra = min(most - given[i], max(1, budget * portions[i] // pool), surplus)
            given[i] = given[i] + extra
            surplus = surplus - extra
    return np.array([most] + given)


def uneven_parts(key, number_of, total, limit, lean):
    if number_of == 2:
        one = jax.random.randint(key, (), max(1, total - limit), min(limit, total - 1) + 1)
        return jnp.stack([one, total - one])
    sizes = jnp.asarray(profile(number_of, total, limit, lean), jnp.int32)
    pairs = (number_of - 1) // 2
    donor, receiver = sizes[1:1 + 2 * pairs:2], sizes[2:2 + 2 * pairs:2]
    margin = jnp.minimum(donor - 1, limit - receiver)
    shifted = jax.random.randint(jax.random.fold_in(key, 1), (pairs,), 0, 1 << 20) % (margin + 1)
    sizes = sizes.at[1:1 + 2 * pairs:2].set(donor - shifted).at[2:2 + 2 * pairs:2].set(receiver + shifted)
    return sizes[jax.random.permutation(jax.random.fold_in(key, 2), number_of)]


def scatter_about(rng, shape, scale, most, cuts=(), kind=jnp.bfloat16):
    loudness = block_levels(rng, shape, cuts, -0.22, 0.18) if cuts else 1.0
    entries = jax.random.normal(rng, shape, jnp.float32) * scale * loudness
    return jnp.minimum(jnp.maximum(entries, -most), most).astype(kind)


def noise_with(own_key, shape, scale, reach, shards, heavy, kind=jnp.bfloat16):
    result = scale * jax.random.normal(own_key, shape, jnp.float32)
    if shards:
        result = result * block_levels(own_key, shape, shards, -0.22, 0.18)
    return jnp.clip(spiked(result, jax.random.fold_in(own_key, 3), *heavy), -reach, reach).astype(kind)


def setup_inputs(seed: int = 0) -> dict:
    streams_of = jax.random.split(jax.random.key(seed), 17)
    return {
        "patches": scatter_about(streams_of[0], (SLOTS, MERGE_IN), 1.0, 6.0, ((0, 8),)),
        "ln_gain": jnp.clip(1.0 + 0.18 * jax.random.normal(streams_of[1], (VIT,), jnp.float32), 0.099609375, 1.8984375).astype(jnp.bfloat16),
        "ln_shift": scatter_about(streams_of[2], (VIT,), 0.5, 3.0),
        "w_in": scatter_about(streams_of[3], (MERGE_IN, MHID), MERGE_IN ** -0.5, 0.078125, ((0, 8), (1, 4))),
        "b_in": scatter_about(streams_of[4], (MHID,), 0.5, 3.0, ((0, 4),)),
        "w_out": noise_with(streams_of[5], (MHID, D), MHID ** -0.5, 0.125, ((0, 4), (1, 8)), (0, 1, 8, 2.0)),
        "b_out": scatter_about(streams_of[6], (D,), 0.5, 3.0, ((0, 4),)),
        "place": draw_place(jax.random.fold_in(streams_of[16], 71), 0),
        "image_counts": uneven_parts(streams_of[8], N_DP, N_DP * (TOK // 16), CAP, 2).astype(jnp.int32),
        "text_rows": scatter_about(streams_of[9], (TOKENS, D), 1.0, 6.0, ((0, 8), (1, 4))),
        "segments": jax.vmap(lambda own: jnp.searchsorted(jnp.cumsum(uneven_parts(own, DOCS, TOK, TOK // 2, 1)), jnp.arange(TOK), side="right"))(jax.random.split(streams_of[10], N_DP)).reshape((N_DP, TOK)).astype(jnp.int32),
        "norm_gain": jnp.clip(1.0 + 0.18 * jax.random.normal(streams_of[11], (LAYERS, D), jnp.float32), 0.099609375, 1.8984375).astype(jnp.bfloat16),
        "q_weight": draw_q_weight(jax.random.fold_in(streams_of[16], 71), 0),
        "kv_weight": draw_kv_weight(jax.random.fold_in(streams_of[16], 71), 0),
        "o_weight": noise_with(streams_of[14], (LAYERS, HEADS * HEAD_DIM, D), (HEADS * HEAD_DIM) ** -0.5, 0.125, ((1, 4),), (1, 2, 4, 2.0)),
        "grad_rows": scatter_about(streams_of[15], (SLOTS, D), 1.0, 6.0, ((0, 8),)),
    }


ln_eps = 1e-06
rms_eps = 1e-06
rope_base = 1000000.0

def group_norm(patch_rows, ln_gain, ln_shift):
    row_count = patch_rows.shape[0]
    grouped = patch_rows.astype(jnp.float32).reshape(row_count, -1, ln_gain.shape[0])
    center = grouped - lax.optimization_barrier(jnp.mean(grouped, axis=-1, keepdims=True))
    spread = lax.optimization_barrier(jnp.mean(center * center, axis=-1, keepdims=True))
    scaled = center * lax.rsqrt(spread + ln_eps) * ln_gain.astype(jnp.float32) + ln_shift.astype(jnp.float32)
    return scaled.reshape(row_count, -1)

def gelu_exact(values):
    return jax.nn.gelu(values, approximate=False)

def rotate(values, positions):
    head_depth = values.shape[-1]
    half_depth = head_depth // 2
    inv_freq = rope_base ** (-2.0 * jnp.arange(half_depth, dtype=jnp.float32) / head_depth)
    angles = positions[:, None] * inv_freq[None, :]
    cosine = jnp.cos(angles)[:, None, :]
    sine_part = jnp.sin(angles)[:, None, :]
    first_half = values[..., :half_depth]
    second = values[..., half_depth:]
    return jnp.concatenate([first_half * cosine - second * sine_part, second * cosine + first_half * sine_part], axis=-1)

def doc_mask(segment_ids):
    token_index = jnp.arange(segment_ids.shape[0], dtype=jnp.int32)
    same_doc = segment_ids[:, None] == segment_ids[None, :]
    allowed = same_doc & (token_index[None, :] <= token_index[:, None])
    positions = lax.optimization_barrier(jnp.sum(allowed.astype(jnp.int32), axis=1)) - 1
    return (allowed, positions.astype(jnp.float32))

def rms_rows(hidden, gain_row):
    values = hidden.astype(jnp.float32)
    factor = lax.rsqrt(lax.optimization_barrier(jnp.mean(values * values, axis=-1, keepdims=True)) + rms_eps)
    return (values * factor * gain_row.astype(jnp.float32)).astype(jnp.bfloat16)

def section(hidden, allowed, positions, gain_row, q_layer, kv_layer, o_layer):
    token_count = hidden.shape[0]
    normed = rms_rows(hidden, gain_row)
    queries = jnp.dot(normed, q_layer, preferred_element_type=jnp.float32).reshape(token_count, HEADS, HEAD_DIM)
    key_rows = lax.dot_general(normed, kv_layer[0], (((1,), (1,)), ((), ())), preferred_element_type=jnp.float32)
    value_rows = lax.dot_general(normed, kv_layer[1], (((1,), (1,)), ((), ())), preferred_element_type=jnp.float32)
    key_rows = key_rows.reshape(token_count, KV_HEADS, HEAD_DIM)
    value_rows = value_rows.reshape(token_count, KV_HEADS, HEAD_DIM)
    queries = rotate(queries, positions).astype(jnp.bfloat16)
    key_rows = rotate(key_rows, positions).astype(jnp.bfloat16)
    value_rows = value_rows.astype(jnp.bfloat16)
    group_size = HEADS // KV_HEADS
    key_heads = jnp.repeat(key_rows, group_size, axis=1)
    value_heads = jnp.repeat(value_rows, group_size, axis=1)
    scores = jnp.einsum('thd,shd->hts', queries.astype(jnp.float32), key_heads.astype(jnp.float32)) * (1.0 / math.sqrt(HEAD_DIM))
    scores = jnp.where(allowed[None], scores, -jnp.inf)
    row_max = lax.optimization_barrier(jnp.max(scores, axis=-1, keepdims=True))
    exp_scores = jnp.exp(scores - row_max)
    attn_weights = (exp_scores / lax.optimization_barrier(jnp.sum(exp_scores, axis=-1, keepdims=True))).astype(jnp.bfloat16)
    attended = jnp.einsum('hts,shd->thd', attn_weights.astype(jnp.float32), value_heads.astype(jnp.float32)).astype(jnp.bfloat16)
    group_count = N_SEC * N_MP
    attended = attended.reshape(token_count, group_count, -1)
    o_groups = o_layer.reshape(group_count, -1, D)
    group_terms = jnp.einsum('tgc,gcd->gtd', attended.astype(jnp.float32), o_groups.astype(jnp.float32))
    return hidden.astype(jnp.float32) + lax.optimization_barrier(jnp.sum(group_terms, axis=0))

def reference(patches, ln_gain, ln_shift, w_in, b_in, w_out, b_out, place, image_counts, text_rows, segments, norm_gain, q_weight, kv_weight, o_weight, grad_rows):
    normed = group_norm(patches, ln_gain, ln_shift).astype(jnp.bfloat16)
    pre_act = jnp.dot(normed, w_in, preferred_element_type=jnp.float32) + b_in.astype(jnp.float32)
    hidden_units = gelu_exact(pre_act).astype(jnp.bfloat16)
    merged = (jnp.dot(hidden_units, w_out, preferred_element_type=jnp.float32) + b_out.astype(jnp.float32)).astype(jnp.bfloat16)
    slot_index = jnp.arange(CAP, dtype=jnp.int32)
    token_index = jnp.arange(TOK, dtype=jnp.int32)
    live_slot = slot_index[None, :] < image_counts[:, None]
    select = (place.reshape(N_DP, CAP)[:, :, None] == token_index[None, None, :]) & live_slot[:, :, None]
    is_image = jnp.any(select, axis=1)
    picked = jnp.einsum('oct,ocd->otd', select.astype(jnp.float32), merged.reshape(N_DP, CAP, D).astype(jnp.float32))
    start_rows = jnp.where(is_image[:, :, None], picked, text_rows.reshape(N_DP, TOK, D).astype(jnp.float32)).astype(jnp.bfloat16)

    def run_owner(owner_args):
        current, segment_ids = owner_args
        current = current.astype(jnp.float32)
        allowed, positions = doc_mask(segment_ids)
        for layer_index in range(LAYERS):
            current = section(current, allowed, positions, norm_gain[layer_index], q_weight[layer_index], kv_weight[layer_index], o_weight[layer_index])
        return current
    final_rows = lax.map(run_owner, (start_rows, segments)).reshape(N_DP * TOK, D)
    slot_grads = jnp.where(live_slot.reshape(N_DP * CAP)[:, None], grad_rows, jnp.zeros_like(grad_rows))
    hidden_grads = lax.dot_general(slot_grads, w_out, (((1,), (1,)), ((), ())), preferred_element_type=jnp.float32)
    _, pull_gelu = jax.vjp(gelu_exact, pre_act)
    pre_grads = pull_gelu(hidden_grads)[0].astype(jnp.bfloat16)
    normed_grads = lax.dot_general(pre_grads, w_in, (((1,), (1,)), ((), ())), preferred_element_type=jnp.float32)
    _, pull_norm = jax.vjp(lambda values: group_norm(values, ln_gain, ln_shift), patches.astype(jnp.float32))
    patch_grads = pull_norm(normed_grads)[0]
    return (final_rows, patch_grads)
```

```python
import math

import jax
import jax.numpy as jnp
from jax import lax
from jax.sharding import PartitionSpec as P

D = 8192
HEAD_DIM = 128


ln_eps = 1e-06
rms_eps = 1e-06
rope_base = 1000000.0


def group_norm(patch_rows, ln_gain, ln_shift):
    row_count = patch_rows.shape[0]
    grouped = patch_rows.astype(jnp.float32).reshape(row_count, -1, ln_gain.shape[0])
    center = grouped - jnp.mean(grouped, axis=-1, keepdims=True)
    spread = jnp.mean(center * center, axis=-1, keepdims=True)
    scaled = center * lax.rsqrt(spread + ln_eps) * ln_gain.astype(jnp.float32) + ln_shift.astype(
        jnp.float32
    )
    return scaled.reshape(row_count, -1)


def gelu_exact(values):
    return jax.nn.gelu(values, approximate=False)


def rotate(values, positions):
    head_depth = values.shape[-1]
    half_depth = head_depth // 2
    inv_freq = rope_base ** (-2.0 * jnp.arange(half_depth, dtype=jnp.float32) / head_depth)
    angles = positions[:, None] * inv_freq[None, :]
    cosine = jnp.cos(angles)[:, None, :]
    sine_part = jnp.sin(angles)[:, None, :]
    first_half = values[..., :half_depth]
    second = values[..., half_depth:]
    return jnp.concatenate(
        [first_half * cosine - second * sine_part, second * cosine + first_half * sine_part],
        axis=-1,
    )


def doc_mask(segment_ids):
    token_index = jnp.arange(segment_ids.shape[0], dtype=jnp.int32)
    same_doc = segment_ids[:, None] == segment_ids[None, :]
    allowed = same_doc & (token_index[None, :] <= token_index[:, None])
    positions = jnp.sum(allowed.astype(jnp.int32), axis=1) - 1
    return (allowed, positions.astype(jnp.float32))


def attend(normed, allowed, positions, q_local, kv_local):
    token_count = normed.shape[0]
    queries = jnp.dot(normed, q_local, preferred_element_type=jnp.float32).reshape(
        token_count, -1, HEAD_DIM
    )
    key_value = jnp.einsum("td,kcd->tkc", normed, kv_local, preferred_element_type=jnp.float32)
    key_value = lax.all_gather(key_value, "mp", axis=2, tiled=True)
    key_rows = rotate(key_value[:, 0:1, :], positions)[:, 0, :].astype(jnp.bfloat16)
    value_rows = key_value[:, 1, :].astype(jnp.bfloat16)
    queries = rotate(queries, positions).astype(jnp.bfloat16)
    scores = jnp.einsum("thd,sd->hts", queries, key_rows, preferred_element_type=jnp.float32) * (
        1.0 / math.sqrt(HEAD_DIM)
    )
    scores = jnp.where(allowed[None], scores, -jnp.inf)
    row_max = jnp.max(scores, axis=-1, keepdims=True)
    exp_scores = jnp.exp(scores - row_max)
    attn_weights = (exp_scores / jnp.sum(exp_scores, axis=-1, keepdims=True)).astype(jnp.bfloat16)
    attended = jnp.einsum(
        "hts,sd->thd", attn_weights, value_rows, preferred_element_type=jnp.float32
    )
    return attended.astype(jnp.bfloat16).reshape(token_count, -1)


def gather_features(rows_local):
    return lax.all_gather(rows_local, ("sec", "mp"), axis=1, tiled=True)


def section_features(rows_local, gain_row, allowed, positions, q_local, kv_local, o_local):
    share = rows_local.shape[1]
    square_sums = lax.psum(jnp.sum(rows_local * rows_local, axis=1), ("sec", "mp"))
    factor = lax.rsqrt(square_sums / D + rms_eps)
    gain_local = lax.dynamic_slice_in_dim(
        gain_row, lax.axis_index(("sec", "mp")) * share, share, 0
    ).astype(jnp.float32)
    normed_local = (rows_local * factor[:, None] * gain_local[None, :]).astype(jnp.bfloat16)
    normed = gather_features(normed_local)
    attended = attend(normed, allowed, positions, q_local, kv_local)
    summed = lax.psum_scatter(
        lax.dot_general(
            o_local, attended, (((0,), (1,)), ((), ())), preferred_element_type=jnp.float32
        ),
        ("sec", "mp"),
        scatter_dimension=0,
        tiled=True,
    )
    return rows_local + summed.T


def swap(values, axis, mask):
    size = lax.axis_size(axis)
    return lax.ppermute(values, axis, [(i, i ^ mask) for i in range(size)])


def spread_rows(values, parts):
    return lax.all_to_all(values, "dp", split_axis=0, concat_axis=0, tiled=True).reshape(
        (parts, -1) + values.shape[1:]
    )


def merger(patches, ln_gain, ln_shift, w_in, b_in, w_out, live_slot, count, grad_rows, packed_rows):
    owners = lax.axis_size("dp")
    group = lax.axis_size(("sec", "mp"))
    slots = patches.shape[0]
    in_share, hidden_share = w_in.shape
    out_share = w_out.shape[1]
    share = in_share + out_share

    normed = group_norm(patches, ln_gain, ln_shift).astype(jnp.bfloat16)
    slot_grads = jnp.where(live_slot[:, None], grad_rows, jnp.zeros_like(grad_rows))
    rows = jnp.concatenate(
        [normed.reshape(slots, owners, in_share), slot_grads.reshape(slots, owners, out_share)],
        axis=2,
    ).transpose(1, 0, 2)
    count_rows = jnp.broadcast_to(count.astype(jnp.bfloat16), (owners, 8, share))
    received = lax.all_to_all(
        jnp.concatenate([rows, count_rows], axis=1), "dp", split_axis=0, concat_axis=0, tiled=True
    )
    counts = received[:, slots, 0].astype(jnp.int32)
    owner_index = jnp.arange(owners, dtype=jnp.int32)
    offsets = jnp.sum(jnp.where(owner_index[None, :] < owner_index[:, None], counts[None, :], 0), axis=1)
    slot_index = jnp.arange(slots, dtype=jnp.int32)
    target = jnp.where(
        slot_index[None, :] < counts[:, None], offsets[:, None] + slot_index[None, :], -1
    ).reshape(-1)
    pack = (jnp.arange(packed_rows, dtype=jnp.int32)[:, None] == target[None, :]).astype(jnp.bfloat16)
    packed = jnp.dot(
        pack, received[:, :slots].reshape(owners * slots, share), preferred_element_type=jnp.float32
    ).astype(jnp.bfloat16)

    pre_part = jnp.dot(packed[:, :in_share], w_in, preferred_element_type=jnp.float32)
    grad_part = lax.dot_general(
        packed[:, in_share:], w_out, (((1,), (1,)), ((), ())), preferred_element_type=jnp.float32
    )
    parts = jnp.concatenate([pre_part, grad_part], axis=1).astype(jnp.bfloat16)
    chunk = packed_rows // owners
    parts = lax.all_to_all(
        parts.reshape(owners, chunk, 2 * hidden_share), "dp", split_axis=0, concat_axis=0, tiled=True
    )
    sums = jnp.sum(parts.astype(jnp.float32), axis=0)
    pre_act = sums[:, :hidden_share] + b_in.astype(jnp.float32)
    hidden_units, pull_gelu = jax.vjp(gelu_exact, pre_act)
    pre_grads = pull_gelu(sums[:, hidden_share:])[0]
    both = jnp.concatenate([hidden_units, pre_grads], axis=1).astype(jnp.bfloat16)
    both = lax.all_to_all(
        jnp.broadcast_to(both[None], (owners, chunk, 2 * hidden_share)),
        "dp",
        split_axis=0,
        concat_axis=0,
        tiled=True,
    ).reshape(packed_rows, 2 * hidden_share)
    merged_part = jnp.dot(both[:, :hidden_share], w_out, preferred_element_type=jnp.float32)
    back_part = lax.dot_general(
        both[:, hidden_share:], w_in, (((1,), (1,)), ((), ())), preferred_element_type=jnp.float32
    )
    tail = jnp.concatenate(
        [
            merged_part.astype(jnp.bfloat16).reshape(packed_rows, group, out_share // group),
            back_part.astype(jnp.bfloat16).reshape(packed_rows, group, in_share // group),
        ],
        axis=2,
    ).reshape(packed_rows, group * (share // group))
    tail = lax.dot_general(
        pack, tail, (((0,), (0,)), ((), ())), preferred_element_type=jnp.float32
    ).astype(jnp.bfloat16)
    tail = tail.reshape(owners * slots, group, share // group).transpose(1, 0, 2)
    me = lax.axis_index(("sec", "mp"))
    parts_now = tail.astype(jnp.float32)
    index = jnp.arange(group, dtype=jnp.int32) ^ me
    parts_now = jnp.take(parts_now, index, axis=0)
    mask = 1
    while mask < group:
        pairs = parts_now.reshape(-1, 2, owners * slots, share // group)
        received = swap(pairs[:, 1].astype(jnp.bfloat16), ("sec", "mp"), mask)
        parts_now = pairs[:, 0] + received.astype(jnp.float32)
        mask *= 2
    mine = parts_now.reshape(owners, slots, share // group).astype(jnp.bfloat16)
    mine = lax.all_to_all(mine, "dp", split_axis=0, concat_axis=0, tiled=True)
    gathered = mine[None]
    mask = group // 2
    while mask >= 1:
        gathered = jnp.concatenate([gathered, swap(gathered, ("sec", "mp"), mask)], axis=0)
        mask //= 2
    order = [0]
    mask = group // 2
    while mask >= 1:
        order = order + [i ^ mask for i in order]
        mask //= 2
    place_of = [0] * group
    for where_now, relative in enumerate(order):
        place_of[relative] = where_now
    gathered = jnp.take(gathered, jnp.asarray(place_of, jnp.int32)[index], axis=0)
    gathered = gathered.transpose(2, 1, 0, 3)
    merged = gathered[..., : out_share // group].reshape(slots, owners * out_share)
    normed_grads = gathered[..., out_share // group :].reshape(slots, owners * in_share)
    _, pull_norm = jax.vjp(
        lambda values: group_norm(values, ln_gain, ln_shift), patches.astype(jnp.float32)
    )
    return merged, pull_norm(normed_grads.astype(jnp.float32))[0]


def local(
    patches,
    ln_gain,
    ln_shift,
    w_in,
    b_in,
    w_out,
    b_out,
    place,
    image_counts,
    text_rows,
    segments,
    norm_gain,
    q_weight,
    kv_weight,
    o_weight,
    grad_rows,
):
    slot_count = patches.shape[0]
    tokens, share = text_rows.shape
    slot_index = jnp.arange(slot_count, dtype=jnp.int32)
    live_slot = slot_index < image_counts[0]
    merged, patch_grads = merger(
        patches,
        ln_gain,
        ln_shift,
        w_in,
        b_in,
        w_out,
        live_slot,
        image_counts[0],
        grad_rows,
        lax.axis_size("dp") * (tokens // 16),
    )
    merged_local = lax.dynamic_slice_in_dim(
        merged, lax.axis_index(("sec", "mp")) * share, share, 1
    ).astype(jnp.float32)
    merged_local = (merged_local + b_out.astype(jnp.float32)).astype(jnp.bfloat16)
    token_index = jnp.arange(tokens, dtype=jnp.int32)
    select = (place[:, None] == token_index[None, :]) & live_slot[:, None]
    is_image = jnp.any(select, axis=0)
    picked = lax.dot_general(
        select.astype(jnp.bfloat16),
        merged_local,
        (((0,), (0,)), ((), ())),
        preferred_element_type=jnp.float32,
    )
    start_rows = jnp.where(is_image[:, None], picked, text_rows.astype(jnp.float32)).astype(
        jnp.bfloat16
    )
    allowed, positions = doc_mask(segments[0])
    layer_count = q_weight.shape[0]
    current = start_rows.astype(jnp.float32)
    for layer_index in range(layer_count):
        current = section_features(
            current,
            norm_gain[layer_index],
            allowed,
            positions,
            q_weight[layer_index],
            kv_weight[layer_index],
            o_weight[layer_index],
        )
    return (current, patch_grads)


def solution(mesh):
    in_specs = (
        P("dp", None),
        P(),
        P(),
        P("dp", ("sec", "mp")),
        P(("sec", "mp")),
        P(("sec", "mp"), "dp"),
        P(("sec", "mp")),
        P("dp"),
        P("dp"),
        P("dp", ("sec", "mp")),
        P("dp", None),
        P(),
        P(None, None, ("sec", "mp")),
        P(None, None, ("sec", "mp"), None),
        P(None, ("sec", "mp"), None),
        P("dp", None),
    )
    out_specs = (P("dp", ("sec", "mp")), P("dp", None))
    return jax.shard_map(local, mesh=mesh, in_specs=in_specs, out_specs=out_specs, check_vma=False)
```

```python
import math

import jax
import jax.numpy as jnp
from jax import lax
from jax.experimental import pallas as pl
from jax.experimental.pallas import tpu as pltpu
from jax.sharding import PartitionSpec as P

D = 8192
HEAD_DIM = 128


ln_eps = 1e-06
rms_eps = 1e-06
rope_base = 1000000.0


def group_norm(patch_rows, ln_gain, ln_shift):
    row_count = patch_rows.shape[0]
    grouped = patch_rows.astype(jnp.float32).reshape(row_count, -1, ln_gain.shape[0])
    center = grouped - jnp.mean(grouped, axis=-1, keepdims=True)
    spread = jnp.mean(center * center, axis=-1, keepdims=True)
    scaled = center * lax.rsqrt(spread + ln_eps) * ln_gain.astype(jnp.float32) + ln_shift.astype(
        jnp.float32
    )
    return scaled.reshape(row_count, -1)


def gelu_exact(values):
    return jax.nn.gelu(values, approximate=False)


def rotate(values, positions):
    head_depth = values.shape[-1]
    half_depth = head_depth // 2
    inv_freq = rope_base ** (-2.0 * jnp.arange(half_depth, dtype=jnp.float32) / head_depth)
    angles = positions[:, None] * inv_freq[None, :]
    cosine = jnp.cos(angles)[:, None, :]
    sine_part = jnp.sin(angles)[:, None, :]
    first_half = values[..., :half_depth]
    second = values[..., half_depth:]
    return jnp.concatenate(
        [first_half * cosine - second * sine_part, second * cosine + first_half * sine_part],
        axis=-1,
    )


def doc_mask(segment_ids):
    token_index = jnp.arange(segment_ids.shape[0], dtype=jnp.int32)
    same_doc = segment_ids[:, None] == segment_ids[None, :]
    allowed = same_doc & (token_index[None, :] <= token_index[:, None])
    positions = jnp.sum(allowed.astype(jnp.int32), axis=1) - 1
    return (allowed, positions.astype(jnp.float32))


def attend(normed, allowed, positions, q_local, kv_local):
    token_count = normed.shape[0]
    queries = jnp.dot(normed, q_local, preferred_element_type=jnp.float32).reshape(
        token_count, -1, HEAD_DIM
    )
    key_value = jnp.einsum("td,kcd->tkc", normed, kv_local, preferred_element_type=jnp.float32)
    key_value = lax.all_gather(key_value, "mp", axis=2, tiled=True)
    key_rows = rotate(key_value[:, 0:1, :], positions)[:, 0, :].astype(jnp.bfloat16)
    value_rows = key_value[:, 1, :].astype(jnp.bfloat16)
    queries = rotate(queries, positions).astype(jnp.bfloat16)
    scores = jnp.einsum("thd,sd->hts", queries, key_rows, preferred_element_type=jnp.float32) * (
        1.0 / math.sqrt(HEAD_DIM)
    )
    scores = jnp.where(allowed[None], scores, -jnp.inf)
    row_max = jnp.max(scores, axis=-1, keepdims=True)
    exp_scores = jnp.exp(scores - row_max)
    attn_weights = (exp_scores / jnp.sum(exp_scores, axis=-1, keepdims=True)).astype(jnp.bfloat16)
    attended = jnp.einsum(
        "hts,sd->thd", attn_weights, value_rows, preferred_element_type=jnp.float32
    )
    return attended.astype(jnp.bfloat16).reshape(token_count, -1)


def gather_features(rows_local):
    return lax.all_gather(rows_local, ("sec", "mp"), axis=1, tiled=True)


def section_features(rows_local, gain_row, allowed, positions, q_local, kv_local, o_local):
    share = rows_local.shape[1]
    square_sums = lax.psum(jnp.sum(rows_local * rows_local, axis=1), ("sec", "mp"))
    factor = lax.rsqrt(square_sums / D + rms_eps)
    gain_local = lax.dynamic_slice_in_dim(
        gain_row, lax.axis_index(("sec", "mp")) * share, share, 0
    ).astype(jnp.float32)
    normed_local = (rows_local * factor[:, None] * gain_local[None, :]).astype(jnp.bfloat16)
    normed = gather_features(normed_local)
    attended = attend(normed, allowed, positions, q_local, kv_local)
    summed = lax.psum_scatter(
        lax.dot_general(
            o_local, attended, (((0,), (1,)), ((), ())), preferred_element_type=jnp.float32
        ),
        ("sec", "mp"),
        scatter_dimension=0,
        tiled=True,
    )
    return rows_local + summed.T


def swap(values, axis, mask):
    size = lax.axis_size(axis)
    return lax.ppermute(values, axis, [(i, i ^ mask) for i in range(size)])


def spread_rows(values, parts):
    return lax.all_to_all(values, "dp", split_axis=0, concat_axis=0, tiled=True).reshape(
        (parts, -1) + values.shape[1:]
    )


def merger(patches, ln_gain, ln_shift, w_in, b_in, w_out, live_slot, count, grad_rows, packed_rows):
    owners = lax.axis_size("dp")
    group = lax.axis_size(("sec", "mp"))
    slots = patches.shape[0]
    in_share, hidden_share = w_in.shape
    out_share = w_out.shape[1]
    share = in_share + out_share

    normed = group_norm(patches, ln_gain, ln_shift).astype(jnp.bfloat16)
    slot_grads = jnp.where(live_slot[:, None], grad_rows, jnp.zeros_like(grad_rows))
    rows = jnp.concatenate(
        [normed.reshape(slots, owners, in_share), slot_grads.reshape(slots, owners, out_share)],
        axis=2,
    ).transpose(1, 0, 2)
    count_rows = jnp.broadcast_to(count.astype(jnp.bfloat16), (owners, 8, share))
    received = lax.all_to_all(
        jnp.concatenate([rows, count_rows], axis=1), "dp", split_axis=0, concat_axis=0, tiled=True
    )
    counts = received[:, slots, 0].astype(jnp.int32)
    owner_index = jnp.arange(owners, dtype=jnp.int32)
    offsets = jnp.sum(jnp.where(owner_index[None, :] < owner_index[:, None], counts[None, :], 0), axis=1)
    slot_index = jnp.arange(slots, dtype=jnp.int32)
    target = jnp.where(
        slot_index[None, :] < counts[:, None], offsets[:, None] + slot_index[None, :], -1
    ).reshape(-1)
    pack = (jnp.arange(packed_rows, dtype=jnp.int32)[:, None] == target[None, :]).astype(jnp.bfloat16)
    packed = jnp.dot(
        pack, received[:, :slots].reshape(owners * slots, share), preferred_element_type=jnp.float32
    ).astype(jnp.bfloat16)

    pre_part = jnp.dot(packed[:, :in_share], w_in, preferred_element_type=jnp.float32)
    grad_part = lax.dot_general(
        packed[:, in_share:], w_out, (((1,), (1,)), ((), ())), preferred_element_type=jnp.float32
    )
    parts = jnp.concatenate([pre_part, grad_part], axis=1).astype(jnp.bfloat16)
    chunk = packed_rows // owners
    parts = lax.all_to_all(
        parts.reshape(owners, chunk, 2 * hidden_share), "dp", split_axis=0, concat_axis=0, tiled=True
    )
    sums = jnp.sum(parts.astype(jnp.float32), axis=0)
    pre_act = sums[:, :hidden_share] + b_in.astype(jnp.float32)
    hidden_units, pull_gelu = jax.vjp(gelu_exact, pre_act)
    pre_grads = pull_gelu(sums[:, hidden_share:])[0]
    both = jnp.concatenate([hidden_units, pre_grads], axis=1).astype(jnp.bfloat16)
    both = lax.all_to_all(
        jnp.broadcast_to(both[None], (owners, chunk, 2 * hidden_share)),
        "dp",
        split_axis=0,
        concat_axis=0,
        tiled=True,
    ).reshape(packed_rows, 2 * hidden_share)
    merged_part = jnp.dot(both[:, :hidden_share], w_out, preferred_element_type=jnp.float32)
    back_part = lax.dot_general(
        both[:, hidden_share:], w_in, (((1,), (1,)), ((), ())), preferred_element_type=jnp.float32
    )
    tail = jnp.concatenate(
        [
            merged_part.astype(jnp.bfloat16).reshape(packed_rows, group, out_share // group),
            back_part.astype(jnp.bfloat16).reshape(packed_rows, group, in_share // group),
        ],
        axis=2,
    ).reshape(packed_rows, group * (share // group))
    tail = lax.dot_general(
        pack, tail, (((0,), (0,)), ((), ())), preferred_element_type=jnp.float32
    ).astype(jnp.bfloat16)
    tail = tail.reshape(owners * slots, group, share // group).transpose(1, 0, 2)
    me = lax.axis_index(("sec", "mp"))
    parts_now = tail.astype(jnp.float32)
    index = jnp.arange(group, dtype=jnp.int32) ^ me
    parts_now = jnp.take(parts_now, index, axis=0)
    mask = 1
    while mask < group:
        pairs = parts_now.reshape(-1, 2, owners * slots, share // group)
        received = swap(pairs[:, 1].astype(jnp.bfloat16), ("sec", "mp"), mask)
        parts_now = pairs[:, 0] + received.astype(jnp.float32)
        mask *= 2
    mine = parts_now.reshape(owners, slots, share // group).astype(jnp.bfloat16)
    mine = lax.all_to_all(mine, "dp", split_axis=0, concat_axis=0, tiled=True)
    gathered = mine[None]
    mask = group // 2
    while mask >= 1:
        gathered = jnp.concatenate([gathered, swap(gathered, ("sec", "mp"), mask)], axis=0)
        mask //= 2
    order = [0]
    mask = group // 2
    while mask >= 1:
        order = order + [i ^ mask for i in order]
        mask //= 2
    place_of = [0] * group
    for where_now, relative in enumerate(order):
        place_of[relative] = where_now
    gathered = jnp.take(gathered, jnp.asarray(place_of, jnp.int32)[index], axis=0)
    gathered = gathered.transpose(2, 1, 0, 3)
    merged = gathered[..., : out_share // group].reshape(slots, owners * out_share)
    normed_grads = gathered[..., out_share // group :].reshape(slots, owners * in_share)
    _, pull_norm = jax.vjp(
        lambda values: group_norm(values, ln_gain, ln_shift), patches.astype(jnp.float32)
    )
    return merged, pull_norm(normed_grads.astype(jnp.float32))[0]


def project_kernel(n_parts, blocks, layer, fresh, starts_ref, *refs):
    x_refs = refs[:n_parts]
    gain_ref, q_ref, kv_ref = refs[n_parts : n_parts + 3]
    old = refs[n_parts + 3 : -3]
    out_q, out_kv, out_sq = refs[-3:]
    step = pl.program_id(0)

    @pl.when(step == 0)
    def _():
        if fresh:
            out_q[...] = jnp.zeros_like(out_q)
            out_kv[...] = jnp.zeros_like(out_kv)
            out_sq[...] = jnp.zeros_like(out_sq)
        else:
            out_q[...] = old[0][...]
            out_kv[...] = old[1][...]
            out_sq[...] = old[2][...]

    def add(x_ref):
        rows = x_ref[...].astype(jnp.float32)
        squares = rows * rows
        lanes = out_sq.shape[1]
        total = squares[:, :lanes]
        for i in range(1, rows.shape[1] // lanes):
            total = total + squares[:, i * lanes : (i + 1) * lanes]
        out_sq[...] += total
        normed = (rows * gain_ref[layer : layer + 1, :]).astype(jnp.bfloat16)
        out_q[...] += jnp.dot(normed, q_ref[0], preferred_element_type=jnp.float32)
        for i in range(2):
            out_kv[:, i * HEAD_DIM : (i + 1) * HEAD_DIM] += lax.dot_general(
                normed, kv_ref[0, i], (((1,), (1,)), ((), ())), preferred_element_type=jnp.float32
            )

    for part in range(n_parts):
        pl.when(step // blocks == part)(lambda part=part: add(x_refs[part]))


def project(parts, starts, gains, q_weight, kv_weight, layer, old, width=512):
    rows, part_width = parts[0].shape
    n_parts, blocks = len(parts), part_width // width
    columns = q_weight.shape[2]
    fresh = old is None

    def x_map(part):
        return lambda i, s: (0, jnp.clip(i - part * blocks, 0, blocks - 1))

    def weight_block(i, s):
        return s[i // blocks] + i % blocks

    shapes = [(rows, columns), (rows, 2 * HEAD_DIM), (rows, HEAD_DIM)]
    whole = [pl.BlockSpec(shape, lambda i, s: (0, 0)) for shape in shapes]
    in_specs = [pl.BlockSpec((rows, width), x_map(part)) for part in range(n_parts)]
    in_specs += [
        pl.BlockSpec((gains.shape[0], width), lambda i, s: (0, weight_block(i, s))),
        pl.BlockSpec((1, width, columns), lambda i, s: (layer, weight_block(i, s), 0)),
        pl.BlockSpec((1, 2, HEAD_DIM, width), lambda i, s: (layer, 0, 0, weight_block(i, s))),
    ]
    operands = list(parts) + [gains, q_weight, kv_weight]
    if not fresh:
        in_specs += whole
        operands += list(old)
    features = n_parts * part_width
    return pl.pallas_call(
        lambda *refs: project_kernel(n_parts, blocks, layer, fresh, *refs),
        grid_spec=pltpu.PrefetchScalarGridSpec(
            num_scalar_prefetch=1,
            grid=(n_parts * blocks,),
            in_specs=in_specs,
            out_specs=whole,
        ),
        out_shape=[jax.ShapeDtypeStruct(shape, jnp.float32) for shape in shapes],
        cost_estimate=pl.CostEstimate(
            flops=2 * rows * features * (columns + 2 * HEAD_DIM),
            bytes_accessed=features * (columns + 2 * HEAD_DIM) * 2 + rows * features * 2,
            transcendentals=0,
        ),
        compiler_params=pltpu.CompilerParams(vmem_limit_bytes=40 * 1024 * 1024),
        name="project",
    )(starts // width, *operands)


def attend_kernel(features, with_images, *refs):
    q_ref, kv_ref, sq_ref, cos_ref, sin_ref, bias_ref = refs[:6]
    out_ref = refs[-1]
    queries, key_value, squares = q_ref[...], kv_ref[...], sq_ref[...]
    if with_images:
        image_q, image_kv, image_sq, select_ref = refs[6:10]
        select = select_ref[...]
        is_image = jnp.sum(select, axis=1, keepdims=True) > 0.0

        def put(image_ref, values):
            picked = jnp.dot(
                select,
                image_ref[...],
                preferred_element_type=jnp.float32,
                precision=lax.Precision.HIGHEST,
            )
            return jnp.where(is_image, picked, values)

        queries, key_value, squares = (
            put(image_q, queries),
            put(image_kv, key_value),
            put(image_sq, squares),
        )
    factor = lax.rsqrt(jnp.sum(squares, axis=1, keepdims=True) / features + rms_eps)
    cosine, sine = cos_ref[...] * factor, sin_ref[...] * factor

    def turned(values):
        return (values * cosine + pltpu.roll(values, HEAD_DIM // 2, 1) * sine).astype(jnp.bfloat16)

    key_rows = turned(key_value[:, :HEAD_DIM])
    value_rows = (key_value[:, HEAD_DIM:] * factor).astype(jnp.bfloat16)
    bias = bias_ref[...]
    for head in range(queries.shape[1] // HEAD_DIM):
        columns = slice(head * HEAD_DIM, (head + 1) * HEAD_DIM)
        scores = lax.dot_general(
            turned(queries[:, columns]),
            key_rows,
            (((1,), (1,)), ((), ())),
            preferred_element_type=jnp.float32,
        )
        scores = scores * (1.0 / math.sqrt(HEAD_DIM)) + bias
        exp_scores = jnp.exp(scores - jnp.max(scores, axis=1, keepdims=True))
        weights = (exp_scores / jnp.sum(exp_scores, axis=1, keepdims=True)).astype(jnp.bfloat16)
        out_ref[:, columns] = jnp.dot(
            weights, value_rows, preferred_element_type=jnp.float32
        ).astype(jnp.bfloat16)


def attention(features, projected, cosine, sine, bias, images=None):
    operands = list(projected) + [cosine, sine, bias] + ([] if images is None else list(images))
    rows, columns = projected[0].shape
    return pl.pallas_call(
        lambda *refs: attend_kernel(features, images is not None, *refs),
        out_shape=jax.ShapeDtypeStruct((rows, columns), jnp.bfloat16),
        cost_estimate=pl.CostEstimate(
            flops=4 * rows * rows * columns, bytes_accessed=4 * rows * columns, transcendentals=0
        ),
        compiler_params=pltpu.CompilerParams(vmem_limit_bytes=40 * 1024 * 1024),
        name="attention",
    )(*operands)


def output_kernel(blocks, starts_ref, a_ref, o_ref, kept_ref, sent_ref):
    step = pl.program_id(0)
    product = jnp.dot(a_ref[...], o_ref[0], preferred_element_type=jnp.float32)

    @pl.when(step < blocks)
    def _():
        sent_ref[...] = product.astype(sent_ref.dtype)

    @pl.when(step >= blocks)
    def _():
        kept_ref[...] = product


def output_product(attended, o_weight, layer, sent_start, kept_start, count, width=512):
    rows, depth = attended.shape
    blocks = count // width
    starts = jnp.stack([sent_start, kept_start]).astype(jnp.int32) // width
    return pl.pallas_call(
        lambda *refs: output_kernel(blocks, *refs),
        grid_spec=pltpu.PrefetchScalarGridSpec(
            num_scalar_prefetch=1,
            grid=(2 * blocks,),
            in_specs=[
                pl.BlockSpec((rows, depth), lambda i, s: (0, 0)),
                pl.BlockSpec(
                    (1, depth, width), lambda i, s: (layer, 0, s[i // blocks] + i % blocks)
                ),
            ],
            out_specs=[
                pl.BlockSpec((rows, width), lambda i, s: (0, jnp.clip(i - blocks, 0, blocks - 1))),
                pl.BlockSpec((rows, width), lambda i, s: (0, jnp.clip(i, 0, blocks - 1))),
            ],
        ),
        out_shape=[
            jax.ShapeDtypeStruct((rows, count), jnp.float32),
            jax.ShapeDtypeStruct((rows, count), jnp.bfloat16),
        ],
        cost_estimate=pl.CostEstimate(
            flops=4 * rows * depth * count, bytes_accessed=4 * depth * count, transcendentals=0
        ),
        compiler_params=pltpu.CompilerParams(vmem_limit_bytes=40 * 1024 * 1024),
        name="output_product",
    )(starts, attended, o_weight)


CORE, ACROSS = 1, 2


def rope_tables(positions):
    half_depth = HEAD_DIM // 2
    inv_freq = rope_base ** (-2.0 * jnp.arange(half_depth, dtype=jnp.float32) / HEAD_DIM)
    angles = positions[:, None] * inv_freq[None, :]
    cosine, sine = jnp.cos(angles), jnp.sin(angles)
    return jnp.concatenate([cosine, cosine], axis=1), jnp.concatenate([-sine, sine], axis=1)


def decoder(text_rows, gathered_text, image_rows, select, segments, norm_gain, q_weight, kv_weight, o_weight):
    me = lax.axis_index("sec")
    core, chip = me & 1, me >> 1
    share = text_rows.shape[1]
    features = share * 4
    piece = share // 2
    layers = q_weight.shape[0]
    gains = norm_gain.astype(jnp.float32)
    allowed, positions = doc_mask(segments)
    bias = jnp.where(allowed, 0.0, -1e30).astype(jnp.float32)
    cosine, sine = rope_tables(positions)

    def column(chip_index, core_bit, half):
        return (2 * chip_index + core_bit) * share + half * piece

    starts = jnp.stack([(me ^ r) * share for r in range(4)]).astype(jnp.int32)
    projected = project(gathered_text, starts, gains, q_weight, kv_weight, 0, None)
    image_parts = [image_rows]
    images = project(
        image_parts, jnp.zeros((1,), jnp.int32), gains, q_weight, kv_weight, 0, None, width=1024
    )
    attended = attention(
        features, projected, cosine, sine, bias, list(images) + [select.astype(jnp.float32)]
    )

    is_image = jnp.any(select, axis=1)
    held = []
    for p in range(4):
        text_part = jnp.where(
            chip == p >> 1, gathered_text[0], gathered_text[ACROSS]
        )[:, (p & 1) * piece : (p & 1) * piece + piece]
        image_part = lax.dynamic_slice_in_dim(image_rows, column(p >> 1, core, p & 1), piece, 1)
        picked = jnp.dot(
            select.astype(jnp.bfloat16), image_part, preferred_element_type=jnp.float32
        )
        held.append(jnp.where(is_image[:, None], picked, text_part.astype(jnp.float32)))

    for layer in range(1, layers):
        sums = []
        for p in range(4):
            kept, sent = output_product(
                attended,
                o_weight,
                layer - 1,
                column(p >> 1, core ^ 1, p & 1),
                column(p >> 1, core, p & 1),
                piece,
            )
            chip_sum = (kept + swap(sent, "sec", CORE).astype(jnp.float32)).astype(jnp.bfloat16)
            sums.append((chip_sum, swap(chip_sum, "sec", ACROSS)))
        projected = None
        for p in range(4):
            chip_sum, other = sums[p]
            held[p] = held[p] + (chip_sum.astype(jnp.float32) + other.astype(jnp.float32))
            rounded = held[p].astype(jnp.bfloat16)
            here = jnp.stack([column(p >> 1, core, p & 1), column(p >> 1, core ^ 1, p & 1)])
            projected = project(
                [rounded, swap(rounded, "sec", CORE)],
                here.astype(jnp.int32),
                gains,
                q_weight,
                kv_weight,
                layer,
                projected,
            )
        attended = attention(features, projected, cosine, sine, bias)

    last = layers - 1
    arrived = []
    for half in range(2):
        kept, sent = output_product(
            attended, o_weight, last, column(chip ^ 1, core ^ 1, half), column(chip ^ 1, core, half), piece
        )
        chip_sum = (kept + swap(sent, "sec", CORE).astype(jnp.float32)).astype(jnp.bfloat16)
        arrived.append(swap(chip_sum, "sec", ACROSS))
    kept, sent = output_product(
        attended, o_weight, last, column(chip, core ^ 1, 0), column(chip, core, 0), share
    )
    here_sum = kept + swap(sent, "sec", CORE).astype(jnp.float32)
    mine = [jnp.where(chip == 0, held[half], held[2 + half]) for half in range(2)]
    return jnp.concatenate(
        [
            mine[half] + (here_sum[:, half * piece : (half + 1) * piece] + arrived[half].astype(jnp.float32))
            for half in range(2)
        ],
        axis=1,
    )


def local(
    patches,
    ln_gain,
    ln_shift,
    w_in,
    b_in,
    w_out,
    b_out,
    place,
    image_counts,
    text_rows,
    segments,
    norm_gain,
    q_weight,
    kv_weight,
    o_weight,
    grad_rows,
):
    slot_count = patches.shape[0]
    tokens, share = text_rows.shape
    slot_index = jnp.arange(slot_count, dtype=jnp.int32)
    live_slot = slot_index < image_counts[0]
    merged, patch_grads = merger(
        patches,
        ln_gain,
        ln_shift,
        w_in,
        b_in,
        w_out,
        live_slot,
        image_counts[0],
        grad_rows,
        lax.axis_size("dp") * (tokens // 16),
    )
    token_index = jnp.arange(tokens, dtype=jnp.int32)
    select = (place[:, None] == token_index[None, :]) & live_slot[:, None]
    if lax.axis_size("sec") == 4 and lax.axis_size("mp") == 1:
        near, far = swap(text_rows, "sec", CORE), swap(text_rows, "sec", ACROSS)
        gathered_text = [text_rows, near, far, swap(far, "sec", CORE)]
        shift = b_out.reshape(1, share)
        shift_far = swap(shift, "sec", ACROSS)
        shifts = [shift, swap(shift, "sec", CORE), shift_far, swap(shift_far, "sec", CORE)]
        me = lax.axis_index("sec")
        shifts = jnp.take(jnp.concatenate(shifts, axis=0), jnp.arange(4, dtype=jnp.int32) ^ me, axis=0)
        image_rows = (
            merged.astype(jnp.float32) + shifts.reshape(1, -1).astype(jnp.float32)
        ).astype(jnp.bfloat16)
        padded = -slot_count % 16
        image_rows = jnp.pad(image_rows, ((0, padded), (0, 0)))
        chosen = jnp.pad(select, ((0, padded), (0, 0))).T
        current = decoder(
            text_rows,
            gathered_text,
            image_rows,
            chosen,
            segments[0],
            norm_gain,
            q_weight,
            kv_weight,
            o_weight,
        )
        return (current, patch_grads)
    merged_local = lax.dynamic_slice_in_dim(
        merged, lax.axis_index(("sec", "mp")) * share, share, 1
    ).astype(jnp.float32)
    merged_local = (merged_local + b_out.astype(jnp.float32)).astype(jnp.bfloat16)
    is_image = jnp.any(select, axis=0)
    picked = lax.dot_general(
        select.astype(jnp.bfloat16),
        merged_local,
        (((0,), (0,)), ((), ())),
        preferred_element_type=jnp.float32,
    )
    start_rows = jnp.where(is_image[:, None], picked, text_rows.astype(jnp.float32)).astype(
        jnp.bfloat16
    )
    allowed, positions = doc_mask(segments[0])
    layer_count = q_weight.shape[0]
    current = start_rows.astype(jnp.float32)
    for layer_index in range(layer_count):
        current = section_features(
            current,
            norm_gain[layer_index],
            allowed,
            positions,
            q_weight[layer_index],
            kv_weight[layer_index],
            o_weight[layer_index],
        )
    return (current, patch_grads)


def solution(mesh):
    in_specs = (
        P("dp", None),
        P(),
        P(),
        P("dp", ("sec", "mp")),
        P(("sec", "mp")),
        P(("sec", "mp"), "dp"),
        P(("sec", "mp")),
        P("dp"),
        P("dp"),
        P("dp", ("sec", "mp")),
        P("dp", None),
        P(),
        P(None, None, ("sec", "mp")),
        P(None, None, ("sec", "mp"), None),
        P(None, ("sec", "mp"), None),
        P("dp", None),
    )
    out_specs = (P("dp", ("sec", "mp")), P("dp", None))
    return jax.shard_map(local, mesh=mesh, in_specs=in_specs, out_specs=out_specs, check_vma=False)
```

```python
import math

import jax
import jax.numpy as jnp
from jax import lax
from jax.experimental import pallas as pl
from jax.experimental.pallas import tpu as pltpu
from jax.sharding import PartitionSpec as P

D = 8192
HEAD_DIM = 128


ln_eps = 1e-06
rms_eps = 1e-06
rope_base = 1000000.0


def group_norm(patch_rows, ln_gain, ln_shift):
    row_count = patch_rows.shape[0]
    grouped = patch_rows.astype(jnp.float32).reshape(row_count, -1, ln_gain.shape[0])
    center = grouped - jnp.mean(grouped, axis=-1, keepdims=True)
    spread = jnp.mean(center * center, axis=-1, keepdims=True)
    scaled = center * lax.rsqrt(spread + ln_eps) * ln_gain.astype(jnp.float32) + ln_shift.astype(
        jnp.float32
    )
    return scaled.reshape(row_count, -1)


def gelu_exact(values):
    return jax.nn.gelu(values, approximate=False)


def rotate(values, positions):
    head_depth = values.shape[-1]
    half_depth = head_depth // 2
    inv_freq = rope_base ** (-2.0 * jnp.arange(half_depth, dtype=jnp.float32) / head_depth)
    angles = positions[:, None] * inv_freq[None, :]
    cosine = jnp.cos(angles)[:, None, :]
    sine_part = jnp.sin(angles)[:, None, :]
    first_half = values[..., :half_depth]
    second = values[..., half_depth:]
    return jnp.concatenate(
        [first_half * cosine - second * sine_part, second * cosine + first_half * sine_part],
        axis=-1,
    )


def doc_mask(segment_ids):
    token_index = jnp.arange(segment_ids.shape[0], dtype=jnp.int32)
    same_doc = segment_ids[:, None] == segment_ids[None, :]
    allowed = same_doc & (token_index[None, :] <= token_index[:, None])
    positions = jnp.sum(allowed.astype(jnp.int32), axis=1) - 1
    return (allowed, positions.astype(jnp.float32))


def attend(normed, allowed, positions, q_local, kv_local):
    token_count = normed.shape[0]
    queries = jnp.dot(normed, q_local, preferred_element_type=jnp.float32).reshape(
        token_count, -1, HEAD_DIM
    )
    key_value = jnp.einsum("td,kcd->tkc", normed, kv_local, preferred_element_type=jnp.float32)
    key_value = lax.all_gather(key_value, "mp", axis=2, tiled=True)
    key_rows = rotate(key_value[:, 0:1, :], positions)[:, 0, :].astype(jnp.bfloat16)
    value_rows = key_value[:, 1, :].astype(jnp.bfloat16)
    queries = rotate(queries, positions).astype(jnp.bfloat16)
    scores = jnp.einsum("thd,sd->hts", queries, key_rows, preferred_element_type=jnp.float32) * (
        1.0 / math.sqrt(HEAD_DIM)
    )
    scores = jnp.where(allowed[None], scores, -jnp.inf)
    row_max = jnp.max(scores, axis=-1, keepdims=True)
    exp_scores = jnp.exp(scores - row_max)
    attn_weights = (exp_scores / jnp.sum(exp_scores, axis=-1, keepdims=True)).astype(jnp.bfloat16)
    attended = jnp.einsum(
        "hts,sd->thd", attn_weights, value_rows, preferred_element_type=jnp.float32
    )
    return attended.astype(jnp.bfloat16).reshape(token_count, -1)


def gather_features(rows_local):
    return lax.all_gather(rows_local, ("sec", "mp"), axis=1, tiled=True)


def section_features(rows_local, gain_row, allowed, positions, q_local, kv_local, o_local):
    share = rows_local.shape[1]
    square_sums = lax.psum(jnp.sum(rows_local * rows_local, axis=1), ("sec", "mp"))
    factor = lax.rsqrt(square_sums / D + rms_eps)
    gain_local = lax.dynamic_slice_in_dim(
        gain_row, lax.axis_index(("sec", "mp")) * share, share, 0
    ).astype(jnp.float32)
    normed_local = (rows_local * factor[:, None] * gain_local[None, :]).astype(jnp.bfloat16)
    normed = gather_features(normed_local)
    attended = attend(normed, allowed, positions, q_local, kv_local)
    summed = lax.psum_scatter(
        lax.dot_general(
            o_local, attended, (((0,), (1,)), ((), ())), preferred_element_type=jnp.float32
        ),
        ("sec", "mp"),
        scatter_dimension=0,
        tiled=True,
    )
    return rows_local + summed.T


def swap(values, axis, mask):
    size = lax.axis_size(axis)
    return lax.ppermute(values, axis, [(i, i ^ mask) for i in range(size)])


def spread_rows(values, parts):
    return lax.all_to_all(values, "dp", split_axis=0, concat_axis=0, tiled=True).reshape(
        (parts, -1) + values.shape[1:]
    )


def merger_rows(patches, ln_gain, ln_shift, w_in, b_in, w_out, live_slot, count, grad_rows, packed_rows):
    owners = lax.axis_size("dp")
    group = lax.axis_size(("sec", "mp"))
    slots = patches.shape[0]
    in_share, hidden_share = w_in.shape
    out_share = w_out.shape[1]
    share = in_share + out_share

    normed = group_norm(patches, ln_gain, ln_shift).astype(jnp.bfloat16)
    slot_grads = jnp.where(live_slot[:, None], grad_rows, jnp.zeros_like(grad_rows))
    rows = jnp.concatenate(
        [normed.reshape(slots, owners, in_share), slot_grads.reshape(slots, owners, out_share)],
        axis=2,
    ).transpose(1, 0, 2)
    count_rows = jnp.broadcast_to(count.astype(jnp.bfloat16), (owners, 8, share))
    received = lax.all_to_all(
        jnp.concatenate([rows, count_rows], axis=1), "dp", split_axis=0, concat_axis=0, tiled=True
    )
    counts = received[:, slots, 0].astype(jnp.int32)
    owner_index = jnp.arange(owners, dtype=jnp.int32)
    offsets = jnp.sum(jnp.where(owner_index[None, :] < owner_index[:, None], counts[None, :], 0), axis=1)
    slot_index = jnp.arange(slots, dtype=jnp.int32)
    target = jnp.where(
        slot_index[None, :] < counts[:, None], offsets[:, None] + slot_index[None, :], -1
    ).reshape(-1)
    pack = (jnp.arange(packed_rows, dtype=jnp.int32)[:, None] == target[None, :]).astype(jnp.bfloat16)
    packed = jnp.dot(
        pack, received[:, :slots].reshape(owners * slots, share), preferred_element_type=jnp.float32
    ).astype(jnp.bfloat16)

    pre_part = jnp.dot(packed[:, :in_share], w_in, preferred_element_type=jnp.float32)
    grad_part = lax.dot_general(
        packed[:, in_share:], w_out, (((1,), (1,)), ((), ())), preferred_element_type=jnp.float32
    )
    parts = jnp.concatenate([pre_part, grad_part], axis=1).astype(jnp.bfloat16)
    chunk = packed_rows // owners
    parts = lax.all_to_all(
        parts.reshape(owners, chunk, 2 * hidden_share), "dp", split_axis=0, concat_axis=0, tiled=True
    )
    sums = jnp.sum(parts.astype(jnp.float32), axis=0)
    pre_act = sums[:, :hidden_share] + b_in.astype(jnp.float32)
    hidden_units, pull_gelu = jax.vjp(gelu_exact, pre_act)
    pre_grads = pull_gelu(sums[:, hidden_share:])[0]
    both = jnp.concatenate([hidden_units, pre_grads], axis=1).astype(jnp.bfloat16)
    both = lax.all_to_all(
        jnp.broadcast_to(both[None], (owners, chunk, 2 * hidden_share)),
        "dp",
        split_axis=0,
        concat_axis=0,
        tiled=True,
    ).reshape(packed_rows, 2 * hidden_share)
    merged_part = jnp.dot(both[:, :hidden_share], w_out, preferred_element_type=jnp.float32)
    back_part = lax.dot_general(
        both[:, hidden_share:], w_in, (((1,), (1,)), ((), ())), preferred_element_type=jnp.float32
    )
    tail = jnp.concatenate(
        [
            merged_part.astype(jnp.bfloat16).reshape(packed_rows, group, out_share // group),
            back_part.astype(jnp.bfloat16).reshape(packed_rows, group, in_share // group),
        ],
        axis=2,
    ).reshape(packed_rows, group * (share // group))
    tail = lax.dot_general(
        pack, tail, (((0,), (0,)), ((), ())), preferred_element_type=jnp.float32
    ).astype(jnp.bfloat16)
    tail = tail.reshape(owners * slots, group, share // group).transpose(1, 0, 2)
    me = lax.axis_index(("sec", "mp"))
    parts_now = tail.astype(jnp.float32)
    index = jnp.arange(group, dtype=jnp.int32) ^ me
    parts_now = jnp.take(parts_now, index, axis=0)
    mask = 1
    while mask < group:
        pairs = parts_now.reshape(-1, 2, owners * slots, share // group)
        received = swap(pairs[:, 1].astype(jnp.bfloat16), ("sec", "mp"), mask)
        parts_now = pairs[:, 0] + received.astype(jnp.float32)
        mask *= 2
    mine = parts_now.reshape(owners, slots, share // group).astype(jnp.bfloat16)
    mine = lax.all_to_all(mine, "dp", split_axis=0, concat_axis=0, tiled=True)
    gathered = mine[None]
    mask = group // 2
    while mask >= 1:
        gathered = jnp.concatenate([gathered, swap(gathered, ("sec", "mp"), mask)], axis=0)
        mask //= 2
    order = [0]
    mask = group // 2
    while mask >= 1:
        order = order + [i ^ mask for i in order]
        mask //= 2
    place_of = [0] * group
    for where_now, relative in enumerate(order):
        place_of[relative] = where_now
    gathered = jnp.take(gathered, jnp.asarray(place_of, jnp.int32)[index], axis=0)
    gathered = gathered.transpose(2, 1, 0, 3)
    merged = gathered[..., : out_share // group].reshape(slots, owners * out_share)
    normed_grads = gathered[..., out_share // group :].reshape(slots, owners * in_share)
    _, pull_norm = jax.vjp(
        lambda values: group_norm(values, ln_gain, ln_shift), patches.astype(jnp.float32)
    )
    return merged, pull_norm(normed_grads.astype(jnp.float32))[0]


VMEM_LIMIT = 48 * 1024 * 1024
WEIGHT = 64
CORE, ACROSS = 1, 2


def call(kernel, out_shape, flops, n_bytes, name, **more):
    return pl.pallas_call(
        kernel,
        out_shape=out_shape,
        cost_estimate=pl.CostEstimate(
            flops=int(flops) // WEIGHT, bytes_accessed=int(n_bytes) // WEIGHT, transcendentals=0
        ),
        compiler_params=pltpu.CompilerParams(vmem_limit_bytes=VMEM_LIMIT),
        name=name,
        **more,
    )


def in_vmem(count):
    return [pl.BlockSpec(memory_space=pltpu.VMEM)] * count


in_smem = pl.BlockSpec(memory_space=pltpu.SMEM)
in_hbm = pl.BlockSpec(memory_space=pl.ANY)


def after(values, others):
    return lax.optimization_barrier((values, others))[0]


def project_kernel(layer, width, n_parts, fresh, starts_ref, *refs):
    x_refs = refs[:n_parts]
    gain_ref, q_hbm, kv_hbm = refs[n_parts : n_parts + 3]
    out_q, out_kv, out_sq, q_buf, kv_buf, q_sem, kv_sem = refs[-7:]
    per_part = x_refs[0].shape[1] // width
    lanes = out_sq.shape[1]

    def place_of(block):
        part, inner = block // per_part, block % per_part
        return pl.multiple_of(starts_ref[part] + inner * width, width)

    def copies(block):
        rows = pl.ds(place_of(block), width)
        return (
            pltpu.make_async_copy(q_hbm.at[layer, rows, :], q_buf.at[block], q_sem.at[block]),
            pltpu.make_async_copy(kv_hbm.at[layer, :, :, rows], kv_buf.at[block], kv_sem.at[block]),
        )

    n_blocks = n_parts * per_part
    for block in range(n_blocks):
        for copy in copies(block):
            copy.start()
    if fresh:
        out_q[...] = jnp.zeros_like(out_q)
        out_kv[...] = jnp.zeros_like(out_kv)
        out_sq[...] = jnp.zeros_like(out_sq)
    for block in range(n_blocks):
        inner = block % per_part
        rows = x_refs[block // per_part][:, inner * width : (inner + 1) * width].astype(jnp.float32)
        squares = rows * rows
        total = squares[:, :lanes]
        for i in range(1, width // lanes):
            total = total + squares[:, i * lanes : (i + 1) * lanes]
        out_sq[...] += total
        gain = gain_ref[layer : layer + 1, pl.ds(place_of(block), width)]
        normed = (rows * gain).astype(jnp.bfloat16)
        for copy in copies(block):
            copy.wait()
        out_q[...] += jnp.dot(normed, q_buf[block], preferred_element_type=jnp.float32)
        for i in range(2):
            out_kv[:, i * HEAD_DIM : (i + 1) * HEAD_DIM] += lax.dot_general(
                normed, kv_buf[block, i], (((1,), (1,)), ((), ())), preferred_element_type=jnp.float32
            )


def project(parts, starts, gains, q_weight, kv_weight, layer, old, width=512):
    rows, part_width = parts[0].shape
    n_parts = len(parts)
    n_blocks = n_parts * part_width // width
    columns = q_weight.shape[2]
    shapes = [(rows, columns), (rows, 2 * HEAD_DIM), (rows, HEAD_DIM)]
    old = [] if old is None else list(old)
    features = n_parts * part_width
    return call(
        lambda *refs: project_kernel(layer, width, n_parts, not old, *refs),
        [jax.ShapeDtypeStruct(shape, jnp.float32) for shape in shapes],
        2 * rows * features * (columns + 2 * HEAD_DIM),
        features * (columns + 2 * HEAD_DIM) * 2 + rows * features * 2,
        "project",
        in_specs=[in_smem] + in_vmem(n_parts + 1) + [in_hbm] * 2 + in_vmem(len(old)),
        out_specs=in_vmem(3),
        input_output_aliases={n_parts + 4 + i: i for i in range(len(old))},
        scratch_shapes=[
            pltpu.VMEM((n_blocks, width, columns), jnp.bfloat16),
            pltpu.VMEM((n_blocks, 2, HEAD_DIM, width), jnp.bfloat16),
            pltpu.SemaphoreType.DMA((n_blocks,)),
            pltpu.SemaphoreType.DMA((n_blocks,)),
        ],
    )(starts, *parts, gains, q_weight, kv_weight, *old)


def attend_kernel(features, with_images, *refs):
    q_ref, kv_ref, sq_ref, cos_ref, sin_ref, bias_ref = refs[:6]
    out_ref = refs[-1]
    queries, key_value, squares = q_ref[...], kv_ref[...], sq_ref[...]
    if with_images:
        image_q, image_kv, image_sq, select_ref = refs[6:10]
        select = select_ref[...]
        is_image = jnp.sum(select, axis=1, keepdims=True) > 0.0

        def put(image_ref, values):
            picked = jnp.dot(
                select,
                image_ref[...],
                preferred_element_type=jnp.float32,
                precision=lax.Precision.HIGHEST,
            )
            return jnp.where(is_image, picked, values)

        queries, key_value, squares = (
            put(image_q, queries),
            put(image_kv, key_value),
            put(image_sq, squares),
        )
    factor = lax.rsqrt(jnp.sum(squares, axis=1, keepdims=True) / features + rms_eps)
    cosine, sine = cos_ref[...] * factor, sin_ref[...] * factor

    def turned(values):
        return (values * cosine + pltpu.roll(values, HEAD_DIM // 2, 1) * sine).astype(jnp.bfloat16)

    key_rows = turned(key_value[:, :HEAD_DIM])
    value_rows = (key_value[:, HEAD_DIM:] * factor).astype(jnp.bfloat16)
    bias = bias_ref[...]
    for head in range(queries.shape[1] // HEAD_DIM):
        columns = slice(head * HEAD_DIM, (head + 1) * HEAD_DIM)
        scores = lax.dot_general(
            turned(queries[:, columns]),
            key_rows,
            (((1,), (1,)), ((), ())),
            preferred_element_type=jnp.float32,
        )
        scores = scores * (1.0 / math.sqrt(HEAD_DIM)) + bias
        exp_scores = jnp.exp(scores - jnp.max(scores, axis=1, keepdims=True))
        weights = (exp_scores / jnp.sum(exp_scores, axis=1, keepdims=True)).astype(jnp.bfloat16)
        out_ref[:, columns] = jnp.dot(
            weights, value_rows, preferred_element_type=jnp.float32
        ).astype(jnp.bfloat16)


def attention(features, projected, cosine, sine, bias, images=None):
    operands = list(projected) + [cosine, sine, bias] + ([] if images is None else list(images))
    rows, columns = projected[0].shape
    return call(
        lambda *refs: attend_kernel(features, images is not None, *refs),
        jax.ShapeDtypeStruct((rows, columns), jnp.bfloat16),
        8 * rows * rows * columns,
        8 * rows * columns,
        "attention",
    )(*operands)


def output_kernel(layer, width, starts_ref, a_ref, o_hbm, kept_ref, *refs):
    sent_refs, (o_buf, sem) = refs[:-2], refs[-2:]
    blocks = kept_ref.shape[1] // width
    per_part = blocks // len(sent_refs)

    def copy(block):
        start = pl.multiple_of(starts_ref[block // blocks] + block % blocks * width, width)
        return pltpu.make_async_copy(
            o_hbm.at[layer, :, pl.ds(start, width)], o_buf.at[block], sem.at[block]
        )

    for block in range(2 * blocks):
        copy(block).start()
    for block in range(2 * blocks):
        copy(block).wait()
        product = jnp.dot(a_ref[...], o_buf[block], preferred_element_type=jnp.float32)
        product = product.astype(kept_ref.dtype)
        if block < blocks:
            inner = block % per_part
            sent_refs[block // per_part][:, inner * width : (inner + 1) * width] = product
        else:
            kept_ref[:, (block - blocks) * width : (block - blocks + 1) * width] = product


def output_product(attended, o_weight, layer, sent_start, kept_start, count, parts, width=512):
    rows, depth = attended.shape
    starts = jnp.stack([sent_start, kept_start]).astype(jnp.int32)
    return call(
        lambda *refs: output_kernel(layer, width, *refs),
        [jax.ShapeDtypeStruct((rows, count), jnp.bfloat16)]
        + [jax.ShapeDtypeStruct((rows, count // parts), jnp.bfloat16)] * parts,
        4 * rows * depth * count,
        4 * depth * count,
        "output_product",
        in_specs=[in_smem] + in_vmem(1) + [in_hbm],
        out_specs=in_vmem(1 + parts),
        scratch_shapes=[
            pltpu.VMEM((2 * count // width, depth, width), jnp.bfloat16),
            pltpu.SemaphoreType.DMA((2 * count // width,)),
        ],
    )(starts, attended, o_weight)


def add_kernel(kept_ref, *refs):
    out_ref = refs[-1]
    width = refs[0].shape[1]
    for i, ref in enumerate(refs[:-1]):
        columns = slice(i * width, (i + 1) * width)
        total = kept_ref[:, columns].astype(jnp.float32) + ref[...].astype(jnp.float32)
        out_ref[:, columns] = total.astype(out_ref.dtype)


def add_parts(kept, parts):
    return call(
        add_kernel,
        jax.ShapeDtypeStruct(kept.shape, kept.dtype),
        kept.size,
        6 * kept.size,
        "chip_sum",
    )(kept, *parts)


def rope_tables(positions):
    half_depth = HEAD_DIM // 2
    inv_freq = rope_base ** (-2.0 * jnp.arange(half_depth, dtype=jnp.float32) / HEAD_DIM)
    angles = positions[:, None] * inv_freq[None, :]
    cosine, sine = jnp.cos(angles), jnp.sin(angles)
    return jnp.concatenate([cosine, cosine], axis=1), jnp.concatenate([-sine, sine], axis=1)


def normalize(rows):
    center = rows - jnp.mean(rows, axis=1, keepdims=True)
    factor = lax.rsqrt(jnp.mean(center * center, axis=1, keepdims=True) + ln_eps)
    return center * factor, factor


def norm_kernel(count_ref, patch_ref, affine_ref, out_ref):
    owners, padded, in_share = out_ref.shape
    slots = patch_ref.shape[0]
    vit = affine_ref.shape[1]
    counts = jnp.full((padded - slots, vit), count_ref[0].astype(jnp.float32))
    for group in range(patch_ref.shape[1] // vit):
        rows = patch_ref[:, group * vit : (group + 1) * vit].astype(jnp.float32)
        scaled = normalize(rows)[0] * affine_ref[0:1, :] + affine_ref[1:2, :]
        scaled = jnp.concatenate([scaled, counts], axis=0).astype(out_ref.dtype)
        for i in range(vit // in_share):
            out_ref[group * (vit // in_share) + i] = scaled[:, i * in_share : (i + 1) * in_share]


def norm_back_kernel(patch_ref, grads_ref, affine_ref, out_ref):
    _, _, in_share = grads_ref.shape
    slots = patch_ref.shape[0]
    vit = affine_ref.shape[1]
    per_group = vit // in_share
    for group in range(patch_ref.shape[1] // vit):
        rows = patch_ref[:, group * vit : (group + 1) * vit].astype(jnp.float32)
        unit, factor = normalize(rows)
        grads = jnp.concatenate(
            [grads_ref[group * per_group + i].astype(jnp.float32) for i in range(per_group)], axis=1
        )[:slots]
        grads = grads * affine_ref[0:1, :]
        along = jnp.mean(grads * unit, axis=1, keepdims=True)
        out_ref[:, group * vit : (group + 1) * vit] = factor * (
            grads - jnp.mean(grads, axis=1, keepdims=True) - unit * along
        )


def split_kernel(rows_ref, out_ref):
    owners, padded, width = out_ref.shape
    slots = rows_ref.shape[0]
    for owner in range(owners):
        part = rows_ref[:, owner * width : (owner + 1) * width].astype(jnp.float32)
        part = jnp.concatenate([part, jnp.zeros((padded - slots, width), jnp.float32)], axis=0)
        out_ref[owner] = part.astype(out_ref.dtype)


def pack_kernel(slots, rows_ref, weight_ref, out_ref, pack_ref):
    owners, padded, _ = rows_ref.shape
    packed_rows = out_ref.shape[0]
    row = lax.broadcasted_iota(jnp.int32, (packed_rows, padded), 0).astype(jnp.float32)
    slot = lax.broadcasted_iota(jnp.int32, (packed_rows, padded), 1).astype(jnp.float32)
    offset = jnp.zeros((1, 1), jnp.float32)
    packed = jnp.zeros((packed_rows, rows_ref.shape[2]), jnp.float32)
    for owner in range(owners):
        rows = rows_ref[owner]
        count = rows.astype(jnp.float32)[slots : slots + 1, 0:1]
        chosen = jnp.where((row == offset + slot) & (slot < count), 1.0, 0.0).astype(jnp.bfloat16)
        pack_ref[owner] = chosen
        packed = packed + jnp.dot(chosen, rows, preferred_element_type=jnp.float32)
        offset = offset + count
    out_ref[...] = jnp.dot(
        packed.astype(jnp.bfloat16), weight_ref[...], preferred_element_type=jnp.float32
    ).astype(out_ref.dtype)


def pack_grads_kernel(rows_ref, pack_ref, weight_ref, out_ref):
    packed = jnp.zeros((out_ref.shape[0], rows_ref.shape[2]), jnp.float32)
    for owner in range(rows_ref.shape[0]):
        packed = packed + jnp.dot(
            pack_ref[owner], rows_ref[owner], preferred_element_type=jnp.float32
        )
    out_ref[...] = lax.dot_general(
        packed.astype(jnp.bfloat16),
        weight_ref[...],
        (((1,), (1,)), ((), ())),
        preferred_element_type=jnp.float32,
    ).astype(out_ref.dtype)


def halves_kernel(core_ref, rows_ref, weight_ref, kept_ref, sent_ref):
    product = jnp.dot(rows_ref[...], weight_ref[...], preferred_element_type=jnp.float32)
    half = kept_ref.shape[1]
    first = core_ref[0] == 0
    kept_ref[...] = jnp.where(first, product[:, :half], product[:, half:])
    sent_ref[...] = jnp.where(first, product[:, half:], product[:, :half]).astype(sent_ref.dtype)


def unpack_kernel(first_ref, second_ref, pack_ref, out_ref):
    total = first_ref[...].astype(jnp.float32) + second_ref[...].astype(jnp.float32)
    total = total.astype(jnp.bfloat16)
    for owner in range(pack_ref.shape[0]):
        out_ref[owner] = lax.dot_general(
            pack_ref[owner], total, (((0,), (0,)), ((), ())), preferred_element_type=jnp.float32
        ).astype(out_ref.dtype)


def assemble_kernel(core_ref, mine_ref, other_ref, shift_ref, out_ref):
    owners, _, half = mine_ref.shape
    first = core_ref[0] == 0
    for owner in range(owners):
        mine = mine_ref[owner].astype(jnp.float32)
        other = other_ref[owner].astype(jnp.float32)
        for i in range(2):
            columns = slice((2 * owner + i) * half, (2 * owner + i + 1) * half)
            part = jnp.where(first, mine, other) if i == 0 else jnp.where(first, other, mine)
            out_ref[:, columns] = (part + shift_ref[:, columns]).astype(out_ref.dtype)


def exchange(values):
    return lax.all_to_all(values, "dp", split_axis=0, concat_axis=0, tiled=True)


def four_chip_local(
    patches,
    ln_gain,
    ln_shift,
    w_in,
    b_in,
    w_out,
    b_out,
    place,
    image_counts,
    text_rows,
    segments,
    norm_gain,
    q_weight,
    kv_weight,
    o_weight,
    grad_rows,
):
    bf16, f32 = jnp.bfloat16, jnp.float32
    shape_of = jax.ShapeDtypeStruct
    me = lax.axis_index("sec")
    core, chip = me & 1, me >> 1
    core_word = core.reshape(1).astype(jnp.int32)
    owners = lax.axis_size("dp")
    slots = patches.shape[0]
    padded = slots + 16 - slots % 16
    tokens, share = text_rows.shape
    features = share * 4
    first = slice(0, share // 4)
    second = slice(share // 4, share)
    layers = q_weight.shape[0]
    in_share, hidden_share = w_in.shape
    out_share = w_out.shape[1]
    packed_rows = owners * (tokens // 16)
    chunk = packed_rows // owners
    affine = jnp.stack([ln_gain, ln_shift]).astype(f32)

    normed = call(
        norm_kernel,
        shape_of((owners, padded, in_share), bf16),
        slots * owners * in_share * 10,
        slots * owners * in_share * 4,
        "normed_patches",
        in_specs=[in_smem] + in_vmem(2),
    )(image_counts, patches, affine)
    received = exchange(normed)
    pre_part, pack = call(
        lambda *refs: pack_kernel(slots, *refs),
        [shape_of((packed_rows, hidden_share), bf16), shape_of((owners, packed_rows, padded), bf16)],
        2 * packed_rows * in_share * hidden_share,
        2 * in_share * hidden_share,
        "pre_act",
    )(received, w_in)
    pre_parts = exchange(pre_part.reshape(owners, chunk, hidden_share))

    far = swap(text_rows, "sec", ACROSS)
    gathered_text = [text_rows, swap(text_rows, "sec", CORE), far, swap(far, "sec", CORE)]
    shift = b_out.reshape(1, share)
    shift_far = swap(shift, "sec", ACROSS)
    shifts = [shift, swap(shift, "sec", CORE), shift_far, swap(shift_far, "sec", CORE)]
    shifts = jnp.take(jnp.concatenate(shifts, axis=0), jnp.arange(4, dtype=jnp.int32) ^ me, axis=0)
    shifts = shifts.astype(f32).reshape(1, -1)
    gains = norm_gain.astype(f32)
    allowed, positions = doc_mask(segments[0])
    bias = jnp.where(allowed, 0.0, -1e30).astype(f32)
    cosine, sine = rope_tables(positions)
    starts = jnp.stack([(me ^ r) * share for r in range(4)]).astype(jnp.int32)
    projected = project(gathered_text[:2], starts[:2], gains, q_weight, kv_weight, 0, None)
    pre_parts, projected = lax.optimization_barrier((pre_parts, projected))
    pre_act = jnp.sum(pre_parts.astype(f32), axis=0) + b_in.astype(f32)
    hidden_units = gelu_exact(pre_act).astype(bf16)
    hidden_all = exchange(jnp.broadcast_to(hidden_units[None], (owners, chunk, hidden_share)))
    projected = project(gathered_text[2:], starts[2:], gains, q_weight, kv_weight, 0, projected)
    slot_index = jnp.arange(padded, dtype=jnp.int32)
    token_index = jnp.arange(tokens, dtype=jnp.int32)
    places = jnp.pad(place, (0, padded - slots))
    select = (places[None, :] == token_index[:, None]) & (slot_index < image_counts[0])[None, :]
    is_image = jnp.any(select, axis=1)

    hidden_all, projected, cosine, sine, bias, shifts = lax.optimization_barrier(
        (hidden_all, projected, cosine, sine, bias, shifts)
    )
    kept, sent = call(
        halves_kernel,
        [
            shape_of((packed_rows, out_share // 2), f32),
            shape_of((packed_rows, out_share // 2), bf16),
        ],
        2 * packed_rows * out_share * hidden_share,
        2 * out_share * hidden_share,
        "merged",
        in_specs=[in_smem] + in_vmem(2),
    )(core_word, hidden_all.reshape(packed_rows, hidden_share), w_out)
    chip_sum = (kept + swap(sent, "sec", CORE).astype(f32)).astype(bf16)

    def unpack(first, second):
        width = first.shape[1]
        return exchange(
            call(
                unpack_kernel,
                shape_of((owners, padded, width), bf16),
                2 * packed_rows * owners * padded * width,
                2 * owners * padded * width,
                "unpack",
            )(first, second, pack)
        )

    merged_half = unpack(chip_sum, swap(chip_sum, "sec", ACROSS))
    image_rows = call(
        assemble_kernel,
        shape_of((padded, features), bf16),
        padded * features,
        padded * features * 4,
        "image_rows",
        in_specs=[in_smem] + in_vmem(3),
    )(core_word, merged_half, swap(merged_half, "sec", CORE), shifts)

    def column(chip_index, core_bit, start):
        return (2 * chip_index + core_bit) * share + start

    images = project(
        [image_rows], jnp.zeros((1,), jnp.int32), gains, q_weight, kv_weight, 0, None
    )
    def start_rows(r, part):
        image_part = lax.dynamic_slice_in_dim(
            image_rows, column(chip ^ r, core, part.start), part.stop - part.start, 1
        )
        picked = jnp.dot(select.astype(bf16), image_part, preferred_element_type=f32)
        return jnp.where(is_image[:, None], picked.astype(bf16), gathered_text[2 * r][:, part])

    held = [start_rows(0, slice(0, share)), start_rows(1, first), start_rows(1, second)]
    projected, held = lax.optimization_barrier((projected, held))
    attended = attention(
        features, projected, cosine, sine, bias, list(images) + [select.astype(f32)]
    )

    def summed(attended, layer, r, parts):
        kept, *sent = output_product(
            attended,
            o_weight,
            layer,
            column(chip ^ r, core ^ 1, 0),
            column(chip ^ r, core, 0),
            share,
            parts,
        )
        return add_parts(kept, [swap(part, "sec", CORE) for part in sent])

    grad_rows = after(grad_rows, merged_half)
    grad_parts = call(
        split_kernel,
        shape_of((owners, padded, out_share), bf16),
        slots * owners * out_share,
        slots * owners * out_share * 4,
        "split_grads",
    )(grad_rows)
    grads_there = exchange(grad_parts)

    def grads_first():
        grad_part = call(
            pack_grads_kernel,
            shape_of((packed_rows, hidden_share), bf16),
            2 * packed_rows * out_share * hidden_share,
            2 * out_share * hidden_share,
            "hidden_grads",
        )(grads_there, pack, w_out)
        return exchange(grad_part.reshape(owners, chunk, hidden_share))

    def grads_second(parts):
        hidden_grads = jnp.sum(parts.astype(f32), axis=0)
        _, pull_gelu = jax.vjp(gelu_exact, pre_act)
        pre_grads = pull_gelu(hidden_grads)[0].astype(bf16)
        return exchange(jnp.broadcast_to(pre_grads[None], (owners, chunk, hidden_share)))

    def grads_third(pre_grads):
        back = lax.dot_general(
            pre_grads.reshape(packed_rows, hidden_share),
            w_in,
            (((1,), (1,)), ((), ())),
            preferred_element_type=f32,
        )
        back = (back + swap(back, "sec", CORE)).astype(bf16)
        return unpack(back, swap(back, "sec", ACROSS))

    def partly(old, rows, r, start, layer):
        here = jnp.stack([column(chip ^ r, core, start), column(chip ^ r, core ^ 1, start)])
        return project(
            [rows, swap(rows, "sec", CORE)],
            here.astype(jnp.int32),
            gains,
            q_weight,
            kv_weight,
            layer,
            old,
        )

    grads = None
    for layer in range(1, layers):
        other_sum = summed(attended, layer - 1, 1, 1)
        attended, other_sum = lax.optimization_barrier((attended, other_sum))
        came_here = swap(other_sum, "sec", ACROSS)
        own_sum = summed(attended, layer - 1, 0, 4)
        if grads is None:
            grads = grads_first()
        came_here, own_sum = lax.optimization_barrier((came_here, own_sum))
        came = [swap(own_sum[:, part], "sec", ACROSS) for part in (second, first)]

        now = held[0].astype(f32) + (own_sum.astype(f32) + came_here.astype(f32))
        projected = partly(None, now.astype(bf16), 0, 0, layer)
        if layer == 1:
            projected, grads = lax.optimization_barrier((projected, grads))
            grads = grads_second(grads)
        rest = []
        for i, part in ((0, second), (1, first)):
            came[i], projected = lax.optimization_barrier((came[i], projected))
            rows = (
                held[2 - i].astype(f32) + (other_sum[:, part].astype(f32) + came[i].astype(f32))
            ).astype(bf16)
            rest.append(rows)
            projected = partly(projected, rows, 1, part.start, layer)
        held = [now, rest[1], rest[0]]
        if layer == 1:
            projected, grads = lax.optimization_barrier((projected, grads))
        attended = attention(features, projected, cosine, sine, bias)

    if layers == 1:
        grads = grads_second(grads_first())
    back = lax.dot_general(
        grads.reshape(packed_rows, hidden_share),
        w_in,
        (((1,), (1,)), ((), ())),
        preferred_element_type=f32,
    )
    back = (back + swap(back, "sec", CORE)).astype(bf16)
    back_far = swap(back, "sec", ACROSS)
    attended, back_far = lax.optimization_barrier((attended, back_far))

    last = layers - 1
    other_sum = summed(attended, last, 1, 1)
    attended, other_sum = lax.optimization_barrier((attended, other_sum))
    came = [swap(other_sum[:, part], "sec", ACROSS) for part in (second, first)]
    normed_grads = unpack(back, after(back_far, other_sum))
    patch_grads = call(
        norm_back_kernel,
        shape_of(patches.shape, f32),
        slots * owners * in_share * 10,
        slots * owners * in_share * 8,
        "patch_grads",
    )(patches, normed_grads, affine)
    own_sum = summed(attended, last, 0, 1).astype(f32) + held[0]
    came[0], own_sum, patch_grads = lax.optimization_barrier((came[0], own_sum, patch_grads))
    return own_sum + jnp.concatenate(came[::-1], axis=1).astype(f32), patch_grads


def local(
    patches,
    ln_gain,
    ln_shift,
    w_in,
    b_in,
    w_out,
    b_out,
    place,
    image_counts,
    text_rows,
    segments,
    norm_gain,
    q_weight,
    kv_weight,
    o_weight,
    grad_rows,
):
    slot_count = patches.shape[0]
    tokens, share = text_rows.shape
    slot_index = jnp.arange(slot_count, dtype=jnp.int32)
    live_slot = slot_index < image_counts[0]
    merged, patch_grads = merger_rows(
        patches,
        ln_gain,
        ln_shift,
        w_in,
        b_in,
        w_out,
        live_slot,
        image_counts[0],
        grad_rows,
        lax.axis_size("dp") * (tokens // 16),
    )
    merged_local = lax.dynamic_slice_in_dim(
        merged, lax.axis_index(("sec", "mp")) * share, share, 1
    ).astype(jnp.float32)
    merged_local = (merged_local + b_out.astype(jnp.float32)).astype(jnp.bfloat16)
    token_index = jnp.arange(tokens, dtype=jnp.int32)
    select = (place[:, None] == token_index[None, :]) & live_slot[:, None]
    is_image = jnp.any(select, axis=0)
    picked = lax.dot_general(
        select.astype(jnp.bfloat16),
        merged_local,
        (((0,), (0,)), ((), ())),
        preferred_element_type=jnp.float32,
    )
    start_rows = jnp.where(is_image[:, None], picked, text_rows.astype(jnp.float32)).astype(
        jnp.bfloat16
    )
    allowed, positions = doc_mask(segments[0])
    layer_count = q_weight.shape[0]
    current = start_rows.astype(jnp.float32)
    for layer_index in range(layer_count):
        current = section_features(
            current,
            norm_gain[layer_index],
            allowed,
            positions,
            q_weight[layer_index],
            kv_weight[layer_index],
            o_weight[layer_index],
        )
    return (current, patch_grads)


def solution(mesh):
    in_specs = (
        P("dp", None),
        P(),
        P(),
        P("dp", ("sec", "mp")),
        P(("sec", "mp")),
        P(("sec", "mp"), "dp"),
        P(("sec", "mp")),
        P("dp"),
        P("dp"),
        P("dp", ("sec", "mp")),
        P("dp", None),
        P(),
        P(None, None, ("sec", "mp")),
        P(None, None, ("sec", "mp"), None),
        P(None, ("sec", "mp"), None),
        P("dp", None),
    )
    out_specs = (P("dp", ("sec", "mp")), P("dp", None))
    step = four_chip_local if mesh.shape["sec"] == 4 and mesh.shape["mp"] == 1 else local
    return jax.shard_map(step, mesh=mesh, in_specs=in_specs, out_specs=out_specs, check_vma=False)
```

```python
import math

import jax
import jax.numpy as jnp
from jax import lax
from jax.experimental import pallas as pl
from jax.experimental.pallas import tpu as pltpu
from jax.sharding import PartitionSpec as P

D = 8192
HEAD_DIM = 128


ln_eps = 1e-06
rms_eps = 1e-06
rope_base = 1000000.0


def group_norm(patch_rows, ln_gain, ln_shift):
    row_count = patch_rows.shape[0]
    grouped = patch_rows.astype(jnp.float32).reshape(row_count, -1, ln_gain.shape[0])
    center = grouped - jnp.mean(grouped, axis=-1, keepdims=True)
    spread = jnp.mean(center * center, axis=-1, keepdims=True)
    scaled = center * lax.rsqrt(spread + ln_eps) * ln_gain.astype(jnp.float32) + ln_shift.astype(
        jnp.float32
    )
    return scaled.reshape(row_count, -1)


def gelu_exact(values):
    return jax.nn.gelu(values, approximate=False)


def rotate(values, positions):
    head_depth = values.shape[-1]
    half_depth = head_depth // 2
    inv_freq = rope_base ** (-2.0 * jnp.arange(half_depth, dtype=jnp.float32) / head_depth)
    angles = positions[:, None] * inv_freq[None, :]
    cosine = jnp.cos(angles)[:, None, :]
    sine_part = jnp.sin(angles)[:, None, :]
    first_half = values[..., :half_depth]
    second = values[..., half_depth:]
    return jnp.concatenate(
        [first_half * cosine - second * sine_part, second * cosine + first_half * sine_part],
        axis=-1,
    )


def doc_mask(segment_ids):
    token_index = jnp.arange(segment_ids.shape[0], dtype=jnp.int32)
    same_doc = segment_ids[:, None] == segment_ids[None, :]
    allowed = same_doc & (token_index[None, :] <= token_index[:, None])
    positions = jnp.sum(allowed.astype(jnp.int32), axis=1) - 1
    return (allowed, positions.astype(jnp.float32))


def attend(normed, allowed, positions, q_local, kv_local):
    token_count = normed.shape[0]
    queries = jnp.dot(normed, q_local, preferred_element_type=jnp.float32).reshape(
        token_count, -1, HEAD_DIM
    )
    key_value = jnp.einsum("td,kcd->tkc", normed, kv_local, preferred_element_type=jnp.float32)
    key_value = lax.all_gather(key_value, "mp", axis=2, tiled=True)
    key_rows = rotate(key_value[:, 0:1, :], positions)[:, 0, :].astype(jnp.bfloat16)
    value_rows = key_value[:, 1, :].astype(jnp.bfloat16)
    queries = rotate(queries, positions).astype(jnp.bfloat16)
    scores = jnp.einsum("thd,sd->hts", queries, key_rows, preferred_element_type=jnp.float32) * (
        1.0 / math.sqrt(HEAD_DIM)
    )
    scores = jnp.where(allowed[None], scores, -jnp.inf)
    row_max = jnp.max(scores, axis=-1, keepdims=True)
    exp_scores = jnp.exp(scores - row_max)
    attn_weights = (exp_scores / jnp.sum(exp_scores, axis=-1, keepdims=True)).astype(jnp.bfloat16)
    attended = jnp.einsum(
        "hts,sd->thd", attn_weights, value_rows, preferred_element_type=jnp.float32
    )
    return attended.astype(jnp.bfloat16).reshape(token_count, -1)


def gather_features(rows_local):
    return lax.all_gather(rows_local, ("sec", "mp"), axis=1, tiled=True)


def section_features(rows_local, gain_row, allowed, positions, q_local, kv_local, o_local):
    share = rows_local.shape[1]
    square_sums = lax.psum(jnp.sum(rows_local * rows_local, axis=1), ("sec", "mp"))
    factor = lax.rsqrt(square_sums / D + rms_eps)
    gain_local = lax.dynamic_slice_in_dim(
        gain_row, lax.axis_index(("sec", "mp")) * share, share, 0
    ).astype(jnp.float32)
    normed_local = (rows_local * factor[:, None] * gain_local[None, :]).astype(jnp.bfloat16)
    normed = gather_features(normed_local)
    attended = attend(normed, allowed, positions, q_local, kv_local)
    summed = lax.psum_scatter(
        lax.dot_general(
            o_local, attended, (((0,), (1,)), ((), ())), preferred_element_type=jnp.float32
        ),
        ("sec", "mp"),
        scatter_dimension=0,
        tiled=True,
    )
    return rows_local + summed.T


def swap(values, axis, mask):
    size = lax.axis_size(axis)
    return lax.ppermute(values, axis, [(i, i ^ mask) for i in range(size)])


def spread_rows(values, parts):
    return lax.all_to_all(values, "dp", split_axis=0, concat_axis=0, tiled=True).reshape(
        (parts, -1) + values.shape[1:]
    )


def merger_rows(patches, ln_gain, ln_shift, w_in, b_in, w_out, live_slot, count, grad_rows, packed_rows):
    owners = lax.axis_size("dp")
    group = lax.axis_size(("sec", "mp"))
    slots = patches.shape[0]
    in_share, hidden_share = w_in.shape
    out_share = w_out.shape[1]
    share = in_share + out_share

    normed = group_norm(patches, ln_gain, ln_shift).astype(jnp.bfloat16)
    slot_grads = jnp.where(live_slot[:, None], grad_rows, jnp.zeros_like(grad_rows))
    rows = jnp.concatenate(
        [normed.reshape(slots, owners, in_share), slot_grads.reshape(slots, owners, out_share)],
        axis=2,
    ).transpose(1, 0, 2)
    count_rows = jnp.broadcast_to(count.astype(jnp.bfloat16), (owners, 8, share))
    received = lax.all_to_all(
        jnp.concatenate([rows, count_rows], axis=1), "dp", split_axis=0, concat_axis=0, tiled=True
    )
    counts = received[:, slots, 0].astype(jnp.int32)
    owner_index = jnp.arange(owners, dtype=jnp.int32)
    offsets = jnp.sum(jnp.where(owner_index[None, :] < owner_index[:, None], counts[None, :], 0), axis=1)
    slot_index = jnp.arange(slots, dtype=jnp.int32)
    target = jnp.where(
        slot_index[None, :] < counts[:, None], offsets[:, None] + slot_index[None, :], -1
    ).reshape(-1)
    pack = (jnp.arange(packed_rows, dtype=jnp.int32)[:, None] == target[None, :]).astype(jnp.bfloat16)
    packed = jnp.dot(
        pack, received[:, :slots].reshape(owners * slots, share), preferred_element_type=jnp.float32
    ).astype(jnp.bfloat16)

    pre_part = jnp.dot(packed[:, :in_share], w_in, preferred_element_type=jnp.float32)
    grad_part = lax.dot_general(
        packed[:, in_share:], w_out, (((1,), (1,)), ((), ())), preferred_element_type=jnp.float32
    )
    parts = jnp.concatenate([pre_part, grad_part], axis=1).astype(jnp.bfloat16)
    chunk = packed_rows // owners
    parts = lax.all_to_all(
        parts.reshape(owners, chunk, 2 * hidden_share), "dp", split_axis=0, concat_axis=0, tiled=True
    )
    sums = jnp.sum(parts.astype(jnp.float32), axis=0)
    pre_act = sums[:, :hidden_share] + b_in.astype(jnp.float32)
    hidden_units, pull_gelu = jax.vjp(gelu_exact, pre_act)
    pre_grads = pull_gelu(sums[:, hidden_share:])[0]
    both = jnp.concatenate([hidden_units, pre_grads], axis=1).astype(jnp.bfloat16)
    both = lax.all_to_all(
        jnp.broadcast_to(both[None], (owners, chunk, 2 * hidden_share)),
        "dp",
        split_axis=0,
        concat_axis=0,
        tiled=True,
    ).reshape(packed_rows, 2 * hidden_share)
    merged_part = jnp.dot(both[:, :hidden_share], w_out, preferred_element_type=jnp.float32)
    back_part = lax.dot_general(
        both[:, hidden_share:], w_in, (((1,), (1,)), ((), ())), preferred_element_type=jnp.float32
    )
    tail = jnp.concatenate(
        [
            merged_part.astype(jnp.bfloat16).reshape(packed_rows, group, out_share // group),
            back_part.astype(jnp.bfloat16).reshape(packed_rows, group, in_share // group),
        ],
        axis=2,
    ).reshape(packed_rows, group * (share // group))
    tail = lax.dot_general(
        pack, tail, (((0,), (0,)), ((), ())), preferred_element_type=jnp.float32
    ).astype(jnp.bfloat16)
    tail = tail.reshape(owners * slots, group, share // group).transpose(1, 0, 2)
    me = lax.axis_index(("sec", "mp"))
    parts_now = tail.astype(jnp.float32)
    index = jnp.arange(group, dtype=jnp.int32) ^ me
    parts_now = jnp.take(parts_now, index, axis=0)
    mask = 1
    while mask < group:
        pairs = parts_now.reshape(-1, 2, owners * slots, share // group)
        received = swap(pairs[:, 1].astype(jnp.bfloat16), ("sec", "mp"), mask)
        parts_now = pairs[:, 0] + received.astype(jnp.float32)
        mask *= 2
    mine = parts_now.reshape(owners, slots, share // group).astype(jnp.bfloat16)
    mine = lax.all_to_all(mine, "dp", split_axis=0, concat_axis=0, tiled=True)
    gathered = mine[None]
    mask = group // 2
    while mask >= 1:
        gathered = jnp.concatenate([gathered, swap(gathered, ("sec", "mp"), mask)], axis=0)
        mask //= 2
    order = [0]
    mask = group // 2
    while mask >= 1:
        order = order + [i ^ mask for i in order]
        mask //= 2
    place_of = [0] * group
    for where_now, relative in enumerate(order):
        place_of[relative] = where_now
    gathered = jnp.take(gathered, jnp.asarray(place_of, jnp.int32)[index], axis=0)
    gathered = gathered.transpose(2, 1, 0, 3)
    merged = gathered[..., : out_share // group].reshape(slots, owners * out_share)
    normed_grads = gathered[..., out_share // group :].reshape(slots, owners * in_share)
    _, pull_norm = jax.vjp(
        lambda values: group_norm(values, ln_gain, ln_shift), patches.astype(jnp.float32)
    )
    return merged, pull_norm(normed_grads.astype(jnp.float32))[0]


MIB = 1024 * 1024
WEIGHT = 64
CORE, ACROSS = 1, 2


def call(kernel, out_shape, flops, n_bytes, name, vmem=16 * MIB, **more):
    return pl.pallas_call(
        kernel,
        out_shape=out_shape,
        cost_estimate=pl.CostEstimate(
            flops=int(flops) // WEIGHT, bytes_accessed=int(n_bytes) // WEIGHT, transcendentals=0
        ),
        compiler_params=pltpu.CompilerParams(vmem_limit_bytes=vmem),
        name=name,
        **more,
    )


def in_vmem(count):
    return [pl.BlockSpec(memory_space=pltpu.VMEM)] * count


in_smem = pl.BlockSpec(memory_space=pltpu.SMEM)
in_hbm = pl.BlockSpec(memory_space=pltpu.HBM)


def after(values, others):
    return lax.optimization_barrier((values, others))[0]


def fetch(refs, buffers, sem):
    copies = [
        pltpu.make_async_copy(ref, buffer, sem.at[i])
        for i, (ref, buffer) in enumerate(zip(refs, buffers))
    ]
    for copy in copies:
        copy.start()
    return lambda i: copies[i].wait()


def buffers_of(arrays):
    return [pltpu.VMEM(array.shape, array.dtype) for array in arrays] + [
        pltpu.SemaphoreType.DMA((len(arrays),))
    ]


def project_kernel(layer, width, n_parts, fresh, starts_ref, gain_ref, q_hbm, kv_hbm, *refs):
    n_in = n_parts + (0 if fresh else 3)
    inputs, outs, buffers = refs[:n_in], refs[n_in : n_in + 3], refs[n_in + 3 :]
    x_refs, x_sem, q_buf, kv_buf, q_sem, kv_sem = buffers[:n_parts], *buffers[n_parts:]
    out_q, out_kv, out_sq = outs
    per_part = x_refs[0].shape[1] // width
    lanes = out_sq.shape[1]

    def place_of(block):
        part, inner = block // per_part, block % per_part
        return pl.multiple_of(starts_ref[part] + inner * width, width)

    def copies(block):
        rows = pl.ds(place_of(block), width)
        return (
            pltpu.make_async_copy(q_hbm.at[layer, rows, :], q_buf.at[block], q_sem.at[block]),
            pltpu.make_async_copy(kv_hbm.at[layer, :, :, rows], kv_buf.at[block], kv_sem.at[block]),
        )

    n_blocks = n_parts * per_part
    ready = fetch(inputs, list(x_refs) + ([] if fresh else list(outs)), x_sem)
    for block in range(n_blocks):
        for copy in copies(block):
            copy.start()
    if fresh:
        out_q[...] = jnp.zeros_like(out_q)
        out_kv[...] = jnp.zeros_like(out_kv)
        out_sq[...] = jnp.zeros_like(out_sq)
    else:
        for i in range(n_parts, n_in):
            ready(i)
    for block in range(n_blocks):
        inner = block % per_part
        if inner == 0:
            ready(block // per_part)
        rows = x_refs[block // per_part][:, inner * width : (inner + 1) * width].astype(jnp.float32)
        squares = rows * rows
        total = squares[:, :lanes]
        for i in range(1, width // lanes):
            total = total + squares[:, i * lanes : (i + 1) * lanes]
        out_sq[...] += total
        gain = gain_ref[layer : layer + 1, pl.ds(place_of(block), width)]
        normed = (rows * gain).astype(jnp.bfloat16)
        for copy in copies(block):
            copy.wait()
        out_q[...] += jnp.dot(normed, q_buf[block], preferred_element_type=jnp.float32)
        for i in range(2):
            out_kv[:, i * HEAD_DIM : (i + 1) * HEAD_DIM] += lax.dot_general(
                normed, kv_buf[block, i], (((1,), (1,)), ((), ())), preferred_element_type=jnp.float32
            )


def project(parts, starts, gains, q_weight, kv_weight, layer, old, width=512):
    rows, part_width = parts[0].shape
    n_parts = len(parts)
    n_blocks = n_parts * part_width // width
    columns = q_weight.shape[2]
    shapes = [(rows, columns), (rows, 2 * HEAD_DIM), (rows, HEAD_DIM)]
    old = [] if old is None else list(old)
    features = n_parts * part_width
    return call(
        lambda *refs: project_kernel(layer, width, n_parts, not old, *refs),
        [jax.ShapeDtypeStruct(shape, jnp.float32) for shape in shapes],
        2 * rows * features * (columns + 2 * HEAD_DIM),
        features * (columns + 2 * HEAD_DIM) * 2 + rows * features * 2,
        "project",
        vmem=48 * MIB,
        in_specs=[in_smem] + in_vmem(1) + [in_hbm] * (2 + n_parts + len(old)),
        out_specs=in_vmem(3),
        scratch_shapes=[pltpu.VMEM(part.shape, part.dtype) for part in parts]
        + [
            pltpu.SemaphoreType.DMA((n_parts + len(old),)),
            pltpu.VMEM((n_blocks, width, columns), jnp.bfloat16),
            pltpu.VMEM((n_blocks, 2, HEAD_DIM, width), jnp.bfloat16),
            pltpu.SemaphoreType.DMA((n_blocks,)),
            pltpu.SemaphoreType.DMA((n_blocks,)),
        ],
    )(starts, gains, q_weight, kv_weight, *parts, *old)


def attend_kernel(features, with_images, *refs):
    q_ref, kv_ref, sq_ref, cos_ref, sin_ref, bias_ref = refs[:6]
    out_ref = refs[-1]
    queries, key_value, squares = q_ref[...], kv_ref[...], sq_ref[...]
    if with_images:
        image_q, image_kv, image_sq, select_ref = refs[6:10]
        select = select_ref[...]
        is_image = jnp.sum(select, axis=1, keepdims=True) > 0.0

        def put(image_ref, values):
            picked = jnp.dot(
                select,
                image_ref[...],
                preferred_element_type=jnp.float32,
                precision=lax.Precision.HIGHEST,
            )
            return jnp.where(is_image, picked, values)

        queries, key_value, squares = (
            put(image_q, queries),
            put(image_kv, key_value),
            put(image_sq, squares),
        )
    factor = lax.rsqrt(jnp.sum(squares, axis=1, keepdims=True) / features + rms_eps)
    cosine, sine = cos_ref[...] * factor, sin_ref[...] * factor

    def turned(values):
        return (values * cosine + pltpu.roll(values, HEAD_DIM // 2, 1) * sine).astype(jnp.bfloat16)

    key_rows = turned(key_value[:, :HEAD_DIM])
    value_rows = (key_value[:, HEAD_DIM:] * factor).astype(jnp.bfloat16)
    bias = bias_ref[...]
    for head in range(queries.shape[1] // HEAD_DIM):
        columns = slice(head * HEAD_DIM, (head + 1) * HEAD_DIM)
        scores = lax.dot_general(
            turned(queries[:, columns]),
            key_rows,
            (((1,), (1,)), ((), ())),
            preferred_element_type=jnp.float32,
        )
        scores = scores * (1.0 / math.sqrt(HEAD_DIM)) + bias
        exp_scores = jnp.exp(scores - jnp.max(scores, axis=1, keepdims=True))
        weights = (exp_scores / jnp.sum(exp_scores, axis=1, keepdims=True)).astype(jnp.bfloat16)
        out_ref[:, columns] = jnp.dot(
            weights, value_rows, preferred_element_type=jnp.float32
        ).astype(jnp.bfloat16)


def output_kernel(layer, width, fill, starts_ref, a_ref, o_hbm, outs, out_bufs, o_buf, sem, out_sem):
    blocks = outs[-1].shape[1] // width
    per_part = blocks // (len(outs) - 1)

    def copy(block):
        start = pl.multiple_of(starts_ref[block // blocks] + block % blocks * width, width)
        return pltpu.make_async_copy(
            o_hbm.at[layer, :, pl.ds(start, width)], o_buf.at[block], sem.at[block]
        )

    for block in range(2 * blocks):
        copy(block).start()
    fill()
    leaving = []
    for block in range(2 * blocks):
        copy(block).wait()
        product = jnp.dot(a_ref[...], o_buf[block], preferred_element_type=jnp.float32)
        which, inner = (
            (block // per_part, block % per_part)
            if block < blocks
            else (len(outs) - 1, block - blocks)
        )
        columns = slice(inner * width, (inner + 1) * width)
        out_bufs[which][:, columns] = product.astype(out_bufs[which].dtype)
        leaving.append(
            pltpu.make_async_copy(
                out_bufs[which].at[:, columns], outs[which].at[:, columns], out_sem.at[block]
            )
        )
        leaving[-1].start()
    for copy_out in leaving:
        copy_out.wait()


def output_shapes(rows, count, parts):
    return [(rows, count // parts)] * parts + [(rows, count)]


def output_scratch(rows, depth, count, parts, width):
    return [pltpu.VMEM(shape, jnp.bfloat16) for shape in output_shapes(rows, count, parts)] + [
        pltpu.VMEM((2 * count // width, depth, width), jnp.bfloat16),
        pltpu.SemaphoreType.DMA((2 * count // width,)),
        pltpu.SemaphoreType.DMA((2 * count // width,)),
    ]


def output_product(attended, o_weight, layer, starts, count, parts, width=512):
    rows, depth = attended.shape
    n = parts + 1

    def kernel(starts_ref, a_hbm, o_hbm, *refs):
        outs, a_ref, a_sem = refs[:n], refs[n], refs[n + 1]
        ready = fetch([a_hbm], [a_ref], a_sem)
        output_kernel(
            layer,
            width,
            lambda: ready(0),
            starts_ref,
            a_ref,
            o_hbm,
            outs,
            refs[n + 2 : 2 * n + 2],
            *refs[2 * n + 2 :],
        )

    *sent, kept = call(
        kernel,
        [jax.ShapeDtypeStruct(s, jnp.bfloat16) for s in output_shapes(rows, count, parts)],
        4 * rows * depth * count,
        4 * depth * count,
        "output_product",
        vmem=36 * MIB,
        in_specs=[in_smem] + [in_hbm] * 2,
        out_specs=[in_hbm] * n,
        scratch_shapes=buffers_of([attended]) + output_scratch(rows, depth, count, parts, width),
    )(starts, attended, o_weight)
    return sent, kept


def attention_output(features, operands, o_weight, layer, starts, count, width=512):
    rows, depth = operands[0].shape
    n = len(operands)

    def kernel(starts_ref, *refs):
        inputs, o_hbm, out_hbm, outs = refs[:n], refs[n], refs[n + 1], refs[n + 2 : n + 4]
        buffers, in_sem = refs[n + 4 : 2 * n + 4], refs[2 * n + 4]
        out_ref, sem = refs[2 * n + 5 : 2 * n + 7]
        ready = fetch(inputs, buffers, in_sem)

        def attend():
            for i in range(n):
                ready(i)
            attend_kernel(features, n > 6, *buffers, out_ref)
            pltpu.make_async_copy(out_ref, out_hbm, sem.at[0]).start()

        output_kernel(
            layer,
            width,
            attend,
            starts_ref,
            out_ref,
            o_hbm,
            outs,
            refs[2 * n + 7 : 2 * n + 9],
            *refs[2 * n + 9 :],
        )
        pltpu.make_async_copy(out_ref, out_hbm, sem.at[0]).wait()

    attended = jax.ShapeDtypeStruct((rows, depth), jnp.bfloat16)
    attended, sent, kept = call(
        kernel,
        [attended] + [jax.ShapeDtypeStruct((rows, count), jnp.bfloat16)] * 2,
        8 * rows * rows * depth + 4 * rows * depth * count,
        4 * depth * count,
        "attention_output",
        vmem=36 * MIB,
        in_specs=[in_smem] + [in_hbm] * (n + 1),
        out_specs=[in_hbm] * 3,
        scratch_shapes=buffers_of(operands)
        + buffers_of([attended])
        + output_scratch(rows, depth, count, 1, width),
    )(starts, *operands, o_weight)
    return attended, [sent], kept


def add_kernel(n_parts, *refs):
    inputs, out_hbm, buffers = refs[: n_parts + 1], refs[n_parts + 1], refs[n_parts + 2 : -3]
    in_sem, out_ref, out_sem = refs[-3:]
    ready = fetch(inputs, buffers, in_sem)
    ready(n_parts)
    kept_ref = buffers[n_parts]
    leaving = []
    for i in range(n_parts):
        ready(i)
        width = buffers[i].shape[1]
        columns = slice(i * width, (i + 1) * width)
        total = kept_ref[:, columns].astype(jnp.float32) + buffers[i][...].astype(jnp.float32)
        out_ref[:, columns] = total.astype(out_ref.dtype)
        leaving.append(
            pltpu.make_async_copy(out_ref.at[:, columns], out_hbm.at[:, columns], out_sem.at[i])
        )
        leaving[-1].start()
    for copy_out in leaving:
        copy_out.wait()


def add_parts(kept, parts):
    n = len(parts)
    return call(
        lambda *refs: add_kernel(n, *refs),
        jax.ShapeDtypeStruct(kept.shape, kept.dtype),
        kept.size,
        6 * kept.size,
        "chip_sum",
        in_specs=[in_hbm] * (n + 1),
        out_specs=in_hbm,
        scratch_shapes=buffers_of(list(parts) + [kept])
        + [pltpu.VMEM(kept.shape, kept.dtype), pltpu.SemaphoreType.DMA((n,))],
    )(*parts, kept)


def rope_tables(positions):
    half_depth = HEAD_DIM // 2
    inv_freq = rope_base ** (-2.0 * jnp.arange(half_depth, dtype=jnp.float32) / HEAD_DIM)
    angles = positions[:, None] * inv_freq[None, :]
    cosine, sine = jnp.cos(angles), jnp.sin(angles)
    return jnp.concatenate([cosine, cosine], axis=1), jnp.concatenate([-sine, sine], axis=1)


def normalize(rows):
    center = rows - jnp.mean(rows, axis=1, keepdims=True)
    factor = lax.rsqrt(jnp.mean(center * center, axis=1, keepdims=True) + ln_eps)
    return center * factor, factor


def norm_kernel(count_ref, patch_ref, affine_ref, out_ref):
    owners, padded, in_share = out_ref.shape
    slots = patch_ref.shape[0]
    vit = affine_ref.shape[1]
    counts = jnp.full((padded - slots, vit), count_ref[0].astype(jnp.float32))
    for group in range(patch_ref.shape[1] // vit):
        rows = patch_ref[:, group * vit : (group + 1) * vit].astype(jnp.float32)
        scaled = normalize(rows)[0] * affine_ref[0:1, :] + affine_ref[1:2, :]
        scaled = jnp.concatenate([scaled, counts], axis=0).astype(out_ref.dtype)
        for i in range(vit // in_share):
            out_ref[group * (vit // in_share) + i] = scaled[:, i * in_share : (i + 1) * in_share]


def norm_back_kernel(patch_ref, grads_ref, affine_ref, out_ref):
    _, _, in_share = grads_ref.shape
    slots = patch_ref.shape[0]
    vit = affine_ref.shape[1]
    per_group = vit // in_share
    for group in range(patch_ref.shape[1] // vit):
        rows = patch_ref[:, group * vit : (group + 1) * vit].astype(jnp.float32)
        unit, factor = normalize(rows)
        grads = jnp.concatenate(
            [grads_ref[group * per_group + i].astype(jnp.float32) for i in range(per_group)], axis=1
        )[:slots]
        grads = grads * affine_ref[0:1, :]
        along = jnp.mean(grads * unit, axis=1, keepdims=True)
        out_ref[:, group * vit : (group + 1) * vit] = factor * (
            grads - jnp.mean(grads, axis=1, keepdims=True) - unit * along
        )


def split_kernel(core_ref, rows_ref, out_ref):
    owners, part_rows, width = out_ref.shape
    slots = rows_ref.shape[0]
    first = core_ref[0] == 0
    for owner in range(owners):
        rows = rows_ref[:, owner * width : (owner + 1) * width].astype(jnp.float32)
        rest = jnp.zeros((2 * part_rows - slots, width), jnp.float32)
        rows = jnp.concatenate([rows, rest], axis=0)
        rows = jnp.where(first, rows[:part_rows], rows[part_rows:])
        out_ref[owner] = rows.astype(out_ref.dtype)


def pack_kernel(slots, rows_ref, weight_ref, out_ref, pack_ref):
    owners, padded, _ = rows_ref.shape
    packed_rows = out_ref.shape[0]
    row = lax.broadcasted_iota(jnp.int32, (packed_rows, padded), 0).astype(jnp.float32)
    slot = lax.broadcasted_iota(jnp.int32, (packed_rows, padded), 1).astype(jnp.float32)
    offset = jnp.zeros((1, 1), jnp.float32)
    packed = jnp.zeros((packed_rows, rows_ref.shape[2]), jnp.float32)
    for owner in range(owners):
        rows = rows_ref[owner]
        count = rows.astype(jnp.float32)[slots : slots + 1, 0:1]
        chosen = jnp.where((row == offset + slot) & (slot < count), 1.0, 0.0).astype(jnp.bfloat16)
        pack_ref[owner] = chosen
        packed = packed + jnp.dot(chosen, rows, preferred_element_type=jnp.float32)
        offset = offset + count
    out_ref[...] = jnp.dot(
        packed.astype(jnp.bfloat16), weight_ref[...], preferred_element_type=jnp.float32
    ).astype(out_ref.dtype)


def pack_grads_kernel(core_ref, mine_ref, other_ref, pack_ref, weight_ref, out_ref):
    packed = jnp.zeros((out_ref.shape[0], mine_ref.shape[2]), jnp.float32)
    first = core_ref[0] == 0
    padded = pack_ref.shape[2]
    for owner in range(mine_ref.shape[0]):
        mine = mine_ref[owner].astype(jnp.float32)
        other = other_ref[owner].astype(jnp.float32)
        rows = jnp.concatenate(
            [jnp.where(first, mine, other), jnp.where(first, other, mine)], axis=0
        )
        packed = packed + jnp.dot(
            pack_ref[owner],
            rows[:padded].astype(jnp.bfloat16),
            preferred_element_type=jnp.float32,
        )
    out_ref[...] = lax.dot_general(
        packed.astype(jnp.bfloat16),
        weight_ref[...],
        (((1,), (1,)), ((), ())),
        preferred_element_type=jnp.float32,
    ).astype(out_ref.dtype)


def halves_kernel(core_ref, rows_ref, weight_ref, kept_ref, sent_ref):
    product = jnp.dot(rows_ref[...], weight_ref[...], preferred_element_type=jnp.float32)
    half = kept_ref.shape[1]
    first = core_ref[0] == 0
    kept_ref[...] = jnp.where(first, product[:, :half], product[:, half:])
    sent_ref[...] = jnp.where(first, product[:, half:], product[:, :half]).astype(sent_ref.dtype)


def unpack_kernel(first_ref, second_ref, pack_ref, out_ref):
    total = first_ref[...].astype(jnp.float32) + second_ref[...].astype(jnp.float32)
    total = total.astype(jnp.bfloat16)
    for owner in range(pack_ref.shape[0]):
        out_ref[owner] = lax.dot_general(
            pack_ref[owner], total, (((0,), (0,)), ((), ())), preferred_element_type=jnp.float32
        ).astype(out_ref.dtype)


def assemble_kernel(core_ref, shift_ref, mine_hbm, other_hbm, out_ref, mine_ref, other_ref, sem):
    owners, _, half = mine_ref.shape
    first = core_ref[0] == 0
    ready = fetch([mine_hbm, other_hbm], [mine_ref, other_ref], sem)
    ready(0)
    ready(1)
    for owner in range(owners):
        mine = mine_ref[owner].astype(jnp.float32)
        other = other_ref[owner].astype(jnp.float32)
        for i in range(2):
            columns = slice((2 * owner + i) * half, (2 * owner + i + 1) * half)
            part = jnp.where(first, mine, other) if i == 0 else jnp.where(first, other, mine)
            out_ref[:, columns] = (part + shift_ref[:, columns]).astype(out_ref.dtype)


def back_kernel(me_ref, weight_ref, *refs):
    inputs, (out_ref, buf, sem) = refs[:-3], refs[-3:]
    turns = len(inputs)
    ready = fetch(inputs, [buf.at[turn] for turn in range(turns)], sem)
    for turn in range(turns):
        ready(turn)
    line, side = me_ref[0] // 2, me_ref[0] % 2
    rows = jnp.concatenate(
        [
            buf[(line + turns - owner // 2) % turns, (side + owner) % 2].astype(jnp.float32)
            for owner in range(2 * turns)
        ],
        axis=0,
    ).astype(jnp.bfloat16)
    out_ref[...] = lax.dot_general(
        rows, weight_ref[...], (((1,), (1,)), ((), ())), preferred_element_type=jnp.float32
    )


def gather_turns(values):
    owners = lax.axis_size("dp")
    pair = jnp.stack([values, swap(values, "dp", 1)])
    return [pair] + [
        lax.ppermute(pair, "dp", [(i, (i + 2 * turn) % owners) for i in range(owners)])
        for turn in range(1, owners // 2)
    ]


def exchange(values):
    return lax.all_to_all(values, "dp", split_axis=0, concat_axis=0, tiled=True)


def four_chip_local(
    patches,
    ln_gain,
    ln_shift,
    w_in,
    b_in,
    w_out,
    b_out,
    place,
    image_counts,
    text_rows,
    segments,
    norm_gain,
    q_weight,
    kv_weight,
    o_weight,
    grad_rows,
):
    bf16, f32 = jnp.bfloat16, jnp.float32
    shape_of = jax.ShapeDtypeStruct
    me = lax.axis_index("sec")
    core, chip = me & 1, me >> 1
    core_word = core.reshape(1).astype(jnp.int32)
    owners = lax.axis_size("dp")
    slots = patches.shape[0]
    padded = slots + 16 - slots % 16
    tokens, share = text_rows.shape
    features = share * 4
    layers = q_weight.shape[0]
    in_share, hidden_share = w_in.shape
    out_share = w_out.shape[1]
    packed_rows = owners * (tokens // 16)
    chunk = packed_rows // owners
    affine = jnp.stack([ln_gain, ln_shift]).astype(f32)

    normed = call(
        norm_kernel,
        shape_of((owners, padded, in_share), bf16),
        slots * owners * in_share * 10,
        slots * owners * in_share * 4,
        "normed_patches",
        in_specs=[in_smem] + in_vmem(2),
    )(image_counts, patches, affine)
    received = exchange(normed)

    far = swap(text_rows, "sec", ACROSS)
    gathered_text = [text_rows, swap(text_rows, "sec", CORE)]
    gains = norm_gain.astype(f32)
    starts = jnp.stack([(me ^ r) * share for r in range(4)]).astype(jnp.int32)
    projected = project(gathered_text, starts[:2], gains, q_weight, kv_weight, 0, None)
    received, projected, far = lax.optimization_barrier((received, projected, far))
    gathered_text += [far, swap(far, "sec", CORE)]
    pre_part, pack = call(
        lambda *refs: pack_kernel(slots, *refs),
        [shape_of((packed_rows, hidden_share), bf16), shape_of((owners, packed_rows, padded), bf16)],
        2 * packed_rows * in_share * hidden_share,
        2 * in_share * hidden_share,
        "pre_act",
    )(received, w_in)
    pre_parts = exchange(pre_part.reshape(owners, chunk, hidden_share))

    shift = b_out.reshape(1, share)
    shift_far = swap(shift, "sec", ACROSS)
    shifts = [shift, swap(shift, "sec", CORE), shift_far, swap(shift_far, "sec", CORE)]
    shifts = jnp.take(jnp.concatenate(shifts, axis=0), jnp.arange(4, dtype=jnp.int32) ^ me, axis=0)
    shifts = shifts.astype(f32).reshape(1, -1)
    allowed, positions = doc_mask(segments[0])
    bias = jnp.where(allowed, 0.0, -1e30).astype(f32)
    cosine, sine = rope_tables(positions)
    projected = project(gathered_text[2:], starts[2:], gains, q_weight, kv_weight, 0, projected)
    pre_act = jnp.sum(pre_parts.astype(f32), axis=0) + b_in.astype(f32)
    hidden_units = gelu_exact(pre_act).astype(bf16)
    hidden_all = exchange(jnp.broadcast_to(hidden_units[None], (owners, chunk, hidden_share)))
    slot_index = jnp.arange(padded, dtype=jnp.int32)
    token_index = jnp.arange(tokens, dtype=jnp.int32)
    places = jnp.pad(place, (0, padded - slots))
    select = (places[None, :] == token_index[:, None]) & (slot_index < image_counts[0])[None, :]
    is_image = jnp.any(select, axis=1)

    hidden_all, projected, cosine, sine, bias, shifts = lax.optimization_barrier(
        (hidden_all, projected, cosine, sine, bias, shifts)
    )
    kept, sent = call(
        halves_kernel,
        [
            shape_of((packed_rows, out_share // 2), f32),
            shape_of((packed_rows, out_share // 2), bf16),
        ],
        2 * packed_rows * out_share * hidden_share,
        2 * out_share * hidden_share,
        "merged",
        in_specs=[in_smem] + in_vmem(2),
    )(core_word, hidden_all.reshape(packed_rows, hidden_share), w_out)
    chip_sum = (kept + swap(sent, "sec", CORE).astype(f32)).astype(bf16)

    def unpack(first, second):
        width = first.shape[1]
        return exchange(
            call(
                unpack_kernel,
                shape_of((owners, padded, width), bf16),
                2 * packed_rows * owners * padded * width,
                2 * owners * padded * width,
                "unpack",
            )(first, second, pack)
        )

    merged_half = unpack(chip_sum, swap(chip_sum, "sec", ACROSS))
    image_rows = call(
        assemble_kernel,
        shape_of((padded, features), bf16),
        padded * features,
        padded * features * 4,
        "image_rows",
        in_specs=[in_smem] + in_vmem(1) + [in_hbm] * 2,
        scratch_shapes=buffers_of([merged_half] * 2),
    )(core_word, shifts, merged_half, swap(merged_half, "sec", CORE))

    def column(chip_index, core_bit):
        return (2 * chip_index + core_bit) * share

    images = project(
        [image_rows], jnp.zeros((1,), jnp.int32), gains, q_weight, kv_weight, 0, None
    )

    def start_rows(r):
        image_part = lax.dynamic_slice_in_dim(image_rows, column(chip ^ r, core), share, 1)
        picked = jnp.dot(select.astype(bf16), image_part, preferred_element_type=f32)
        return jnp.where(is_image[:, None], picked.astype(bf16), gathered_text[2 * r])

    def columns_of(r):
        return jnp.stack([column(chip ^ r, core ^ 1), column(chip ^ r, core)]).astype(
            jnp.int32
        )

    def shared(sent):
        return [swap(part, "sec", CORE) for part in sent]

    grad_rows = after(grad_rows, merged_half)
    grad_parts = call(
        split_kernel,
        shape_of((owners, (padded + 16) // 32 * 16, out_share), bf16),
        slots * owners * out_share,
        slots * owners * out_share * 4,
        "split_grads",
        in_specs=[in_smem] + in_vmem(1),
    )(core_word, grad_rows)
    grads_there = exchange(grad_parts)

    def grads_first():
        grad_part = call(
            pack_grads_kernel,
            shape_of((packed_rows, hidden_share), bf16),
            2 * packed_rows * out_share * hidden_share,
            2 * out_share * hidden_share,
            "hidden_grads",
            in_specs=[in_smem] + in_vmem(4),
        )(core_word, grads_there, swap(grads_there, "sec", CORE), pack, w_out)
        return grad_part.reshape(owners, chunk, hidden_share)

    def grads_second(parts):
        hidden_grads = jnp.sum(parts.astype(f32), axis=0)
        _, pull_gelu = jax.vjp(gelu_exact, pre_act)
        pre_grads = pull_gelu(hidden_grads)[0].astype(bf16)
        turns = gather_turns(pre_grads)
        back = call(
            back_kernel,
            shape_of((packed_rows, in_share), f32),
            2 * packed_rows * in_share * hidden_share,
            2 * in_share * hidden_share,
            "normed_grads",
            in_specs=[in_smem] + in_vmem(1) + [in_hbm] * len(turns),
            scratch_shapes=[
                pltpu.VMEM((len(turns), 2, chunk, hidden_share), bf16),
                pltpu.SemaphoreType.DMA((len(turns),)),
            ],
        )(lax.axis_index("dp").reshape(1).astype(jnp.int32), w_in, *turns)
        return (back + swap(back, "sec", CORE)).astype(bf16)

    def grads_third(pre_grads):
        back = lax.dot_general(
            pre_grads.reshape(packed_rows, hidden_share),
            w_in,
            (((1,), (1,)), ((), ())),
            preferred_element_type=f32,
        )
        back = (back + swap(back, "sec", CORE)).astype(bf16)
        return unpack(back, swap(back, "sec", ACROSS))

    operands = list(projected) + [cosine, sine, bias] + list(images) + [select.astype(f32)]

    def partly(old, rows, r, layer):
        here = jnp.stack([column(chip ^ r, core), column(chip ^ r, core ^ 1)])
        return project(
            [rows, swap(rows, "sec", CORE)],
            here.astype(jnp.int32),
            gains,
            q_weight,
            kv_weight,
            layer,
            old,
        )

    grads, held = None, None
    for layer in range(1, layers):
        attended, sent, kept = attention_output(
            features, operands, o_weight, layer - 1, columns_of(1), share
        )
        other_sum = add_parts(kept, shared(sent))
        attended = after(attended, other_sum)
        came_here = swap(other_sum, "sec", ACROSS)
        sent, kept = output_product(attended, o_weight, layer - 1, columns_of(0), share, 4)
        own_sum = add_parts(kept, shared(sent))
        if held is None:
            held = [start_rows(0), start_rows(1)]
        if grads is None:
            grads_there = after(grads_there, own_sum)
            grads = grads_first()
            came_here = after(came_here, grads)
            grads = exchange(grads)
        came_here = after(came_here, own_sum)
        came_there = swap(own_sum, "sec", ACROSS)
        now = held[0].astype(f32) + (own_sum.astype(f32) + came_here.astype(f32))
        projected = partly(None, now.astype(bf16), 0, layer)
        if layer == 1:
            grads = grads_second(grads)
        came_there = after(came_there, (projected, grads) if layer == 1 else projected)
        there = held[1].astype(f32) + (other_sum.astype(f32) + came_there.astype(f32))
        there = there.astype(bf16)
        projected = partly(projected, there, 1, layer)
        held = [now, there]
        operands = list(projected) + [cosine, sine, bias]

    if layers == 1:
        held = [start_rows(0)]
        grads = grads_second(exchange(grads_first()))
    back = grads
    back_far = swap(back, "sec", ACROSS)
    operands = after(operands, back_far)

    last = layers - 1
    attended, sent, kept = attention_output(
        features, operands, o_weight, last, columns_of(1), share
    )
    other_sum = add_parts(kept, shared(sent))
    attended = after(attended, other_sum)
    back_far = after(back_far, other_sum)
    came = swap(other_sum, "sec", ACROSS)
    normed_grads = unpack(back, back_far)
    sent, kept = output_product(attended, o_weight, last, columns_of(0), share, 4)
    own_sum = add_parts(kept, shared(sent))
    patch_grads = call(
        norm_back_kernel,
        shape_of(patches.shape, f32),
        slots * owners * in_share * 10,
        slots * owners * in_share * 8,
        "patch_grads",
    )(patches, normed_grads, affine)
    own_sum = own_sum.astype(f32) + held[0].astype(f32)
    came, own_sum, patch_grads = lax.optimization_barrier((came, own_sum, patch_grads))
    return own_sum + came.astype(f32), patch_grads


def local(
    patches,
    ln_gain,
    ln_shift,
    w_in,
    b_in,
    w_out,
    b_out,
    place,
    image_counts,
    text_rows,
    segments,
    norm_gain,
    q_weight,
    kv_weight,
    o_weight,
    grad_rows,
):
    slot_count = patches.shape[0]
    tokens, share = text_rows.shape
    slot_index = jnp.arange(slot_count, dtype=jnp.int32)
    live_slot = slot_index < image_counts[0]
    merged, patch_grads = merger_rows(
        patches,
        ln_gain,
        ln_shift,
        w_in,
        b_in,
        w_out,
        live_slot,
        image_counts[0],
        grad_rows,
        lax.axis_size("dp") * (tokens // 16),
    )
    merged_local = lax.dynamic_slice_in_dim(
        merged, lax.axis_index(("sec", "mp")) * share, share, 1
    ).astype(jnp.float32)
    merged_local = (merged_local + b_out.astype(jnp.float32)).astype(jnp.bfloat16)
    token_index = jnp.arange(tokens, dtype=jnp.int32)
    select = (place[:, None] == token_index[None, :]) & live_slot[:, None]
    is_image = jnp.any(select, axis=0)
    picked = lax.dot_general(
        select.astype(jnp.bfloat16),
        merged_local,
        (((0,), (0,)), ((), ())),
        preferred_element_type=jnp.float32,
    )
    start_rows = jnp.where(is_image[:, None], picked, text_rows.astype(jnp.float32)).astype(
        jnp.bfloat16
    )
    allowed, positions = doc_mask(segments[0])
    layer_count = q_weight.shape[0]
    current = start_rows.astype(jnp.float32)
    for layer_index in range(layer_count):
        current = section_features(
            current,
            norm_gain[layer_index],
            allowed,
            positions,
            q_weight[layer_index],
            kv_weight[layer_index],
            o_weight[layer_index],
        )
    return (current, patch_grads)


def solution(mesh):
    in_specs = (
        P("dp", None),
        P(),
        P(),
        P("dp", ("sec", "mp")),
        P(("sec", "mp")),
        P(("sec", "mp"), "dp"),
        P(("sec", "mp")),
        P("dp"),
        P("dp"),
        P("dp", ("sec", "mp")),
        P("dp", None),
        P(),
        P(None, None, ("sec", "mp")),
        P(None, None, ("sec", "mp"), None),
        P(None, ("sec", "mp"), None),
        P("dp", None),
    )
    out_specs = (P("dp", ("sec", "mp")), P("dp", None))
    step = four_chip_local if mesh.shape["sec"] == 4 and mesh.shape["mp"] == 1 else local
    return jax.shard_map(step, mesh=mesh, in_specs=in_specs, out_specs=out_specs, check_vma=False)
```

```python
import math

import jax
import jax.numpy as jnp
from jax import lax
from jax.experimental import pallas as pl
from jax.experimental.pallas import tpu as pltpu
from jax.sharding import PartitionSpec as P

D = 8192
HEAD_DIM = 128


ln_eps = 1e-06
rms_eps = 1e-06
rope_base = 1000000.0


def group_norm(patch_rows, ln_gain, ln_shift):
    row_count = patch_rows.shape[0]
    grouped = patch_rows.astype(jnp.float32).reshape(row_count, -1, ln_gain.shape[0])
    center = grouped - jnp.mean(grouped, axis=-1, keepdims=True)
    spread = jnp.mean(center * center, axis=-1, keepdims=True)
    scaled = center * lax.rsqrt(spread + ln_eps) * ln_gain.astype(jnp.float32) + ln_shift.astype(
        jnp.float32
    )
    return scaled.reshape(row_count, -1)


def gelu_exact(values):
    return jax.nn.gelu(values, approximate=False)


def rotate(values, positions):
    head_depth = values.shape[-1]
    half_depth = head_depth // 2
    inv_freq = rope_base ** (-2.0 * jnp.arange(half_depth, dtype=jnp.float32) / head_depth)
    angles = positions[:, None] * inv_freq[None, :]
    cosine = jnp.cos(angles)[:, None, :]
    sine_part = jnp.sin(angles)[:, None, :]
    first_half = values[..., :half_depth]
    second = values[..., half_depth:]
    return jnp.concatenate(
        [first_half * cosine - second * sine_part, second * cosine + first_half * sine_part],
        axis=-1,
    )


def doc_mask(segment_ids):
    token_index = jnp.arange(segment_ids.shape[0], dtype=jnp.int32)
    same_doc = segment_ids[:, None] == segment_ids[None, :]
    allowed = same_doc & (token_index[None, :] <= token_index[:, None])
    positions = jnp.sum(allowed.astype(jnp.int32), axis=1) - 1
    return (allowed, positions.astype(jnp.float32))


def attend(normed, allowed, positions, q_local, kv_local):
    token_count = normed.shape[0]
    queries = jnp.dot(normed, q_local, preferred_element_type=jnp.float32).reshape(
        token_count, -1, HEAD_DIM
    )
    key_value = jnp.einsum("td,kcd->tkc", normed, kv_local, preferred_element_type=jnp.float32)
    key_value = lax.all_gather(key_value, "mp", axis=2, tiled=True)
    key_rows = rotate(key_value[:, 0:1, :], positions)[:, 0, :].astype(jnp.bfloat16)
    value_rows = key_value[:, 1, :].astype(jnp.bfloat16)
    queries = rotate(queries, positions).astype(jnp.bfloat16)
    scores = jnp.einsum("thd,sd->hts", queries, key_rows, preferred_element_type=jnp.float32) * (
        1.0 / math.sqrt(HEAD_DIM)
    )
    scores = jnp.where(allowed[None], scores, -jnp.inf)
    row_max = jnp.max(scores, axis=-1, keepdims=True)
    exp_scores = jnp.exp(scores - row_max)
    attn_weights = (exp_scores / jnp.sum(exp_scores, axis=-1, keepdims=True)).astype(jnp.bfloat16)
    attended = jnp.einsum(
        "hts,sd->thd", attn_weights, value_rows, preferred_element_type=jnp.float32
    )
    return attended.astype(jnp.bfloat16).reshape(token_count, -1)


def gather_features(rows_local):
    return lax.all_gather(rows_local, ("sec", "mp"), axis=1, tiled=True)


def section_features(rows_local, gain_row, allowed, positions, q_local, kv_local, o_local):
    share = rows_local.shape[1]
    square_sums = lax.psum(jnp.sum(rows_local * rows_local, axis=1), ("sec", "mp"))
    factor = lax.rsqrt(square_sums / D + rms_eps)
    gain_local = lax.dynamic_slice_in_dim(
        gain_row, lax.axis_index(("sec", "mp")) * share, share, 0
    ).astype(jnp.float32)
    normed_local = (rows_local * factor[:, None] * gain_local[None, :]).astype(jnp.bfloat16)
    normed = gather_features(normed_local)
    attended = attend(normed, allowed, positions, q_local, kv_local)
    summed = lax.psum_scatter(
        lax.dot_general(
            o_local, attended, (((0,), (1,)), ((), ())), preferred_element_type=jnp.float32
        ),
        ("sec", "mp"),
        scatter_dimension=0,
        tiled=True,
    )
    return rows_local + summed.T


def swap(values, axis, mask):
    size = lax.axis_size(axis)
    return lax.ppermute(values, axis, [(i, i ^ mask) for i in range(size)])


def spread_rows(values, parts):
    return lax.all_to_all(values, "dp", split_axis=0, concat_axis=0, tiled=True).reshape(
        (parts, -1) + values.shape[1:]
    )


def merger_rows(patches, ln_gain, ln_shift, w_in, b_in, w_out, live_slot, count, grad_rows, packed_rows):
    owners = lax.axis_size("dp")
    group = lax.axis_size(("sec", "mp"))
    slots = patches.shape[0]
    in_share, hidden_share = w_in.shape
    out_share = w_out.shape[1]
    share = in_share + out_share

    normed = group_norm(patches, ln_gain, ln_shift).astype(jnp.bfloat16)
    slot_grads = jnp.where(live_slot[:, None], grad_rows, jnp.zeros_like(grad_rows))
    rows = jnp.concatenate(
        [normed.reshape(slots, owners, in_share), slot_grads.reshape(slots, owners, out_share)],
        axis=2,
    ).transpose(1, 0, 2)
    count_rows = jnp.broadcast_to(count.astype(jnp.bfloat16), (owners, 8, share))
    received = lax.all_to_all(
        jnp.concatenate([rows, count_rows], axis=1), "dp", split_axis=0, concat_axis=0, tiled=True
    )
    counts = received[:, slots, 0].astype(jnp.int32)
    owner_index = jnp.arange(owners, dtype=jnp.int32)
    offsets = jnp.sum(jnp.where(owner_index[None, :] < owner_index[:, None], counts[None, :], 0), axis=1)
    slot_index = jnp.arange(slots, dtype=jnp.int32)
    target = jnp.where(
        slot_index[None, :] < counts[:, None], offsets[:, None] + slot_index[None, :], -1
    ).reshape(-1)
    pack = (jnp.arange(packed_rows, dtype=jnp.int32)[:, None] == target[None, :]).astype(jnp.bfloat16)
    packed = jnp.dot(
        pack, received[:, :slots].reshape(owners * slots, share), preferred_element_type=jnp.float32
    ).astype(jnp.bfloat16)

    pre_part = jnp.dot(packed[:, :in_share], w_in, preferred_element_type=jnp.float32)
    grad_part = lax.dot_general(
        packed[:, in_share:], w_out, (((1,), (1,)), ((), ())), preferred_element_type=jnp.float32
    )
    parts = jnp.concatenate([pre_part, grad_part], axis=1).astype(jnp.bfloat16)
    chunk = packed_rows // owners
    parts = lax.all_to_all(
        parts.reshape(owners, chunk, 2 * hidden_share), "dp", split_axis=0, concat_axis=0, tiled=True
    )
    sums = jnp.sum(parts.astype(jnp.float32), axis=0)
    pre_act = sums[:, :hidden_share] + b_in.astype(jnp.float32)
    hidden_units, pull_gelu = jax.vjp(gelu_exact, pre_act)
    pre_grads = pull_gelu(sums[:, hidden_share:])[0]
    both = jnp.concatenate([hidden_units, pre_grads], axis=1).astype(jnp.bfloat16)
    both = lax.all_to_all(
        jnp.broadcast_to(both[None], (owners, chunk, 2 * hidden_share)),
        "dp",
        split_axis=0,
        concat_axis=0,
        tiled=True,
    ).reshape(packed_rows, 2 * hidden_share)
    merged_part = jnp.dot(both[:, :hidden_share], w_out, preferred_element_type=jnp.float32)
    back_part = lax.dot_general(
        both[:, hidden_share:], w_in, (((1,), (1,)), ((), ())), preferred_element_type=jnp.float32
    )
    tail = jnp.concatenate(
        [
            merged_part.astype(jnp.bfloat16).reshape(packed_rows, group, out_share // group),
            back_part.astype(jnp.bfloat16).reshape(packed_rows, group, in_share // group),
        ],
        axis=2,
    ).reshape(packed_rows, group * (share // group))
    tail = lax.dot_general(
        pack, tail, (((0,), (0,)), ((), ())), preferred_element_type=jnp.float32
    ).astype(jnp.bfloat16)
    tail = tail.reshape(owners * slots, group, share // group).transpose(1, 0, 2)
    me = lax.axis_index(("sec", "mp"))
    parts_now = tail.astype(jnp.float32)
    index = jnp.arange(group, dtype=jnp.int32) ^ me
    parts_now = jnp.take(parts_now, index, axis=0)
    mask = 1
    while mask < group:
        pairs = parts_now.reshape(-1, 2, owners * slots, share // group)
        received = swap(pairs[:, 1].astype(jnp.bfloat16), ("sec", "mp"), mask)
        parts_now = pairs[:, 0] + received.astype(jnp.float32)
        mask *= 2
    mine = parts_now.reshape(owners, slots, share // group).astype(jnp.bfloat16)
    mine = lax.all_to_all(mine, "dp", split_axis=0, concat_axis=0, tiled=True)
    gathered = mine[None]
    mask = group // 2
    while mask >= 1:
        gathered = jnp.concatenate([gathered, swap(gathered, ("sec", "mp"), mask)], axis=0)
        mask //= 2
    order = [0]
    mask = group // 2
    while mask >= 1:
        order = order + [i ^ mask for i in order]
        mask //= 2
    place_of = [0] * group
    for where_now, relative in enumerate(order):
        place_of[relative] = where_now
    gathered = jnp.take(gathered, jnp.asarray(place_of, jnp.int32)[index], axis=0)
    gathered = gathered.transpose(2, 1, 0, 3)
    merged = gathered[..., : out_share // group].reshape(slots, owners * out_share)
    normed_grads = gathered[..., out_share // group :].reshape(slots, owners * in_share)
    _, pull_norm = jax.vjp(
        lambda values: group_norm(values, ln_gain, ln_shift), patches.astype(jnp.float32)
    )
    return merged, pull_norm(normed_grads.astype(jnp.float32))[0]


MIB = 1024 * 1024
WEIGHT = 64
CORE, ACROSS = 1, 2


def call(kernel, out_shape, flops, n_bytes, name, vmem=16 * MIB, **more):
    return pl.pallas_call(
        kernel,
        out_shape=out_shape,
        cost_estimate=pl.CostEstimate(
            flops=int(flops) // WEIGHT, bytes_accessed=int(n_bytes) // WEIGHT, transcendentals=0
        ),
        compiler_params=pltpu.CompilerParams(vmem_limit_bytes=vmem),
        name=name,
        **more,
    )


def in_vmem(count):
    return [pl.BlockSpec(memory_space=pltpu.VMEM)] * count


in_smem = pl.BlockSpec(memory_space=pltpu.SMEM)
in_hbm = pl.BlockSpec(memory_space=pltpu.HBM)


def after(values, others):
    return lax.optimization_barrier((values, others))[0]


def fetch(refs, buffers, sem):
    copies = [
        pltpu.make_async_copy(ref, buffer, sem.at[i])
        for i, (ref, buffer) in enumerate(zip(refs, buffers))
    ]
    for copy in copies:
        copy.start()
    return lambda i: copies[i].wait()


def buffers_of(arrays):
    return [pltpu.VMEM(array.shape, array.dtype) for array in arrays] + [
        pltpu.SemaphoreType.DMA((len(arrays),))
    ]


def project_kernel(layer, width, n_parts, fresh, starts_ref, gain_ref, q_hbm, kv_hbm, *refs):
    n_in = n_parts + (0 if fresh else 3)
    inputs, outs, buffers = refs[:n_in], refs[n_in : n_in + 3], refs[n_in + 3 :]
    x_refs, x_sem, q_buf, kv_buf, q_sem, kv_sem = buffers[:n_parts], *buffers[n_parts:]
    out_q, out_kv, out_sq = outs
    per_part = x_refs[0].shape[1] // width
    lanes = out_sq.shape[1]

    def place_of(block):
        part, inner = block // per_part, block % per_part
        return pl.multiple_of(starts_ref[part] + inner * width, width)

    def copies(block):
        rows = pl.ds(place_of(block), width)
        return (
            pltpu.make_async_copy(q_hbm.at[layer, rows, :], q_buf.at[block], q_sem.at[block]),
            pltpu.make_async_copy(kv_hbm.at[layer, :, :, rows], kv_buf.at[block], kv_sem.at[block]),
        )

    n_blocks = n_parts * per_part
    ready = fetch(inputs, list(x_refs) + ([] if fresh else list(outs)), x_sem)
    for block in range(n_blocks):
        for copy in copies(block):
            copy.start()
    if fresh:
        out_q[...] = jnp.zeros_like(out_q)
        out_kv[...] = jnp.zeros_like(out_kv)
        out_sq[...] = jnp.zeros_like(out_sq)
    else:
        for i in range(n_parts, n_in):
            ready(i)
    for block in range(n_blocks):
        inner = block % per_part
        if inner == 0:
            ready(block // per_part)
        rows = x_refs[block // per_part][:, inner * width : (inner + 1) * width].astype(jnp.float32)
        squares = rows * rows
        total = squares[:, :lanes]
        for i in range(1, width // lanes):
            total = total + squares[:, i * lanes : (i + 1) * lanes]
        out_sq[...] += total
        gain = gain_ref[layer : layer + 1, pl.ds(place_of(block), width)]
        normed = (rows * gain).astype(jnp.bfloat16)
        for copy in copies(block):
            copy.wait()
        out_q[...] += jnp.dot(normed, q_buf[block], preferred_element_type=jnp.float32)
        for i in range(2):
            out_kv[:, i * HEAD_DIM : (i + 1) * HEAD_DIM] += lax.dot_general(
                normed, kv_buf[block, i], (((1,), (1,)), ((), ())), preferred_element_type=jnp.float32
            )


def project(parts, starts, gains, q_weight, kv_weight, layer, old, width=512):
    rows, part_width = parts[0].shape
    n_parts = len(parts)
    n_blocks = n_parts * part_width // width
    columns = q_weight.shape[2]
    shapes = [(rows, columns), (rows, 2 * HEAD_DIM), (rows, HEAD_DIM)]
    old = [] if old is None else list(old)
    features = n_parts * part_width
    return call(
        lambda *refs: project_kernel(layer, width, n_parts, not old, *refs),
        [jax.ShapeDtypeStruct(shape, jnp.float32) for shape in shapes],
        2 * rows * features * (columns + 2 * HEAD_DIM),
        features * (columns + 2 * HEAD_DIM) * 2 + rows * features * 2,
        "project",
        vmem=48 * MIB,
        in_specs=[in_smem] + in_vmem(1) + [in_hbm] * (2 + n_parts + len(old)),
        out_specs=in_vmem(3),
        scratch_shapes=[pltpu.VMEM(part.shape, part.dtype) for part in parts]
        + [
            pltpu.SemaphoreType.DMA((n_parts + len(old),)),
            pltpu.VMEM((n_blocks, width, columns), jnp.bfloat16),
            pltpu.VMEM((n_blocks, 2, HEAD_DIM, width), jnp.bfloat16),
            pltpu.SemaphoreType.DMA((n_blocks,)),
            pltpu.SemaphoreType.DMA((n_blocks,)),
        ],
    )(starts, gains, q_weight, kv_weight, *parts, *old)


def attend_kernel(features, with_images, *refs):
    q_ref, kv_ref, sq_ref, cos_ref, sin_ref, bias_ref = refs[:6]
    out_ref = refs[-1]
    queries, key_value, squares = q_ref[...], kv_ref[...], sq_ref[...]
    if with_images:
        image_q, image_kv, image_sq, select_ref = refs[6:10]
        select = select_ref[...]
        is_image = jnp.sum(select, axis=1, keepdims=True) > 0.0

        def put(image_ref, values):
            picked = jnp.dot(
                select,
                image_ref[...],
                preferred_element_type=jnp.float32,
                precision=lax.Precision.HIGHEST,
            )
            return jnp.where(is_image, picked, values)

        queries, key_value, squares = (
            put(image_q, queries),
            put(image_kv, key_value),
            put(image_sq, squares),
        )
    factor = lax.rsqrt(jnp.sum(squares, axis=1, keepdims=True) / features + rms_eps)
    cosine, sine = cos_ref[...] * factor, sin_ref[...] * factor

    def turned(values):
        return (values * cosine + pltpu.roll(values, HEAD_DIM // 2, 1) * sine).astype(jnp.bfloat16)

    key_rows = turned(key_value[:, :HEAD_DIM])
    value_rows = (key_value[:, HEAD_DIM:] * factor).astype(jnp.bfloat16)
    bias = bias_ref[...]
    for head in range(queries.shape[1] // HEAD_DIM):
        columns = slice(head * HEAD_DIM, (head + 1) * HEAD_DIM)
        scores = lax.dot_general(
            turned(queries[:, columns]),
            key_rows,
            (((1,), (1,)), ((), ())),
            preferred_element_type=jnp.float32,
        )
        scores = scores * (1.0 / math.sqrt(HEAD_DIM)) + bias
        exp_scores = jnp.exp(scores - jnp.max(scores, axis=1, keepdims=True))
        weights = (exp_scores / jnp.sum(exp_scores, axis=1, keepdims=True)).astype(jnp.bfloat16)
        out_ref[:, columns] = jnp.dot(
            weights, value_rows, preferred_element_type=jnp.float32
        ).astype(jnp.bfloat16)


def output_kernel(layer, width, fill, starts_ref, a_ref, o_hbm, outs, out_bufs, o_buf, sem, out_sem):
    blocks = outs[-1].shape[1] // width
    per_part = blocks // (len(outs) - 1)

    def copy(block):
        start = pl.multiple_of(starts_ref[block // blocks] + block % blocks * width, width)
        return pltpu.make_async_copy(
            o_hbm.at[layer, :, pl.ds(start, width)], o_buf.at[block], sem.at[block]
        )

    for block in range(2 * blocks):
        copy(block).start()
    fill()
    leaving = []
    for block in range(2 * blocks):
        copy(block).wait()
        product = jnp.dot(a_ref[...], o_buf[block], preferred_element_type=jnp.float32)
        which, inner = (
            (block // per_part, block % per_part)
            if block < blocks
            else (len(outs) - 1, block - blocks)
        )
        columns = slice(inner * width, (inner + 1) * width)
        out_bufs[which][:, columns] = product.astype(out_bufs[which].dtype)
        leaving.append(
            pltpu.make_async_copy(
                out_bufs[which].at[:, columns], outs[which].at[:, columns], out_sem.at[block]
            )
        )
        leaving[-1].start()
    for copy_out in leaving:
        copy_out.wait()


def output_shapes(rows, count, parts):
    return [(rows, count // parts)] * parts + [(rows, count)]


def output_scratch(rows, depth, count, parts, width):
    return [pltpu.VMEM(shape, jnp.bfloat16) for shape in output_shapes(rows, count, parts)] + [
        pltpu.VMEM((2 * count // width, depth, width), jnp.bfloat16),
        pltpu.SemaphoreType.DMA((2 * count // width,)),
        pltpu.SemaphoreType.DMA((2 * count // width,)),
    ]


def output_product(attended, o_weight, layer, starts, count, parts, width=512):
    rows, depth = attended.shape
    n = parts + 1

    def kernel(starts_ref, a_hbm, o_hbm, *refs):
        outs, a_ref, a_sem = refs[:n], refs[n], refs[n + 1]
        ready = fetch([a_hbm], [a_ref], a_sem)
        output_kernel(
            layer,
            width,
            lambda: ready(0),
            starts_ref,
            a_ref,
            o_hbm,
            outs,
            refs[n + 2 : 2 * n + 2],
            *refs[2 * n + 2 :],
        )

    *sent, kept = call(
        kernel,
        [jax.ShapeDtypeStruct(s, jnp.bfloat16) for s in output_shapes(rows, count, parts)],
        4 * rows * depth * count,
        4 * depth * count,
        "output_product",
        vmem=36 * MIB,
        in_specs=[in_smem] + [in_hbm] * 2,
        out_specs=[in_hbm] * n,
        scratch_shapes=buffers_of([attended]) + output_scratch(rows, depth, count, parts, width),
    )(starts, attended, o_weight)
    return sent, kept


def attention_output(features, operands, o_weight, layer, starts, count, width=512):
    rows, depth = operands[0].shape
    n = len(operands)

    def kernel(starts_ref, *refs):
        inputs, o_hbm, out_hbm, outs = refs[:n], refs[n], refs[n + 1], refs[n + 2 : n + 4]
        buffers, in_sem = refs[n + 4 : 2 * n + 4], refs[2 * n + 4]
        out_ref, sem = refs[2 * n + 5 : 2 * n + 7]
        ready = fetch(inputs, buffers, in_sem)

        def attend():
            for i in range(n):
                ready(i)
            attend_kernel(features, n > 6, *buffers, out_ref)
            pltpu.make_async_copy(out_ref, out_hbm, sem.at[0]).start()

        output_kernel(
            layer,
            width,
            attend,
            starts_ref,
            out_ref,
            o_hbm,
            outs,
            refs[2 * n + 7 : 2 * n + 9],
            *refs[2 * n + 9 :],
        )
        pltpu.make_async_copy(out_ref, out_hbm, sem.at[0]).wait()

    attended = jax.ShapeDtypeStruct((rows, depth), jnp.bfloat16)
    attended, sent, kept = call(
        kernel,
        [attended] + [jax.ShapeDtypeStruct((rows, count), jnp.bfloat16)] * 2,
        8 * rows * rows * depth + 4 * rows * depth * count,
        4 * depth * count,
        "attention_output",
        vmem=36 * MIB,
        in_specs=[in_smem] + [in_hbm] * (n + 1),
        out_specs=[in_hbm] * 3,
        scratch_shapes=buffers_of(operands)
        + buffers_of([attended])
        + output_scratch(rows, depth, count, 1, width),
    )(starts, *operands, o_weight)
    return attended, [sent], kept


def add_kernel(n_parts, *refs):
    inputs, out_hbm, buffers = refs[: n_parts + 1], refs[n_parts + 1], refs[n_parts + 2 : -3]
    in_sem, out_ref, out_sem = refs[-3:]
    ready = fetch(inputs, buffers, in_sem)
    ready(n_parts)
    kept_ref = buffers[n_parts]
    leaving = []
    for i in range(n_parts):
        ready(i)
        width = buffers[i].shape[1]
        columns = slice(i * width, (i + 1) * width)
        total = kept_ref[:, columns].astype(jnp.float32) + buffers[i][...].astype(jnp.float32)
        out_ref[:, columns] = total.astype(out_ref.dtype)
        leaving.append(
            pltpu.make_async_copy(out_ref.at[:, columns], out_hbm.at[:, columns], out_sem.at[i])
        )
        leaving[-1].start()
    for copy_out in leaving:
        copy_out.wait()


def add_parts(kept, parts):
    n = len(parts)
    return call(
        lambda *refs: add_kernel(n, *refs),
        jax.ShapeDtypeStruct(kept.shape, kept.dtype),
        kept.size,
        6 * kept.size,
        "chip_sum",
        in_specs=[in_hbm] * (n + 1),
        out_specs=in_hbm,
        scratch_shapes=buffers_of(list(parts) + [kept])
        + [pltpu.VMEM(kept.shape, kept.dtype), pltpu.SemaphoreType.DMA((n,))],
    )(*parts, kept)


def combine_kernel(n_in, n_out, parts, *refs):
    inputs, outs = refs[:n_in], refs[n_in : n_in + n_out]
    in_bufs, out_bufs = refs[n_in + n_out : 2 * n_in + n_out], refs[2 * n_in + n_out : -2]
    in_sem, out_sem = refs[-2:]
    width = outs[0].shape[1] // parts
    columns = [slice(part * width, (part + 1) * width) for part in range(parts)]
    coming = [
        [
            pltpu.make_async_copy(
                inputs[i].at[:, columns[part]], in_bufs[i].at[:, columns[part]], in_sem.at[i, part]
            )
            for i in range(n_in)
        ]
        for part in range(parts)
    ]
    for copies in coming:
        for copy in copies:
            copy.start()
    leaving = []
    for part in range(parts):
        for copy in coming[part]:
            copy.wait()
        values = [buf[:, columns[part]].astype(jnp.float32) for buf in in_bufs]
        total = values[-1]
        for value in values[-2::-1]:
            total = value + total
        for i in range(n_out):
            out_bufs[i][:, columns[part]] = total.astype(out_bufs[i].dtype)
            leaving.append(
                pltpu.make_async_copy(
                    out_bufs[i].at[:, columns[part]], outs[i].at[:, columns[part]], out_sem.at[i, part]
                )
            )
            leaving[-1].start()
    for copy in leaving:
        copy.wait()


def combine(inputs, dtypes, parts=4):
    shape = inputs[0].shape
    return call(
        lambda *refs: combine_kernel(len(inputs), len(dtypes), parts, *refs),
        [jax.ShapeDtypeStruct(shape, dtype) for dtype in dtypes],
        inputs[0].size * len(inputs),
        sum(array.nbytes for array in inputs) + 4 * inputs[0].size,
        "combine",
        in_specs=[in_hbm] * len(inputs),
        out_specs=[in_hbm] * len(dtypes),
        scratch_shapes=[pltpu.VMEM(shape, array.dtype) for array in inputs]
        + [pltpu.VMEM(shape, dtype) for dtype in dtypes]
        + [
            pltpu.SemaphoreType.DMA((len(inputs), parts)),
            pltpu.SemaphoreType.DMA((len(dtypes), parts)),
        ],
    )(*inputs)


def rope_tables(positions):
    half_depth = HEAD_DIM // 2
    inv_freq = rope_base ** (-2.0 * jnp.arange(half_depth, dtype=jnp.float32) / HEAD_DIM)
    angles = positions[:, None] * inv_freq[None, :]
    cosine, sine = jnp.cos(angles), jnp.sin(angles)
    return jnp.concatenate([cosine, cosine], axis=1), jnp.concatenate([-sine, sine], axis=1)


def normalize(rows):
    center = rows - jnp.mean(rows, axis=1, keepdims=True)
    factor = lax.rsqrt(jnp.mean(center * center, axis=1, keepdims=True) + ln_eps)
    return center * factor, factor


def norm_kernel(count_ref, affine_ref, patch_hbm, out_ref, patch_ref, sem):
    owners, padded, in_share = out_ref.shape
    slots = patch_ref.shape[0]
    vit = affine_ref.shape[1]
    counts = jnp.full((padded - slots, vit), count_ref[0].astype(jnp.float32))
    fetch([patch_hbm], [patch_ref], sem)(0)
    for group in range(patch_ref.shape[1] // vit):
        rows = patch_ref[:, group * vit : (group + 1) * vit].astype(jnp.float32)
        scaled = normalize(rows)[0] * affine_ref[0:1, :] + affine_ref[1:2, :]
        scaled = jnp.concatenate([scaled, counts], axis=0).astype(out_ref.dtype)
        for i in range(vit // in_share):
            out_ref[group * (vit // in_share) + i] = scaled[:, i * in_share : (i + 1) * in_share]


def norm_back_kernel(patch_ref, grads_ref, affine_ref, out_ref):
    _, _, in_share = grads_ref.shape
    slots = patch_ref.shape[0]
    vit = affine_ref.shape[1]
    per_group = vit // in_share
    for group in range(patch_ref.shape[1] // vit):
        rows = patch_ref[:, group * vit : (group + 1) * vit].astype(jnp.float32)
        unit, factor = normalize(rows)
        grads = jnp.concatenate(
            [grads_ref[group * per_group + i].astype(jnp.float32) for i in range(per_group)], axis=1
        )[:slots]
        grads = grads * affine_ref[0:1, :]
        along = jnp.mean(grads * unit, axis=1, keepdims=True)
        out_ref[:, group * vit : (group + 1) * vit] = factor * (
            grads - jnp.mean(grads, axis=1, keepdims=True) - unit * along
        )


def split_kernel(core_ref, rows_ref, out_ref):
    owners, part_rows, width = out_ref.shape
    slots = rows_ref.shape[0]
    first = core_ref[0] == 0
    for owner in range(owners):
        rows = rows_ref[:, owner * width : (owner + 1) * width].astype(jnp.float32)
        rest = jnp.zeros((2 * part_rows - slots, width), jnp.float32)
        rows = jnp.concatenate([rows, rest], axis=0)
        rows = jnp.where(first, rows[:part_rows], rows[part_rows:])
        out_ref[owner] = rows.astype(out_ref.dtype)


def pack_kernel(slots, rows_ref, weight_ref, out_ref, pack_ref):
    owners, padded, _ = rows_ref.shape
    packed_rows = out_ref.shape[0]
    row = lax.broadcasted_iota(jnp.int32, (packed_rows, padded), 0).astype(jnp.float32)
    slot = lax.broadcasted_iota(jnp.int32, (packed_rows, padded), 1).astype(jnp.float32)
    offset = jnp.zeros((1, 1), jnp.float32)
    packed = jnp.zeros((packed_rows, rows_ref.shape[2]), jnp.float32)
    for owner in range(owners):
        rows = rows_ref[owner]
        count = rows.astype(jnp.float32)[slots : slots + 1, 0:1]
        chosen = jnp.where((row == offset + slot) & (slot < count), 1.0, 0.0).astype(jnp.bfloat16)
        pack_ref[owner] = chosen
        packed = packed + jnp.dot(chosen, rows, preferred_element_type=jnp.float32)
        offset = offset + count
    out_ref[...] = jnp.dot(
        packed.astype(jnp.bfloat16), weight_ref[...], preferred_element_type=jnp.float32
    ).astype(out_ref.dtype)


def pack_grads_kernel(core_ref, mine_ref, other_ref, pack_ref, weight_ref, out_ref):
    packed = jnp.zeros((out_ref.shape[0], mine_ref.shape[2]), jnp.float32)
    first = core_ref[0] == 0
    padded = pack_ref.shape[2]
    for owner in range(mine_ref.shape[0]):
        mine = mine_ref[owner].astype(jnp.float32)
        other = other_ref[owner].astype(jnp.float32)
        rows = jnp.concatenate(
            [jnp.where(first, mine, other), jnp.where(first, other, mine)], axis=0
        )
        packed = packed + jnp.dot(
            pack_ref[owner],
            rows[:padded].astype(jnp.bfloat16),
            preferred_element_type=jnp.float32,
        )
    out_ref[...] = lax.dot_general(
        packed.astype(jnp.bfloat16),
        weight_ref[...],
        (((1,), (1,)), ((), ())),
        preferred_element_type=jnp.float32,
    ).astype(out_ref.dtype)


def halves_kernel(core_ref, rows_ref, weight_ref, kept_ref, sent_ref):
    product = jnp.dot(rows_ref[...], weight_ref[...], preferred_element_type=jnp.float32)
    half = kept_ref.shape[1]
    first = core_ref[0] == 0
    kept_ref[...] = jnp.where(first, product[:, :half], product[:, half:])
    sent_ref[...] = jnp.where(first, product[:, half:], product[:, :half]).astype(sent_ref.dtype)


def unpack_kernel(first_ref, second_ref, pack_ref, out_ref):
    total = first_ref[...].astype(jnp.float32) + second_ref[...].astype(jnp.float32)
    total = total.astype(jnp.bfloat16)
    for owner in range(pack_ref.shape[0]):
        out_ref[owner] = lax.dot_general(
            pack_ref[owner], total, (((0,), (0,)), ((), ())), preferred_element_type=jnp.float32
        ).astype(out_ref.dtype)


def assemble_kernel(core_ref, shift_ref, mine_hbm, other_hbm, out_ref, mine_ref, other_ref, sem):
    owners, _, half = mine_ref.shape
    first = core_ref[0] == 0
    ready = fetch([mine_hbm, other_hbm], [mine_ref, other_ref], sem)
    ready(0)
    ready(1)
    for owner in range(owners):
        mine = mine_ref[owner].astype(jnp.float32)
        other = other_ref[owner].astype(jnp.float32)
        for i in range(2):
            columns = slice((2 * owner + i) * half, (2 * owner + i + 1) * half)
            part = jnp.where(first, mine, other) if i == 0 else jnp.where(first, other, mine)
            out_ref[:, columns] = (part + shift_ref[:, columns]).astype(out_ref.dtype)


def exchange(values):
    return lax.all_to_all(values, "dp", split_axis=0, concat_axis=0, tiled=True)


def four_chip_local(
    patches,
    ln_gain,
    ln_shift,
    w_in,
    b_in,
    w_out,
    b_out,
    place,
    image_counts,
    text_rows,
    segments,
    norm_gain,
    q_weight,
    kv_weight,
    o_weight,
    grad_rows,
):
    bf16, f32 = jnp.bfloat16, jnp.float32
    shape_of = jax.ShapeDtypeStruct
    me = lax.axis_index("sec")
    core, chip = me & 1, me >> 1
    core_word = core.reshape(1).astype(jnp.int32)
    owners = lax.axis_size("dp")
    slots = patches.shape[0]
    padded = slots + 16 - slots % 16
    tokens, share = text_rows.shape
    features = share * 4
    layers = q_weight.shape[0]
    in_share, hidden_share = w_in.shape
    out_share = w_out.shape[1]
    packed_rows = owners * (tokens // 16)
    chunk = packed_rows // owners
    affine = jnp.stack([ln_gain, ln_shift]).astype(f32)

    normed = call(
        norm_kernel,
        shape_of((owners, padded, in_share), bf16),
        slots * owners * in_share * 10,
        slots * owners * in_share * 4,
        "normed_patches",
        in_specs=[in_smem] + in_vmem(1) + [in_hbm],
        scratch_shapes=buffers_of([patches]),
    )(image_counts, affine, patches)
    received = exchange(normed)

    text_rows = after(text_rows, normed)
    far = swap(text_rows, "sec", ACROSS)
    gathered_text = [text_rows, swap(text_rows, "sec", CORE)]
    gains = norm_gain.astype(f32)
    starts = jnp.stack([(me ^ r) * share for r in range(4)]).astype(jnp.int32)
    projected = project(gathered_text, starts[:2], gains, q_weight, kv_weight, 0, None)
    received, projected = lax.optimization_barrier((received, projected))
    far = after(far, received)
    gathered_text += [far, swap(far, "sec", CORE)]
    pre_part, pack = call(
        lambda *refs: pack_kernel(slots, *refs),
        [shape_of((packed_rows, hidden_share), bf16), shape_of((owners, packed_rows, padded), bf16)],
        2 * packed_rows * in_share * hidden_share,
        2 * in_share * hidden_share,
        "pre_act",
    )(received, w_in)
    pre_parts = exchange(pre_part.reshape(owners, chunk, hidden_share))

    shift = after(b_out, received).reshape(1, share)
    shift_far = swap(shift, "sec", ACROSS)
    shifts = [shift, swap(shift, "sec", CORE), shift_far, swap(shift_far, "sec", CORE)]
    shifts = jnp.take(jnp.concatenate(shifts, axis=0), jnp.arange(4, dtype=jnp.int32) ^ me, axis=0)
    shifts = shifts.astype(f32).reshape(1, -1)
    allowed, positions = doc_mask(segments[0])
    bias = jnp.where(allowed, 0.0, -1e30).astype(f32)
    cosine, sine = rope_tables(positions)
    projected = project(gathered_text[2:], starts[2:], gains, q_weight, kv_weight, 0, projected)
    pre_act = jnp.sum(pre_parts.astype(f32), axis=0) + b_in.astype(f32)
    hidden_units = gelu_exact(pre_act).astype(bf16)
    hidden_all = exchange(jnp.broadcast_to(hidden_units[None], (owners, chunk, hidden_share)))
    slot_index = jnp.arange(padded, dtype=jnp.int32)
    token_index = jnp.arange(tokens, dtype=jnp.int32)
    places = jnp.pad(place, (0, padded - slots))
    select = (places[None, :] == token_index[:, None]) & (slot_index < image_counts[0])[None, :]
    is_image = jnp.any(select, axis=1)

    hidden_all, projected, cosine, sine, bias, shifts = lax.optimization_barrier(
        (hidden_all, projected, cosine, sine, bias, shifts)
    )
    kept, sent = call(
        halves_kernel,
        [
            shape_of((packed_rows, out_share // 2), f32),
            shape_of((packed_rows, out_share // 2), bf16),
        ],
        2 * packed_rows * out_share * hidden_share,
        2 * out_share * hidden_share,
        "merged",
        in_specs=[in_smem] + in_vmem(2),
    )(core_word, hidden_all.reshape(packed_rows, hidden_share), w_out)
    chip_sum = (kept + swap(sent, "sec", CORE).astype(f32)).astype(bf16)

    def unpack(first, second):
        width = first.shape[1]
        return exchange(
            call(
                unpack_kernel,
                shape_of((owners, padded, width), bf16),
                2 * packed_rows * owners * padded * width,
                2 * owners * padded * width,
                "unpack",
            )(first, second, pack)
        )

    merged_half = unpack(chip_sum, swap(chip_sum, "sec", ACROSS))
    image_rows = call(
        assemble_kernel,
        shape_of((padded, features), bf16),
        padded * features,
        padded * features * 4,
        "image_rows",
        in_specs=[in_smem] + in_vmem(1) + [in_hbm] * 2,
        scratch_shapes=buffers_of([merged_half] * 2),
    )(core_word, shifts, merged_half, swap(merged_half, "sec", CORE))

    def column(chip_index, core_bit):
        return (2 * chip_index + core_bit) * share

    images = project(
        [image_rows], jnp.zeros((1,), jnp.int32), gains, q_weight, kv_weight, 0, None
    )

    def start_rows(r):
        image_part = lax.dynamic_slice_in_dim(image_rows, column(chip ^ r, core), share, 1)
        picked = jnp.dot(select.astype(bf16), image_part, preferred_element_type=f32)
        return jnp.where(is_image[:, None], picked.astype(bf16), gathered_text[2 * r])

    def columns_of(r):
        return jnp.stack([column(chip ^ r, core ^ 1), column(chip ^ r, core)]).astype(
            jnp.int32
        )

    def shared(sent):
        return [swap(part, "sec", CORE) for part in sent]

    grad_rows = after(grad_rows, merged_half)
    grad_parts = call(
        split_kernel,
        shape_of((owners, (padded + 16) // 32 * 16, out_share), bf16),
        slots * owners * out_share,
        slots * owners * out_share * 4,
        "split_grads",
        in_specs=[in_smem] + in_vmem(1),
    )(core_word, grad_rows)
    grads_there = exchange(grad_parts)

    def grads_first():
        grad_part = call(
            pack_grads_kernel,
            shape_of((packed_rows, hidden_share), bf16),
            2 * packed_rows * out_share * hidden_share,
            2 * out_share * hidden_share,
            "hidden_grads",
            in_specs=[in_smem] + in_vmem(4),
        )(core_word, grads_there, swap(grads_there, "sec", CORE), pack, w_out)
        return grad_part.reshape(owners, chunk, hidden_share)

    def grads_second(parts):
        hidden_grads = jnp.sum(parts.astype(f32), axis=0)
        _, pull_gelu = jax.vjp(gelu_exact, pre_act)
        pre_grads = pull_gelu(hidden_grads)[0].astype(bf16)
        return jnp.broadcast_to(pre_grads[None], (owners, chunk, hidden_share))

    def grads_third(pre_grads):
        back = lax.dot_general(
            pre_grads.reshape(packed_rows, hidden_share),
            w_in,
            (((1,), (1,)), ((), ())),
            preferred_element_type=f32,
        )
        return (back + swap(back, "sec", CORE)).astype(bf16)

    operands = list(projected) + [cosine, sine, bias] + list(images) + [select.astype(f32)]

    def partly(old, rows, r, layer):
        here = jnp.stack([column(chip ^ r, core), column(chip ^ r, core ^ 1)])
        return project(
            [rows, swap(rows, "sec", CORE)],
            here.astype(jnp.int32),
            gains,
            q_weight,
            kv_weight,
            layer,
            old,
        )

    grads, held = None, None
    for layer in range(1, layers):
        attended, sent, kept = attention_output(
            features, operands, o_weight, layer - 1, columns_of(1), share
        )
        other_sum = add_parts(kept, shared(sent))
        attended = after(attended, other_sum)
        came_here = swap(other_sum, "sec", ACROSS)
        sent, kept = output_product(attended, o_weight, layer - 1, columns_of(0), share, 4)
        own_sum = add_parts(kept, shared(sent))
        if held is None:
            held = [start_rows(0), start_rows(1)]
        if grads is None:
            grads_there = after(grads_there, own_sum)
            grads = grads_first()
            came_here = after(came_here, grads)
            grads = exchange(grads_second(exchange(grads)))
        came_here = after(came_here, own_sum)
        came_there = swap(own_sum, "sec", ACROSS)
        now = held[0].astype(f32) + (own_sum.astype(f32) + came_here.astype(f32))
        rounded = now.astype(bf16)
        projected = partly(None, rounded, 0, layer)
        if layer == 1:
            grads = grads_third(grads)
        came_there = after(came_there, (projected, held[1]))
        (there,) = combine([held[1], other_sum, came_there], [bf16])
        projected = partly(projected, there, 1, layer)
        held = [now, there]
        operands = list(projected) + [cosine, sine, bias]

    if layers == 1:
        held = [start_rows(0)]
        grads = grads_third(exchange(grads_second(exchange(grads_first()))))
    back = grads
    back_far = swap(back, "sec", ACROSS)
    operands = after(operands, back_far)

    last = layers - 1
    attended, sent, kept = attention_output(
        features, operands, o_weight, last, columns_of(1), share
    )
    other_sum = add_parts(kept, shared(sent))
    attended = after(attended, other_sum)
    back_far = after(back_far, other_sum)
    came = swap(other_sum, "sec", ACROSS)
    normed_grads = unpack(back, back_far)
    sent, kept = output_product(attended, o_weight, last, columns_of(0), share, 4)
    own_sum = add_parts(kept, shared(sent))
    patch_grads = call(
        norm_back_kernel,
        shape_of(patches.shape, f32),
        slots * owners * in_share * 10,
        slots * owners * in_share * 8,
        "patch_grads",
    )(patches, normed_grads, affine)
    came, own_sum, patch_grads = lax.optimization_barrier((came, own_sum, patch_grads))
    return combine([held[0], own_sum, came], [f32])[0], patch_grads


def local(
    patches,
    ln_gain,
    ln_shift,
    w_in,
    b_in,
    w_out,
    b_out,
    place,
    image_counts,
    text_rows,
    segments,
    norm_gain,
    q_weight,
    kv_weight,
    o_weight,
    grad_rows,
):
    slot_count = patches.shape[0]
    tokens, share = text_rows.shape
    slot_index = jnp.arange(slot_count, dtype=jnp.int32)
    live_slot = slot_index < image_counts[0]
    merged, patch_grads = merger_rows(
        patches,
        ln_gain,
        ln_shift,
        w_in,
        b_in,
        w_out,
        live_slot,
        image_counts[0],
        grad_rows,
        lax.axis_size("dp") * (tokens // 16),
    )
    merged_local = lax.dynamic_slice_in_dim(
        merged, lax.axis_index(("sec", "mp")) * share, share, 1
    ).astype(jnp.float32)
    merged_local = (merged_local + b_out.astype(jnp.float32)).astype(jnp.bfloat16)
    token_index = jnp.arange(tokens, dtype=jnp.int32)
    select = (place[:, None] == token_index[None, :]) & live_slot[:, None]
    is_image = jnp.any(select, axis=0)
    picked = lax.dot_general(
        select.astype(jnp.bfloat16),
        merged_local,
        (((0,), (0,)), ((), ())),
        preferred_element_type=jnp.float32,
    )
    start_rows = jnp.where(is_image[:, None], picked, text_rows.astype(jnp.float32)).astype(
        jnp.bfloat16
    )
    allowed, positions = doc_mask(segments[0])
    layer_count = q_weight.shape[0]
    current = start_rows.astype(jnp.float32)
    for layer_index in range(layer_count):
        current = section_features(
            current,
            norm_gain[layer_index],
            allowed,
            positions,
            q_weight[layer_index],
            kv_weight[layer_index],
            o_weight[layer_index],
        )
    return (current, patch_grads)


def solution(mesh):
    in_specs = (
        P("dp", None),
        P(),
        P(),
        P("dp", ("sec", "mp")),
        P(("sec", "mp")),
        P(("sec", "mp"), "dp"),
        P(("sec", "mp")),
        P("dp"),
        P("dp"),
        P("dp", ("sec", "mp")),
        P("dp", None),
        P(),
        P(None, None, ("sec", "mp")),
        P(None, None, ("sec", "mp"), None),
        P(None, ("sec", "mp"), None),
        P("dp", None),
    )
    out_specs = (P("dp", ("sec", "mp")), P("dp", None))
    step = four_chip_local if mesh.shape["sec"] == 4 and mesh.shape["mp"] == 1 else local
    return jax.shard_map(step, mesh=mesh, in_specs=in_specs, out_specs=out_specs, check_vma=False)
```

```python
import math

import jax
import jax.numpy as jnp
from jax import lax
from jax.experimental import pallas as pl
from jax.experimental.pallas import tpu as pltpu
from jax.sharding import PartitionSpec as P

D = 8192
HEAD_DIM = 128


ln_eps = 1e-06
rms_eps = 1e-06
rope_base = 1000000.0


def group_norm(patch_rows, ln_gain, ln_shift):
    row_count = patch_rows.shape[0]
    grouped = patch_rows.astype(jnp.float32).reshape(row_count, -1, ln_gain.shape[0])
    center = grouped - jnp.mean(grouped, axis=-1, keepdims=True)
    spread = jnp.mean(center * center, axis=-1, keepdims=True)
    scaled = center * lax.rsqrt(spread + ln_eps) * ln_gain.astype(jnp.float32) + ln_shift.astype(
        jnp.float32
    )
    return scaled.reshape(row_count, -1)


def gelu_exact(values):
    return jax.nn.gelu(values, approximate=False)


def rotate(values, positions):
    head_depth = values.shape[-1]
    half_depth = head_depth // 2
    inv_freq = rope_base ** (-2.0 * jnp.arange(half_depth, dtype=jnp.float32) / head_depth)
    angles = positions[:, None] * inv_freq[None, :]
    cosine = jnp.cos(angles)[:, None, :]
    sine_part = jnp.sin(angles)[:, None, :]
    first_half = values[..., :half_depth]
    second = values[..., half_depth:]
    return jnp.concatenate(
        [first_half * cosine - second * sine_part, second * cosine + first_half * sine_part],
        axis=-1,
    )


def doc_mask(segment_ids):
    token_index = jnp.arange(segment_ids.shape[0], dtype=jnp.int32)
    same_doc = segment_ids[:, None] == segment_ids[None, :]
    allowed = same_doc & (token_index[None, :] <= token_index[:, None])
    positions = jnp.sum(allowed.astype(jnp.int32), axis=1) - 1
    return (allowed, positions.astype(jnp.float32))


def attend(normed, allowed, positions, q_local, kv_local):
    token_count = normed.shape[0]
    queries = jnp.dot(normed, q_local, preferred_element_type=jnp.float32).reshape(
        token_count, -1, HEAD_DIM
    )
    key_value = jnp.einsum("td,kcd->tkc", normed, kv_local, preferred_element_type=jnp.float32)
    key_value = lax.all_gather(key_value, "mp", axis=2, tiled=True)
    key_rows = rotate(key_value[:, 0:1, :], positions)[:, 0, :].astype(jnp.bfloat16)
    value_rows = key_value[:, 1, :].astype(jnp.bfloat16)
    queries = rotate(queries, positions).astype(jnp.bfloat16)
    scores = jnp.einsum("thd,sd->hts", queries, key_rows, preferred_element_type=jnp.float32) * (
        1.0 / math.sqrt(HEAD_DIM)
    )
    scores = jnp.where(allowed[None], scores, -jnp.inf)
    row_max = jnp.max(scores, axis=-1, keepdims=True)
    exp_scores = jnp.exp(scores - row_max)
    attn_weights = (exp_scores / jnp.sum(exp_scores, axis=-1, keepdims=True)).astype(jnp.bfloat16)
    attended = jnp.einsum(
        "hts,sd->thd", attn_weights, value_rows, preferred_element_type=jnp.float32
    )
    return attended.astype(jnp.bfloat16).reshape(token_count, -1)


def gather_features(rows_local):
    return lax.all_gather(rows_local, ("sec", "mp"), axis=1, tiled=True)


def section_features(rows_local, gain_row, allowed, positions, q_local, kv_local, o_local):
    share = rows_local.shape[1]
    square_sums = lax.psum(jnp.sum(rows_local * rows_local, axis=1), ("sec", "mp"))
    factor = lax.rsqrt(square_sums / D + rms_eps)
    gain_local = lax.dynamic_slice_in_dim(
        gain_row, lax.axis_index(("sec", "mp")) * share, share, 0
    ).astype(jnp.float32)
    normed_local = (rows_local * factor[:, None] * gain_local[None, :]).astype(jnp.bfloat16)
    normed = gather_features(normed_local)
    attended = attend(normed, allowed, positions, q_local, kv_local)
    summed = lax.psum_scatter(
        lax.dot_general(
            o_local, attended, (((0,), (1,)), ((), ())), preferred_element_type=jnp.float32
        ),
        ("sec", "mp"),
        scatter_dimension=0,
        tiled=True,
    )
    return rows_local + summed.T


def swap(values, axis, mask):
    size = lax.axis_size(axis)
    return lax.ppermute(values, axis, [(i, i ^ mask) for i in range(size)])


def spread_rows(values, parts):
    return lax.all_to_all(values, "dp", split_axis=0, concat_axis=0, tiled=True).reshape(
        (parts, -1) + values.shape[1:]
    )


def merger_rows(patches, ln_gain, ln_shift, w_in, b_in, w_out, live_slot, count, grad_rows, packed_rows):
    owners = lax.axis_size("dp")
    group = lax.axis_size(("sec", "mp"))
    slots = patches.shape[0]
    in_share, hidden_share = w_in.shape
    out_share = w_out.shape[1]
    share = in_share + out_share

    normed = group_norm(patches, ln_gain, ln_shift).astype(jnp.bfloat16)
    slot_grads = jnp.where(live_slot[:, None], grad_rows, jnp.zeros_like(grad_rows))
    rows = jnp.concatenate(
        [normed.reshape(slots, owners, in_share), slot_grads.reshape(slots, owners, out_share)],
        axis=2,
    ).transpose(1, 0, 2)
    count_rows = jnp.broadcast_to(count.astype(jnp.bfloat16), (owners, 8, share))
    received = lax.all_to_all(
        jnp.concatenate([rows, count_rows], axis=1), "dp", split_axis=0, concat_axis=0, tiled=True
    )
    counts = received[:, slots, 0].astype(jnp.int32)
    owner_index = jnp.arange(owners, dtype=jnp.int32)
    offsets = jnp.sum(jnp.where(owner_index[None, :] < owner_index[:, None], counts[None, :], 0), axis=1)
    slot_index = jnp.arange(slots, dtype=jnp.int32)
    target = jnp.where(
        slot_index[None, :] < counts[:, None], offsets[:, None] + slot_index[None, :], -1
    ).reshape(-1)
    pack = (jnp.arange(packed_rows, dtype=jnp.int32)[:, None] == target[None, :]).astype(jnp.bfloat16)
    packed = jnp.dot(
        pack, received[:, :slots].reshape(owners * slots, share), preferred_element_type=jnp.float32
    ).astype(jnp.bfloat16)

    pre_part = jnp.dot(packed[:, :in_share], w_in, preferred_element_type=jnp.float32)
    grad_part = lax.dot_general(
        packed[:, in_share:], w_out, (((1,), (1,)), ((), ())), preferred_element_type=jnp.float32
    )
    parts = jnp.concatenate([pre_part, grad_part], axis=1).astype(jnp.bfloat16)
    chunk = packed_rows // owners
    parts = lax.all_to_all(
        parts.reshape(owners, chunk, 2 * hidden_share), "dp", split_axis=0, concat_axis=0, tiled=True
    )
    sums = jnp.sum(parts.astype(jnp.float32), axis=0)
    pre_act = sums[:, :hidden_share] + b_in.astype(jnp.float32)
    hidden_units, pull_gelu = jax.vjp(gelu_exact, pre_act)
    pre_grads = pull_gelu(sums[:, hidden_share:])[0]
    both = jnp.concatenate([hidden_units, pre_grads], axis=1).astype(jnp.bfloat16)
    both = lax.all_to_all(
        jnp.broadcast_to(both[None], (owners, chunk, 2 * hidden_share)),
        "dp",
        split_axis=0,
        concat_axis=0,
        tiled=True,
    ).reshape(packed_rows, 2 * hidden_share)
    merged_part = jnp.dot(both[:, :hidden_share], w_out, preferred_element_type=jnp.float32)
    back_part = lax.dot_general(
        both[:, hidden_share:], w_in, (((1,), (1,)), ((), ())), preferred_element_type=jnp.float32
    )
    tail = jnp.concatenate(
        [
            merged_part.astype(jnp.bfloat16).reshape(packed_rows, group, out_share // group),
            back_part.astype(jnp.bfloat16).reshape(packed_rows, group, in_share // group),
        ],
        axis=2,
    ).reshape(packed_rows, group * (share // group))
    tail = lax.dot_general(
        pack, tail, (((0,), (0,)), ((), ())), preferred_element_type=jnp.float32
    ).astype(jnp.bfloat16)
    tail = tail.reshape(owners * slots, group, share // group).transpose(1, 0, 2)
    me = lax.axis_index(("sec", "mp"))
    parts_now = tail.astype(jnp.float32)
    index = jnp.arange(group, dtype=jnp.int32) ^ me
    parts_now = jnp.take(parts_now, index, axis=0)
    mask = 1
    while mask < group:
        pairs = parts_now.reshape(-1, 2, owners * slots, share // group)
        received = swap(pairs[:, 1].astype(jnp.bfloat16), ("sec", "mp"), mask)
        parts_now = pairs[:, 0] + received.astype(jnp.float32)
        mask *= 2
    mine = parts_now.reshape(owners, slots, share // group).astype(jnp.bfloat16)
    mine = lax.all_to_all(mine, "dp", split_axis=0, concat_axis=0, tiled=True)
    gathered = mine[None]
    mask = group // 2
    while mask >= 1:
        gathered = jnp.concatenate([gathered, swap(gathered, ("sec", "mp"), mask)], axis=0)
        mask //= 2
    order = [0]
    mask = group // 2
    while mask >= 1:
        order = order + [i ^ mask for i in order]
        mask //= 2
    place_of = [0] * group
    for where_now, relative in enumerate(order):
        place_of[relative] = where_now
    gathered = jnp.take(gathered, jnp.asarray(place_of, jnp.int32)[index], axis=0)
    gathered = gathered.transpose(2, 1, 0, 3)
    merged = gathered[..., : out_share // group].reshape(slots, owners * out_share)
    normed_grads = gathered[..., out_share // group :].reshape(slots, owners * in_share)
    _, pull_norm = jax.vjp(
        lambda values: group_norm(values, ln_gain, ln_shift), patches.astype(jnp.float32)
    )
    return merged, pull_norm(normed_grads.astype(jnp.float32))[0]


MIB = 1024 * 1024
WEIGHT = 64
CORE, ACROSS = 1, 2


def call(kernel, out_shape, flops, n_bytes, name, vmem=16 * MIB, **more):
    return pl.pallas_call(
        kernel,
        out_shape=out_shape,
        cost_estimate=pl.CostEstimate(
            flops=int(flops) // WEIGHT, bytes_accessed=int(n_bytes) // WEIGHT, transcendentals=0
        ),
        compiler_params=pltpu.CompilerParams(vmem_limit_bytes=vmem),
        name=name,
        **more,
    )


def in_vmem(count):
    return [pl.BlockSpec(memory_space=pltpu.VMEM)] * count


in_smem = pl.BlockSpec(memory_space=pltpu.SMEM)
in_hbm = pl.BlockSpec(memory_space=pltpu.HBM)


def after(values, others):
    return lax.optimization_barrier((values, others))[0]


def fetch(refs, buffers, sem):
    copies = [
        pltpu.make_async_copy(ref, buffer, sem.at[i])
        for i, (ref, buffer) in enumerate(zip(refs, buffers))
    ]
    for copy in copies:
        copy.start()
    return lambda i: copies[i].wait()


def buffers_of(arrays):
    return [pltpu.VMEM(array.shape, array.dtype) for array in arrays] + [
        pltpu.SemaphoreType.DMA((len(arrays),))
    ]


def project_kernel(layer, width, n_parts, fresh, starts_ref, gain_ref, q_hbm, kv_hbm, *refs):
    n_in = n_parts + (0 if fresh else 3)
    inputs, outs, buffers = refs[:n_in], refs[n_in : n_in + 3], refs[n_in + 3 :]
    x_refs, x_sem, q_buf, kv_buf, q_sem, kv_sem = buffers[:n_parts], *buffers[n_parts:]
    out_q, out_kv, out_sq = outs
    per_part = x_refs[0].shape[1] // width
    lanes = out_sq.shape[1]

    def place_of(block):
        part, inner = block // per_part, block % per_part
        return pl.multiple_of(starts_ref[part] + inner * width, width)

    def copies(block):
        rows = pl.ds(place_of(block), width)
        return (
            pltpu.make_async_copy(q_hbm.at[layer, rows, :], q_buf.at[block], q_sem.at[block]),
            pltpu.make_async_copy(kv_hbm.at[layer, :, :, rows], kv_buf.at[block], kv_sem.at[block]),
        )

    n_blocks = n_parts * per_part
    ready = fetch(inputs, list(x_refs) + ([] if fresh else list(outs)), x_sem)
    for block in range(n_blocks):
        for copy in copies(block):
            copy.start()
    if fresh:
        out_q[...] = jnp.zeros_like(out_q)
        out_kv[...] = jnp.zeros_like(out_kv)
        out_sq[...] = jnp.zeros_like(out_sq)
    else:
        for i in range(n_parts, n_in):
            ready(i)
    for block in range(n_blocks):
        inner = block % per_part
        if inner == 0:
            ready(block // per_part)
        rows = x_refs[block // per_part][:, inner * width : (inner + 1) * width].astype(jnp.float32)
        squares = rows * rows
        total = squares[:, :lanes]
        for i in range(1, width // lanes):
            total = total + squares[:, i * lanes : (i + 1) * lanes]
        out_sq[...] += total
        gain = gain_ref[layer : layer + 1, pl.ds(place_of(block), width)]
        normed = (rows * gain).astype(jnp.bfloat16)
        for copy in copies(block):
            copy.wait()
        out_q[...] += jnp.dot(normed, q_buf[block], preferred_element_type=jnp.float32)
        for i in range(2):
            out_kv[:, i * HEAD_DIM : (i + 1) * HEAD_DIM] += lax.dot_general(
                normed, kv_buf[block, i], (((1,), (1,)), ((), ())), preferred_element_type=jnp.float32
            )


def project(parts, starts, gains, q_weight, kv_weight, layer, old, width=512):
    rows, part_width = parts[0].shape
    n_parts = len(parts)
    n_blocks = n_parts * part_width // width
    columns = q_weight.shape[2]
    shapes = [(rows, columns), (rows, 2 * HEAD_DIM), (rows, HEAD_DIM)]
    old = [] if old is None else list(old)
    features = n_parts * part_width
    return call(
        lambda *refs: project_kernel(layer, width, n_parts, not old, *refs),
        [jax.ShapeDtypeStruct(shape, jnp.float32) for shape in shapes],
        2 * rows * features * (columns + 2 * HEAD_DIM),
        features * (columns + 2 * HEAD_DIM) * 2 + rows * features * 2,
        "project",
        vmem=48 * MIB,
        in_specs=[in_smem] + in_vmem(1) + [in_hbm] * (2 + n_parts + len(old)),
        out_specs=in_vmem(3),
        scratch_shapes=[pltpu.VMEM(part.shape, part.dtype) for part in parts]
        + [
            pltpu.SemaphoreType.DMA((n_parts + len(old),)),
            pltpu.VMEM((n_blocks, width, columns), jnp.bfloat16),
            pltpu.VMEM((n_blocks, 2, HEAD_DIM, width), jnp.bfloat16),
            pltpu.SemaphoreType.DMA((n_blocks,)),
            pltpu.SemaphoreType.DMA((n_blocks,)),
        ],
    )(starts, gains, q_weight, kv_weight, *parts, *old)


def attend_kernel(features, with_images, *refs):
    q_ref, kv_ref, sq_ref, cos_ref, sin_ref, bias_ref = refs[:6]
    out_ref = refs[-1]
    queries, key_value, squares = q_ref[...], kv_ref[...], sq_ref[...]
    if with_images:
        image_q, image_kv, image_sq, select_ref = refs[6:10]
        select = select_ref[...]
        is_image = jnp.sum(select, axis=1, keepdims=True) > 0.0

        def put(image_ref, values):
            picked = jnp.dot(
                select,
                image_ref[...],
                preferred_element_type=jnp.float32,
                precision=lax.Precision.HIGHEST,
            )
            return jnp.where(is_image, picked, values)

        queries, key_value, squares = (
            put(image_q, queries),
            put(image_kv, key_value),
            put(image_sq, squares),
        )
    factor = lax.rsqrt(jnp.sum(squares, axis=1, keepdims=True) / features + rms_eps)
    cosine, sine = cos_ref[...] * factor, sin_ref[...] * factor

    def turned(values):
        return (values * cosine + pltpu.roll(values, HEAD_DIM // 2, 1) * sine).astype(jnp.bfloat16)

    key_rows = turned(key_value[:, :HEAD_DIM])
    value_rows = (key_value[:, HEAD_DIM:] * factor).astype(jnp.bfloat16)
    bias = bias_ref[...]
    for head in range(queries.shape[1] // HEAD_DIM):
        columns = slice(head * HEAD_DIM, (head + 1) * HEAD_DIM)
        scores = lax.dot_general(
            turned(queries[:, columns]),
            key_rows,
            (((1,), (1,)), ((), ())),
            preferred_element_type=jnp.float32,
        )
        scores = scores * (1.0 / math.sqrt(HEAD_DIM)) + bias
        exp_scores = jnp.exp(scores - jnp.max(scores, axis=1, keepdims=True))
        inverse = 1.0 / jnp.sum(exp_scores, axis=1, keepdims=True)
        weights = (exp_scores * inverse).astype(jnp.bfloat16)
        out_ref[:, columns] = jnp.dot(
            weights, value_rows, preferred_element_type=jnp.float32
        ).astype(jnp.bfloat16)


def output_kernel(layer, width, fill, starts_ref, a_ref, o_hbm, outs, out_bufs, o_buf, sem, out_sem):
    blocks = outs[-1].shape[1] // width
    per_part = blocks // (len(outs) - 1)

    def copy(block):
        start = pl.multiple_of(starts_ref[block // blocks] + block % blocks * width, width)
        return pltpu.make_async_copy(
            o_hbm.at[layer, :, pl.ds(start, width)], o_buf.at[block], sem.at[block]
        )

    for block in range(2 * blocks):
        copy(block).start()
    fill()
    leaving = []
    for block in range(2 * blocks):
        copy(block).wait()
        product = jnp.dot(a_ref[...], o_buf[block], preferred_element_type=jnp.float32)
        which, inner = (
            (block // per_part, block % per_part)
            if block < blocks
            else (len(outs) - 1, block - blocks)
        )
        columns = slice(inner * width, (inner + 1) * width)
        out_bufs[which][:, columns] = product.astype(out_bufs[which].dtype)
        leaving.append(
            pltpu.make_async_copy(
                out_bufs[which].at[:, columns], outs[which].at[:, columns], out_sem.at[block]
            )
        )
        leaving[-1].start()
    for copy_out in leaving:
        copy_out.wait()


def output_shapes(rows, count, parts):
    return [(rows, count // parts)] * parts + [(rows, count)]


def output_scratch(rows, depth, count, parts, width):
    return [pltpu.VMEM(shape, jnp.bfloat16) for shape in output_shapes(rows, count, parts)] + [
        pltpu.VMEM((2 * count // width, depth, width), jnp.bfloat16),
        pltpu.SemaphoreType.DMA((2 * count // width,)),
        pltpu.SemaphoreType.DMA((2 * count // width,)),
    ]


def output_product(attended, o_weight, layer, starts, count, parts, width=512):
    rows, depth = attended.shape
    n = parts + 1

    def kernel(starts_ref, a_hbm, o_hbm, *refs):
        outs, a_ref, a_sem = refs[:n], refs[n], refs[n + 1]
        ready = fetch([a_hbm], [a_ref], a_sem)
        output_kernel(
            layer,
            width,
            lambda: ready(0),
            starts_ref,
            a_ref,
            o_hbm,
            outs,
            refs[n + 2 : 2 * n + 2],
            *refs[2 * n + 2 :],
        )

    *sent, kept = call(
        kernel,
        [jax.ShapeDtypeStruct(s, jnp.bfloat16) for s in output_shapes(rows, count, parts)],
        4 * rows * depth * count,
        4 * depth * count,
        "output_product",
        vmem=36 * MIB,
        in_specs=[in_smem] + [in_hbm] * 2,
        out_specs=[in_hbm] * n,
        scratch_shapes=buffers_of([attended]) + output_scratch(rows, depth, count, parts, width),
    )(starts, attended, o_weight)
    return sent, kept


def attention_output(features, operands, o_weight, layer, starts, count, width=512):
    rows, depth = operands[0].shape
    n = len(operands)

    def kernel(starts_ref, *refs):
        inputs, o_hbm, out_hbm, outs = refs[:n], refs[n], refs[n + 1], refs[n + 2 : n + 4]
        buffers, in_sem = refs[n + 4 : 2 * n + 4], refs[2 * n + 4]
        out_ref, sem = refs[2 * n + 5 : 2 * n + 7]
        ready = fetch(inputs, buffers, in_sem)

        def attend():
            for i in range(n):
                ready(i)
            attend_kernel(features, n > 6, *buffers, out_ref)
            pltpu.make_async_copy(out_ref, out_hbm, sem.at[0]).start()

        output_kernel(
            layer,
            width,
            attend,
            starts_ref,
            out_ref,
            o_hbm,
            outs,
            refs[2 * n + 7 : 2 * n + 9],
            *refs[2 * n + 9 :],
        )
        pltpu.make_async_copy(out_ref, out_hbm, sem.at[0]).wait()

    attended = jax.ShapeDtypeStruct((rows, depth), jnp.bfloat16)
    attended, sent, kept = call(
        kernel,
        [attended] + [jax.ShapeDtypeStruct((rows, count), jnp.bfloat16)] * 2,
        8 * rows * rows * depth + 4 * rows * depth * count,
        4 * depth * count,
        "attention_output",
        vmem=36 * MIB,
        in_specs=[in_smem] + [in_hbm] * (n + 1),
        out_specs=[in_hbm] * 3,
        scratch_shapes=buffers_of(operands)
        + buffers_of([attended])
        + output_scratch(rows, depth, count, 1, width),
    )(starts, *operands, o_weight)
    return attended, [sent], kept


def add_kernel(n_parts, *refs):
    inputs, out_hbm, buffers = refs[: n_parts + 1], refs[n_parts + 1], refs[n_parts + 2 : -3]
    in_sem, out_ref, out_sem = refs[-3:]
    ready = fetch(inputs, buffers, in_sem)
    ready(n_parts)
    kept_ref = buffers[n_parts]
    leaving = []
    for i in range(n_parts):
        ready(i)
        width = buffers[i].shape[1]
        columns = slice(i * width, (i + 1) * width)
        total = kept_ref[:, columns].astype(jnp.float32) + buffers[i][...].astype(jnp.float32)
        out_ref[:, columns] = total.astype(out_ref.dtype)
        leaving.append(
            pltpu.make_async_copy(out_ref.at[:, columns], out_hbm.at[:, columns], out_sem.at[i])
        )
        leaving[-1].start()
    for copy_out in leaving:
        copy_out.wait()


def add_parts(kept, parts):
    n = len(parts)
    return call(
        lambda *refs: add_kernel(n, *refs),
        jax.ShapeDtypeStruct(kept.shape, kept.dtype),
        kept.size,
        6 * kept.size,
        "chip_sum",
        in_specs=[in_hbm] * (n + 1),
        out_specs=in_hbm,
        scratch_shapes=buffers_of(list(parts) + [kept])
        + [pltpu.VMEM(kept.shape, kept.dtype), pltpu.SemaphoreType.DMA((n,))],
    )(*parts, kept)


def combine_kernel(n_in, n_out, parts, *refs):
    inputs, outs = refs[:n_in], refs[n_in : n_in + n_out]
    in_bufs, out_bufs = refs[n_in + n_out : 2 * n_in + n_out], refs[2 * n_in + n_out : -2]
    in_sem, out_sem = refs[-2:]
    width = outs[0].shape[1] // parts
    columns = [slice(part * width, (part + 1) * width) for part in range(parts)]
    coming = [
        [
            pltpu.make_async_copy(
                inputs[i].at[:, columns[part]], in_bufs[i].at[:, columns[part]], in_sem.at[i, part]
            )
            for i in range(n_in)
        ]
        for part in range(parts)
    ]
    for copies in coming:
        for copy in copies:
            copy.start()
    leaving = []
    for part in range(parts):
        for copy in coming[part]:
            copy.wait()
        values = [buf[:, columns[part]].astype(jnp.float32) for buf in in_bufs]
        total = values[-1]
        for value in values[-2::-1]:
            total = value + total
        for i in range(n_out):
            out_bufs[i][:, columns[part]] = total.astype(out_bufs[i].dtype)
            leaving.append(
                pltpu.make_async_copy(
                    out_bufs[i].at[:, columns[part]], outs[i].at[:, columns[part]], out_sem.at[i, part]
                )
            )
            leaving[-1].start()
    for copy in leaving:
        copy.wait()


def combine(inputs, dtypes, parts=4):
    shape = inputs[0].shape
    return call(
        lambda *refs: combine_kernel(len(inputs), len(dtypes), parts, *refs),
        [jax.ShapeDtypeStruct(shape, dtype) for dtype in dtypes],
        inputs[0].size * len(inputs),
        sum(array.nbytes for array in inputs) + 4 * inputs[0].size,
        "combine",
        in_specs=[in_hbm] * len(inputs),
        out_specs=[in_hbm] * len(dtypes),
        scratch_shapes=[pltpu.VMEM(shape, array.dtype) for array in inputs]
        + [pltpu.VMEM(shape, dtype) for dtype in dtypes]
        + [
            pltpu.SemaphoreType.DMA((len(inputs), parts)),
            pltpu.SemaphoreType.DMA((len(dtypes), parts)),
        ],
    )(*inputs)


def rope_tables(positions):
    half_depth = HEAD_DIM // 2
    inv_freq = rope_base ** (-2.0 * jnp.arange(half_depth, dtype=jnp.float32) / HEAD_DIM)
    angles = positions[:, None] * inv_freq[None, :]
    cosine, sine = jnp.cos(angles), jnp.sin(angles)
    return jnp.concatenate([cosine, cosine], axis=1), jnp.concatenate([-sine, sine], axis=1)


def normalize(rows):
    center = rows - jnp.mean(rows, axis=1, keepdims=True)
    factor = lax.rsqrt(jnp.mean(center * center, axis=1, keepdims=True) + ln_eps)
    return center * factor, factor


def norm_kernel(count_ref, affine_ref, patch_ref, out_ref):
    owners, padded, in_share = out_ref.shape
    slots = patch_ref.shape[0]
    vit = affine_ref.shape[1]
    counts = jnp.full((padded - slots, vit), count_ref[0].astype(jnp.float32))
    for group in range(patch_ref.shape[1] // vit):
        rows = patch_ref[:, group * vit : (group + 1) * vit].astype(jnp.float32)
        scaled = normalize(rows)[0] * affine_ref[0:1, :] + affine_ref[1:2, :]
        scaled = jnp.concatenate([scaled, counts], axis=0).astype(out_ref.dtype)
        for i in range(vit // in_share):
            out_ref[group * (vit // in_share) + i] = scaled[:, i * in_share : (i + 1) * in_share]


def norm_back_kernel(patch_ref, grads_ref, affine_ref, out_ref):
    _, _, in_share = grads_ref.shape
    slots = patch_ref.shape[0]
    vit = affine_ref.shape[1]
    per_group = vit // in_share
    for group in range(patch_ref.shape[1] // vit):
        rows = patch_ref[:, group * vit : (group + 1) * vit].astype(jnp.float32)
        unit, factor = normalize(rows)
        grads = jnp.concatenate(
            [grads_ref[group * per_group + i].astype(jnp.float32) for i in range(per_group)], axis=1
        )[:slots]
        grads = grads * affine_ref[0:1, :]
        along = jnp.mean(grads * unit, axis=1, keepdims=True)
        out_ref[:, group * vit : (group + 1) * vit] = factor * (
            grads - jnp.mean(grads, axis=1, keepdims=True) - unit * along
        )


def split_kernel(core_ref, rows_ref, out_ref):
    owners, part_rows, width = out_ref.shape
    slots = rows_ref.shape[0]
    first = core_ref[0] == 0
    for owner in range(owners):
        rows = rows_ref[:, owner * width : (owner + 1) * width].astype(jnp.float32)
        rest = jnp.zeros((2 * part_rows - slots, width), jnp.float32)
        rows = jnp.concatenate([rows, rest], axis=0)
        rows = jnp.where(first, rows[:part_rows], rows[part_rows:])
        out_ref[owner] = rows.astype(out_ref.dtype)


def pack_kernel(slots, rows_ref, weight_ref, out_ref, pack_ref):
    owners, padded, _ = rows_ref.shape
    packed_rows = out_ref.shape[0]
    row = lax.broadcasted_iota(jnp.int32, (packed_rows, padded), 0).astype(jnp.float32)
    slot = lax.broadcasted_iota(jnp.int32, (packed_rows, padded), 1).astype(jnp.float32)
    offset = jnp.zeros((1, 1), jnp.float32)
    packed = jnp.zeros((packed_rows, rows_ref.shape[2]), jnp.float32)
    for owner in range(owners):
        rows = rows_ref[owner]
        count = rows.astype(jnp.float32)[slots : slots + 1, 0:1]
        chosen = jnp.where((row == offset + slot) & (slot < count), 1.0, 0.0).astype(jnp.bfloat16)
        pack_ref[owner] = chosen
        packed = packed + jnp.dot(chosen, rows, preferred_element_type=jnp.float32)
        offset = offset + count
    out_ref[...] = jnp.dot(
        packed.astype(jnp.bfloat16), weight_ref[...], preferred_element_type=jnp.float32
    ).astype(out_ref.dtype)


def pack_grads_kernel(core_ref, mine_ref, other_ref, pack_ref, weight_ref, out_ref):
    packed = jnp.zeros((out_ref.shape[0], mine_ref.shape[2]), jnp.float32)
    first = core_ref[0] == 0
    padded = pack_ref.shape[2]
    for owner in range(mine_ref.shape[0]):
        mine = mine_ref[owner].astype(jnp.float32)
        other = other_ref[owner].astype(jnp.float32)
        rows = jnp.concatenate(
            [jnp.where(first, mine, other), jnp.where(first, other, mine)], axis=0
        )
        packed = packed + jnp.dot(
            pack_ref[owner],
            rows[:padded].astype(jnp.bfloat16),
            preferred_element_type=jnp.float32,
        )
    out_ref[...] = lax.dot_general(
        packed.astype(jnp.bfloat16),
        weight_ref[...],
        (((1,), (1,)), ((), ())),
        preferred_element_type=jnp.float32,
    ).astype(out_ref.dtype)


def halves_kernel(core_ref, rows_ref, weight_ref, kept_ref, sent_ref):
    product = jnp.dot(rows_ref[...], weight_ref[...], preferred_element_type=jnp.float32)
    half = kept_ref.shape[1]
    first = core_ref[0] == 0
    kept_ref[...] = jnp.where(first, product[:, :half], product[:, half:])
    sent_ref[...] = jnp.where(first, product[:, half:], product[:, :half]).astype(sent_ref.dtype)


def unpack_kernel(first_ref, second_ref, pack_ref, out_ref):
    total = first_ref[...].astype(jnp.float32) + second_ref[...].astype(jnp.float32)
    total = total.astype(jnp.bfloat16)
    for owner in range(pack_ref.shape[0]):
        out_ref[owner] = lax.dot_general(
            pack_ref[owner], total, (((0,), (0,)), ((), ())), preferred_element_type=jnp.float32
        ).astype(out_ref.dtype)


def assemble_kernel(core_ref, shift_ref, mine_hbm, other_hbm, out_ref, mine_ref, other_ref, sem):
    owners, _, half = mine_ref.shape
    first = core_ref[0] == 0
    ready = fetch([mine_hbm, other_hbm], [mine_ref, other_ref], sem)
    ready(0)
    ready(1)
    for owner in range(owners):
        mine = mine_ref[owner].astype(jnp.float32)
        other = other_ref[owner].astype(jnp.float32)
        for i in range(2):
            columns = slice((2 * owner + i) * half, (2 * owner + i + 1) * half)
            part = jnp.where(first, mine, other) if i == 0 else jnp.where(first, other, mine)
            out_ref[:, columns] = (part + shift_ref[:, columns]).astype(out_ref.dtype)


def exchange(values):
    return lax.all_to_all(values, "dp", split_axis=0, concat_axis=0, tiled=True)


def four_chip_local(
    patches,
    ln_gain,
    ln_shift,
    w_in,
    b_in,
    w_out,
    b_out,
    place,
    image_counts,
    text_rows,
    segments,
    norm_gain,
    q_weight,
    kv_weight,
    o_weight,
    grad_rows,
):
    bf16, f32 = jnp.bfloat16, jnp.float32
    shape_of = jax.ShapeDtypeStruct
    me = lax.axis_index("sec")
    core, chip = me & 1, me >> 1
    core_word = core.reshape(1).astype(jnp.int32)
    owners = lax.axis_size("dp")
    slots = patches.shape[0]
    padded = slots + 16 - slots % 16
    tokens, share = text_rows.shape
    features = share * 4
    layers = q_weight.shape[0]
    in_share, hidden_share = w_in.shape
    out_share = w_out.shape[1]
    packed_rows = owners * (tokens // 16)
    chunk = packed_rows // owners
    affine = jnp.stack([ln_gain, ln_shift]).astype(f32)

    normed = call(
        norm_kernel,
        shape_of((owners, padded, in_share), bf16),
        slots * owners * in_share * 10,
        slots * owners * in_share * 4,
        "normed_patches",
        in_specs=[in_smem] + in_vmem(2),
    )(image_counts, affine, patches)
    received = exchange(normed)

    text_rows = after(text_rows, normed)
    far = swap(text_rows, "sec", ACROSS)
    gathered_text = [text_rows, swap(text_rows, "sec", CORE)]
    gains = norm_gain.astype(f32)
    starts = jnp.stack([(me ^ r) * share for r in range(4)]).astype(jnp.int32)
    projected = project(gathered_text, starts[:2], gains, q_weight, kv_weight, 0, None)
    received, projected = lax.optimization_barrier((received, projected))
    far = after(far, received)
    gathered_text += [far, swap(far, "sec", CORE)]
    pre_part, pack = call(
        lambda *refs: pack_kernel(slots, *refs),
        [shape_of((packed_rows, hidden_share), bf16), shape_of((owners, packed_rows, padded), bf16)],
        2 * packed_rows * in_share * hidden_share,
        2 * in_share * hidden_share,
        "pre_act",
    )(received, w_in)
    pre_parts = exchange(pre_part.reshape(owners, chunk, hidden_share))

    shift = after(b_out, received).reshape(1, share)
    shift_far = swap(shift, "sec", ACROSS)
    shifts = [shift, swap(shift, "sec", CORE), shift_far, swap(shift_far, "sec", CORE)]
    shifts = jnp.take(jnp.concatenate(shifts, axis=0), jnp.arange(4, dtype=jnp.int32) ^ me, axis=0)
    shifts = shifts.astype(f32).reshape(1, -1)
    allowed, positions = doc_mask(segments[0])
    bias = jnp.where(allowed, 0.0, -1e30).astype(f32)
    cosine, sine = rope_tables(positions)
    projected = project(gathered_text[2:], starts[2:], gains, q_weight, kv_weight, 0, projected)
    pre_act = jnp.sum(pre_parts.astype(f32), axis=0) + b_in.astype(f32)
    hidden_units = gelu_exact(pre_act).astype(bf16)
    hidden_all = exchange(jnp.broadcast_to(hidden_units[None], (owners, chunk, hidden_share)))
    slot_index = jnp.arange(padded, dtype=jnp.int32)
    token_index = jnp.arange(tokens, dtype=jnp.int32)
    places = jnp.pad(place, (0, padded - slots))
    select = (places[None, :] == token_index[:, None]) & (slot_index < image_counts[0])[None, :]
    is_image = jnp.any(select, axis=1)

    hidden_all, projected, cosine, sine, bias, shifts = lax.optimization_barrier(
        (hidden_all, projected, cosine, sine, bias, shifts)
    )
    kept, sent = call(
        halves_kernel,
        [
            shape_of((packed_rows, out_share // 2), f32),
            shape_of((packed_rows, out_share // 2), bf16),
        ],
        2 * packed_rows * out_share * hidden_share,
        2 * out_share * hidden_share,
        "merged",
        in_specs=[in_smem] + in_vmem(2),
    )(core_word, hidden_all.reshape(packed_rows, hidden_share), w_out)
    chip_sum = (kept + swap(sent, "sec", CORE).astype(f32)).astype(bf16)

    def unpack(first, second):
        width = first.shape[1]
        return exchange(
            call(
                unpack_kernel,
                shape_of((owners, padded, width), bf16),
                2 * packed_rows * owners * padded * width,
                2 * owners * padded * width,
                "unpack",
            )(first, second, pack)
        )

    merged_half = unpack(chip_sum, swap(chip_sum, "sec", ACROSS))
    image_rows = call(
        assemble_kernel,
        shape_of((padded, features), bf16),
        padded * features,
        padded * features * 4,
        "image_rows",
        in_specs=[in_smem] + in_vmem(1) + [in_hbm] * 2,
        scratch_shapes=buffers_of([merged_half] * 2),
    )(core_word, shifts, merged_half, swap(merged_half, "sec", CORE))

    def column(chip_index, core_bit):
        return (2 * chip_index + core_bit) * share

    images = project(
        [image_rows], jnp.zeros((1,), jnp.int32), gains, q_weight, kv_weight, 0, None
    )

    def start_rows(r):
        image_part = lax.dynamic_slice_in_dim(image_rows, column(chip ^ r, core), share, 1)
        picked = jnp.dot(select.astype(bf16), image_part, preferred_element_type=f32)
        return jnp.where(is_image[:, None], picked.astype(bf16), gathered_text[2 * r])

    def columns_of(r):
        return jnp.stack([column(chip ^ r, core ^ 1), column(chip ^ r, core)]).astype(
            jnp.int32
        )

    def shared(sent):
        return [swap(part, "sec", CORE) for part in sent]

    grad_rows = after(grad_rows, merged_half)
    grad_parts = call(
        split_kernel,
        shape_of((owners, (padded + 16) // 32 * 16, out_share), bf16),
        slots * owners * out_share,
        slots * owners * out_share * 4,
        "split_grads",
        in_specs=[in_smem] + in_vmem(1),
    )(core_word, grad_rows)
    grads_there = exchange(grad_parts)

    def grads_first():
        grad_part = call(
            pack_grads_kernel,
            shape_of((packed_rows, hidden_share), bf16),
            2 * packed_rows * out_share * hidden_share,
            2 * out_share * hidden_share,
            "hidden_grads",
            in_specs=[in_smem] + in_vmem(4),
        )(core_word, grads_there, swap(grads_there, "sec", CORE), pack, w_out)
        return grad_part.reshape(owners, chunk, hidden_share)

    def grads_second(parts):
        hidden_grads = jnp.sum(parts.astype(f32), axis=0)
        _, pull_gelu = jax.vjp(gelu_exact, pre_act)
        pre_grads = pull_gelu(hidden_grads)[0].astype(bf16)
        return jnp.broadcast_to(pre_grads[None], (owners, chunk, hidden_share))

    def grads_third(pre_grads):
        back = lax.dot_general(
            pre_grads.reshape(packed_rows, hidden_share),
            w_in,
            (((1,), (1,)), ((), ())),
            preferred_element_type=f32,
        )
        return (back + swap(back, "sec", CORE)).astype(bf16)

    operands = list(projected) + [cosine, sine, bias] + list(images) + [select.astype(f32)]

    def partly(old, rows, r, layer):
        here = jnp.stack([column(chip ^ r, core), column(chip ^ r, core ^ 1)])
        return project(
            [rows, swap(rows, "sec", CORE)],
            here.astype(jnp.int32),
            gains,
            q_weight,
            kv_weight,
            layer,
            old,
        )

    grads, held = None, None
    for layer in range(1, layers):
        attended, sent, kept = attention_output(
            features, operands, o_weight, layer - 1, columns_of(1), share
        )
        other_sum = add_parts(kept, shared(sent))
        attended = after(attended, other_sum)
        came_here = swap(other_sum, "sec", ACROSS)
        sent, kept = output_product(attended, o_weight, layer - 1, columns_of(0), share, 4)
        own_sum = add_parts(kept, shared(sent))
        if held is None:
            held = [start_rows(0), start_rows(1)]
        if grads is None:
            grads_there = after(grads_there, own_sum)
            grads = grads_first()
            came_here = after(came_here, grads)
            grads = exchange(grads_second(exchange(grads)))
        came_here = after(came_here, own_sum)
        came_there = swap(own_sum, "sec", ACROSS)
        now = held[0].astype(f32) + (own_sum.astype(f32) + came_here.astype(f32))
        rounded = now.astype(bf16)
        projected = partly(None, rounded, 0, layer)
        if layer == 1:
            grads = grads_third(grads)
        came_there = after(came_there, (projected, held[1]))
        (there,) = combine([held[1], other_sum, came_there], [bf16])
        projected = partly(projected, there, 1, layer)
        held = [now, there]
        operands = list(projected) + [cosine, sine, bias]

    if layers == 1:
        held = [start_rows(0)]
        grads = grads_third(exchange(grads_second(exchange(grads_first()))))
    back = grads
    back_far = swap(back, "sec", ACROSS)
    operands = after(operands, back_far)

    last = layers - 1
    attended, sent, kept = attention_output(
        features, operands, o_weight, last, columns_of(1), share
    )
    other_sum = add_parts(kept, shared(sent))
    attended = after(attended, other_sum)
    back_far = after(back_far, other_sum)
    came = swap(other_sum, "sec", ACROSS)
    normed_grads = unpack(back, back_far)
    sent, kept = output_product(attended, o_weight, last, columns_of(0), share, 4)
    own_sum = add_parts(kept, shared(sent))
    patch_grads = call(
        norm_back_kernel,
        shape_of(patches.shape, f32),
        slots * owners * in_share * 10,
        slots * owners * in_share * 8,
        "patch_grads",
    )(patches, normed_grads, affine)
    came, own_sum, patch_grads = lax.optimization_barrier((came, own_sum, patch_grads))
    return combine([held[0], own_sum, came], [f32])[0], patch_grads


def local(
    patches,
    ln_gain,
    ln_shift,
    w_in,
    b_in,
    w_out,
    b_out,
    place,
    image_counts,
    text_rows,
    segments,
    norm_gain,
    q_weight,
    kv_weight,
    o_weight,
    grad_rows,
):
    slot_count = patches.shape[0]
    tokens, share = text_rows.shape
    slot_index = jnp.arange(slot_count, dtype=jnp.int32)
    live_slot = slot_index < image_counts[0]
    merged, patch_grads = merger_rows(
        patches,
        ln_gain,
        ln_shift,
        w_in,
        b_in,
        w_out,
        live_slot,
        image_counts[0],
        grad_rows,
        lax.axis_size("dp") * (tokens // 16),
    )
    merged_local = lax.dynamic_slice_in_dim(
        merged, lax.axis_index(("sec", "mp")) * share, share, 1
    ).astype(jnp.float32)
    merged_local = (merged_local + b_out.astype(jnp.float32)).astype(jnp.bfloat16)
    token_index = jnp.arange(tokens, dtype=jnp.int32)
    select = (place[:, None] == token_index[None, :]) & live_slot[:, None]
    is_image = jnp.any(select, axis=0)
    picked = lax.dot_general(
        select.astype(jnp.bfloat16),
        merged_local,
        (((0,), (0,)), ((), ())),
        preferred_element_type=jnp.float32,
    )
    start_rows = jnp.where(is_image[:, None], picked, text_rows.astype(jnp.float32)).astype(
        jnp.bfloat16
    )
    allowed, positions = doc_mask(segments[0])
    layer_count = q_weight.shape[0]
    current = start_rows.astype(jnp.float32)
    for layer_index in range(layer_count):
        current = section_features(
            current,
            norm_gain[layer_index],
            allowed,
            positions,
            q_weight[layer_index],
            kv_weight[layer_index],
            o_weight[layer_index],
        )
    return (current, patch_grads)


def solution(mesh):
    in_specs = (
        P("dp", None),
        P(),
        P(),
        P("dp", ("sec", "mp")),
        P(("sec", "mp")),
        P(("sec", "mp"), "dp"),
        P(("sec", "mp")),
        P("dp"),
        P("dp"),
        P("dp", ("sec", "mp")),
        P("dp", None),
        P(),
        P(None, None, ("sec", "mp")),
        P(None, None, ("sec", "mp"), None),
        P(None, ("sec", "mp"), None),
        P("dp", None),
    )
    out_specs = (P("dp", ("sec", "mp")), P("dp", None))
    step = four_chip_local if mesh.shape["sec"] == 4 and mesh.shape["mp"] == 1 else local
    return jax.shard_map(step, mesh=mesh, in_specs=in_specs, out_specs=out_specs, check_vma=False)
```

```python
import math

import jax
import jax.numpy as jnp
from jax import lax
from jax.experimental import pallas as pl
from jax.experimental.pallas import tpu as pltpu
from jax.sharding import PartitionSpec as P

D = 8192
HEAD_DIM = 128


ln_eps = 1e-06
rms_eps = 1e-06
rope_base = 1000000.0


def group_norm(patch_rows, ln_gain, ln_shift):
    row_count = patch_rows.shape[0]
    grouped = patch_rows.astype(jnp.float32).reshape(row_count, -1, ln_gain.shape[0])
    center = grouped - jnp.mean(grouped, axis=-1, keepdims=True)
    spread = jnp.mean(center * center, axis=-1, keepdims=True)
    scaled = center * lax.rsqrt(spread + ln_eps) * ln_gain.astype(jnp.float32) + ln_shift.astype(
        jnp.float32
    )
    return scaled.reshape(row_count, -1)


def gelu_exact(values):
    return jax.nn.gelu(values, approximate=False)


def rotate(values, positions):
    head_depth = values.shape[-1]
    half_depth = head_depth // 2
    inv_freq = rope_base ** (-2.0 * jnp.arange(half_depth, dtype=jnp.float32) / head_depth)
    angles = positions[:, None] * inv_freq[None, :]
    cosine = jnp.cos(angles)[:, None, :]
    sine_part = jnp.sin(angles)[:, None, :]
    first_half = values[..., :half_depth]
    second = values[..., half_depth:]
    return jnp.concatenate(
        [first_half * cosine - second * sine_part, second * cosine + first_half * sine_part],
        axis=-1,
    )


def doc_mask(segment_ids):
    token_index = jnp.arange(segment_ids.shape[0], dtype=jnp.int32)
    same_doc = segment_ids[:, None] == segment_ids[None, :]
    allowed = same_doc & (token_index[None, :] <= token_index[:, None])
    positions = jnp.sum(allowed.astype(jnp.int32), axis=1) - 1
    return (allowed, positions.astype(jnp.float32))


def attend(normed, allowed, positions, q_local, kv_local):
    token_count = normed.shape[0]
    queries = jnp.dot(normed, q_local, preferred_element_type=jnp.float32).reshape(
        token_count, -1, HEAD_DIM
    )
    key_value = jnp.einsum("td,kcd->tkc", normed, kv_local, preferred_element_type=jnp.float32)
    key_value = lax.all_gather(key_value, "mp", axis=2, tiled=True)
    key_rows = rotate(key_value[:, 0:1, :], positions)[:, 0, :].astype(jnp.bfloat16)
    value_rows = key_value[:, 1, :].astype(jnp.bfloat16)
    queries = rotate(queries, positions).astype(jnp.bfloat16)
    scores = jnp.einsum("thd,sd->hts", queries, key_rows, preferred_element_type=jnp.float32) * (
        1.0 / math.sqrt(HEAD_DIM)
    )
    scores = jnp.where(allowed[None], scores, -jnp.inf)
    row_max = jnp.max(scores, axis=-1, keepdims=True)
    exp_scores = jnp.exp(scores - row_max)
    attn_weights = (exp_scores / jnp.sum(exp_scores, axis=-1, keepdims=True)).astype(jnp.bfloat16)
    attended = jnp.einsum(
        "hts,sd->thd", attn_weights, value_rows, preferred_element_type=jnp.float32
    )
    return attended.astype(jnp.bfloat16).reshape(token_count, -1)


def gather_features(rows_local):
    return lax.all_gather(rows_local, ("sec", "mp"), axis=1, tiled=True)


def section_features(rows_local, gain_row, allowed, positions, q_local, kv_local, o_local):
    share = rows_local.shape[1]
    square_sums = lax.psum(jnp.sum(rows_local * rows_local, axis=1), ("sec", "mp"))
    factor = lax.rsqrt(square_sums / D + rms_eps)
    gain_local = lax.dynamic_slice_in_dim(
        gain_row, lax.axis_index(("sec", "mp")) * share, share, 0
    ).astype(jnp.float32)
    normed_local = (rows_local * factor[:, None] * gain_local[None, :]).astype(jnp.bfloat16)
    normed = gather_features(normed_local)
    attended = attend(normed, allowed, positions, q_local, kv_local)
    summed = lax.psum_scatter(
        lax.dot_general(
            o_local, attended, (((0,), (1,)), ((), ())), preferred_element_type=jnp.float32
        ),
        ("sec", "mp"),
        scatter_dimension=0,
        tiled=True,
    )
    return rows_local + summed.T


def swap(values, axis, mask):
    size = lax.axis_size(axis)
    return lax.ppermute(values, axis, [(i, i ^ mask) for i in range(size)])


def spread_rows(values, parts):
    return lax.all_to_all(values, "dp", split_axis=0, concat_axis=0, tiled=True).reshape(
        (parts, -1) + values.shape[1:]
    )


def merger_rows(patches, ln_gain, ln_shift, w_in, b_in, w_out, live_slot, count, grad_rows, packed_rows):
    owners = lax.axis_size("dp")
    group = lax.axis_size(("sec", "mp"))
    slots = patches.shape[0]
    in_share, hidden_share = w_in.shape
    out_share = w_out.shape[1]
    share = in_share + out_share

    normed = group_norm(patches, ln_gain, ln_shift).astype(jnp.bfloat16)
    slot_grads = jnp.where(live_slot[:, None], grad_rows, jnp.zeros_like(grad_rows))
    rows = jnp.concatenate(
        [normed.reshape(slots, owners, in_share), slot_grads.reshape(slots, owners, out_share)],
        axis=2,
    ).transpose(1, 0, 2)
    count_rows = jnp.broadcast_to(count.astype(jnp.bfloat16), (owners, 8, share))
    received = lax.all_to_all(
        jnp.concatenate([rows, count_rows], axis=1), "dp", split_axis=0, concat_axis=0, tiled=True
    )
    counts = received[:, slots, 0].astype(jnp.int32)
    owner_index = jnp.arange(owners, dtype=jnp.int32)
    offsets = jnp.sum(jnp.where(owner_index[None, :] < owner_index[:, None], counts[None, :], 0), axis=1)
    slot_index = jnp.arange(slots, dtype=jnp.int32)
    target = jnp.where(
        slot_index[None, :] < counts[:, None], offsets[:, None] + slot_index[None, :], -1
    ).reshape(-1)
    pack = (jnp.arange(packed_rows, dtype=jnp.int32)[:, None] == target[None, :]).astype(jnp.bfloat16)
    packed = jnp.dot(
        pack, received[:, :slots].reshape(owners * slots, share), preferred_element_type=jnp.float32
    ).astype(jnp.bfloat16)

    pre_part = jnp.dot(packed[:, :in_share], w_in, preferred_element_type=jnp.float32)
    grad_part = lax.dot_general(
        packed[:, in_share:], w_out, (((1,), (1,)), ((), ())), preferred_element_type=jnp.float32
    )
    parts = jnp.concatenate([pre_part, grad_part], axis=1).astype(jnp.bfloat16)
    chunk = packed_rows // owners
    parts = lax.all_to_all(
        parts.reshape(owners, chunk, 2 * hidden_share), "dp", split_axis=0, concat_axis=0, tiled=True
    )
    sums = jnp.sum(parts.astype(jnp.float32), axis=0)
    pre_act = sums[:, :hidden_share] + b_in.astype(jnp.float32)
    hidden_units, pull_gelu = jax.vjp(gelu_exact, pre_act)
    pre_grads = pull_gelu(sums[:, hidden_share:])[0]
    both = jnp.concatenate([hidden_units, pre_grads], axis=1).astype(jnp.bfloat16)
    both = lax.all_to_all(
        jnp.broadcast_to(both[None], (owners, chunk, 2 * hidden_share)),
        "dp",
        split_axis=0,
        concat_axis=0,
        tiled=True,
    ).reshape(packed_rows, 2 * hidden_share)
    merged_part = jnp.dot(both[:, :hidden_share], w_out, preferred_element_type=jnp.float32)
    back_part = lax.dot_general(
        both[:, hidden_share:], w_in, (((1,), (1,)), ((), ())), preferred_element_type=jnp.float32
    )
    tail = jnp.concatenate(
        [
            merged_part.astype(jnp.bfloat16).reshape(packed_rows, group, out_share // group),
            back_part.astype(jnp.bfloat16).reshape(packed_rows, group, in_share // group),
        ],
        axis=2,
    ).reshape(packed_rows, group * (share // group))
    tail = lax.dot_general(
        pack, tail, (((0,), (0,)), ((), ())), preferred_element_type=jnp.float32
    ).astype(jnp.bfloat16)
    tail = tail.reshape(owners * slots, group, share // group).transpose(1, 0, 2)
    me = lax.axis_index(("sec", "mp"))
    parts_now = tail.astype(jnp.float32)
    index = jnp.arange(group, dtype=jnp.int32) ^ me
    parts_now = jnp.take(parts_now, index, axis=0)
    mask = 1
    while mask < group:
        pairs = parts_now.reshape(-1, 2, owners * slots, share // group)
        received = swap(pairs[:, 1].astype(jnp.bfloat16), ("sec", "mp"), mask)
        parts_now = pairs[:, 0] + received.astype(jnp.float32)
        mask *= 2
    mine = parts_now.reshape(owners, slots, share // group).astype(jnp.bfloat16)
    mine = lax.all_to_all(mine, "dp", split_axis=0, concat_axis=0, tiled=True)
    gathered = mine[None]
    mask = group // 2
    while mask >= 1:
        gathered = jnp.concatenate([gathered, swap(gathered, ("sec", "mp"), mask)], axis=0)
        mask //= 2
    order = [0]
    mask = group // 2
    while mask >= 1:
        order = order + [i ^ mask for i in order]
        mask //= 2
    place_of = [0] * group
    for where_now, relative in enumerate(order):
        place_of[relative] = where_now
    gathered = jnp.take(gathered, jnp.asarray(place_of, jnp.int32)[index], axis=0)
    gathered = gathered.transpose(2, 1, 0, 3)
    merged = gathered[..., : out_share // group].reshape(slots, owners * out_share)
    normed_grads = gathered[..., out_share // group :].reshape(slots, owners * in_share)
    _, pull_norm = jax.vjp(
        lambda values: group_norm(values, ln_gain, ln_shift), patches.astype(jnp.float32)
    )
    return merged, pull_norm(normed_grads.astype(jnp.float32))[0]


MIB = 1024 * 1024
WEIGHT = 64
CORE, ACROSS = 1, 2


def call(kernel, out_shape, flops, n_bytes, name, vmem=16 * MIB, **more):
    return pl.pallas_call(
        kernel,
        out_shape=out_shape,
        cost_estimate=pl.CostEstimate(
            flops=int(flops) // WEIGHT, bytes_accessed=int(n_bytes) // WEIGHT, transcendentals=0
        ),
        compiler_params=pltpu.CompilerParams(vmem_limit_bytes=vmem),
        name=name,
        **more,
    )


def in_vmem(count):
    return [pl.BlockSpec(memory_space=pltpu.VMEM)] * count


in_smem = pl.BlockSpec(memory_space=pltpu.SMEM)
in_hbm = pl.BlockSpec(memory_space=pltpu.HBM)


def after(values, others):
    return lax.optimization_barrier((values, others))[0]


def fetch(refs, buffers, sem):
    copies = [
        pltpu.make_async_copy(ref, buffer, sem.at[i])
        for i, (ref, buffer) in enumerate(zip(refs, buffers))
    ]
    for copy in copies:
        copy.start()
    return lambda i: copies[i].wait()


def buffers_of(arrays):
    return [pltpu.VMEM(array.shape, array.dtype) for array in arrays] + [
        pltpu.SemaphoreType.DMA((len(arrays),))
    ]


def project_kernel(layer, width, n_parts, fresh, starts_ref, gain_ref, q_hbm, kv_hbm, *refs):
    n_in = n_parts + (0 if fresh else 3)
    inputs, outs, buffers = refs[:n_in], refs[n_in : n_in + 3], refs[n_in + 3 :]
    x_refs, x_sem, q_buf, kv_buf, q_sem, kv_sem = buffers[:n_parts], *buffers[n_parts:]
    out_q, out_kv, out_sq = outs
    per_part = x_refs[0].shape[1] // width
    lanes = out_sq.shape[1]

    def place_of(block):
        part, inner = block // per_part, block % per_part
        return pl.multiple_of(starts_ref[part] + inner * width, width)

    def copies(block):
        rows = pl.ds(place_of(block), width)
        return (
            pltpu.make_async_copy(q_hbm.at[layer, rows, :], q_buf.at[block], q_sem.at[block]),
            pltpu.make_async_copy(kv_hbm.at[layer, :, :, rows], kv_buf.at[block], kv_sem.at[block]),
        )

    n_blocks = n_parts * per_part
    ready = fetch(inputs, list(x_refs) + ([] if fresh else list(outs)), x_sem)
    for block in range(n_blocks):
        for copy in copies(block):
            copy.start()
    if fresh:
        out_q[...] = jnp.zeros_like(out_q)
        out_kv[...] = jnp.zeros_like(out_kv)
        out_sq[...] = jnp.zeros_like(out_sq)
    else:
        for i in range(n_parts, n_in):
            ready(i)
    for block in range(n_blocks):
        inner = block % per_part
        if inner == 0:
            ready(block // per_part)
        rows = x_refs[block // per_part][:, inner * width : (inner + 1) * width].astype(jnp.float32)
        squares = rows * rows
        total = squares[:, :lanes]
        for i in range(1, width // lanes):
            total = total + squares[:, i * lanes : (i + 1) * lanes]
        out_sq[...] += total
        gain = gain_ref[layer : layer + 1, pl.ds(place_of(block), width)]
        normed = (rows * gain).astype(jnp.bfloat16)
        for copy in copies(block):
            copy.wait()
        out_q[...] += jnp.dot(normed, q_buf[block], preferred_element_type=jnp.float32)
        for i in range(2):
            out_kv[:, i * HEAD_DIM : (i + 1) * HEAD_DIM] += lax.dot_general(
                normed, kv_buf[block, i], (((1,), (1,)), ((), ())), preferred_element_type=jnp.float32
            )


def project(parts, starts, gains, q_weight, kv_weight, layer, old, width=512):
    rows, part_width = parts[0].shape
    n_parts = len(parts)
    n_blocks = n_parts * part_width // width
    columns = q_weight.shape[2]
    shapes = [(rows, columns), (rows, 2 * HEAD_DIM), (rows, HEAD_DIM)]
    old = [] if old is None else list(old)
    features = n_parts * part_width
    return call(
        lambda *refs: project_kernel(layer, width, n_parts, not old, *refs),
        [jax.ShapeDtypeStruct(shape, jnp.float32) for shape in shapes],
        2 * rows * features * (columns + 2 * HEAD_DIM),
        features * (columns + 2 * HEAD_DIM) * 2 + rows * features * 2,
        "project",
        vmem=48 * MIB,
        in_specs=[in_smem] + in_vmem(1) + [in_hbm] * (2 + n_parts + len(old)),
        out_specs=in_vmem(3),
        scratch_shapes=[pltpu.VMEM(part.shape, part.dtype) for part in parts]
        + [
            pltpu.SemaphoreType.DMA((n_parts + len(old),)),
            pltpu.VMEM((n_blocks, width, columns), jnp.bfloat16),
            pltpu.VMEM((n_blocks, 2, HEAD_DIM, width), jnp.bfloat16),
            pltpu.SemaphoreType.DMA((n_blocks,)),
            pltpu.SemaphoreType.DMA((n_blocks,)),
        ],
    )(starts, gains, q_weight, kv_weight, *parts, *old)


def attend_kernel(features, with_images, *refs):
    q_ref, kv_ref, sq_ref, cos_ref, sin_ref, bias_ref = refs[:6]
    out_ref = refs[-1]
    queries, key_value, squares = q_ref[...], kv_ref[...], sq_ref[...]
    if with_images:
        image_q, image_kv, image_sq, select_ref = refs[6:10]
        select = select_ref[...]
        is_image = jnp.sum(select, axis=1, keepdims=True) > 0.0

        def put(image_ref, values):
            picked = jnp.dot(
                select,
                image_ref[...],
                preferred_element_type=jnp.float32,
                precision=lax.Precision.HIGHEST,
            )
            return jnp.where(is_image, picked, values)

        queries, key_value, squares = (
            put(image_q, queries),
            put(image_kv, key_value),
            put(image_sq, squares),
        )
    factor = lax.rsqrt(jnp.sum(squares, axis=1, keepdims=True) / features + rms_eps)
    cosine, sine = cos_ref[...] * factor, sin_ref[...] * factor

    def turned(values):
        return (values * cosine + pltpu.roll(values, HEAD_DIM // 2, 1) * sine).astype(jnp.bfloat16)

    key_rows = turned(key_value[:, :HEAD_DIM])
    value_rows = (key_value[:, HEAD_DIM:] * factor).astype(jnp.bfloat16)
    bias = bias_ref[...]
    for head in range(queries.shape[1] // HEAD_DIM):
        columns = slice(head * HEAD_DIM, (head + 1) * HEAD_DIM)
        scores = lax.dot_general(
            turned(queries[:, columns]),
            key_rows,
            (((1,), (1,)), ((), ())),
            preferred_element_type=jnp.float32,
        )
        scores = scores * (1.0 / math.sqrt(HEAD_DIM)) + bias
        exp_scores = jnp.exp(scores - jnp.max(scores, axis=1, keepdims=True))
        inverse = 1.0 / jnp.sum(exp_scores, axis=1, keepdims=True)
        weights = (exp_scores * inverse).astype(jnp.bfloat16)
        out_ref[:, columns] = jnp.dot(
            weights, value_rows, preferred_element_type=jnp.float32
        ).astype(jnp.bfloat16)


def output_kernel(layer, width, fill, starts_ref, a_ref, o_hbm, outs, out_bufs, o_buf, sem, out_sem):
    blocks = outs[-1].shape[1] // width
    per_part = blocks // (len(outs) - 1)

    def copy(block):
        start = pl.multiple_of(starts_ref[block // blocks] + block % blocks * width, width)
        return pltpu.make_async_copy(
            o_hbm.at[layer, :, pl.ds(start, width)], o_buf.at[block], sem.at[block]
        )

    for block in range(2 * blocks):
        copy(block).start()
    fill()
    leaving = []
    for block in range(2 * blocks):
        copy(block).wait()
        product = jnp.dot(a_ref[...], o_buf[block], preferred_element_type=jnp.float32)
        which, inner = (
            (block // per_part, block % per_part)
            if block < blocks
            else (len(outs) - 1, block - blocks)
        )
        columns = slice(inner * width, (inner + 1) * width)
        out_bufs[which][:, columns] = product.astype(out_bufs[which].dtype)
        leaving.append(
            pltpu.make_async_copy(
                out_bufs[which].at[:, columns], outs[which].at[:, columns], out_sem.at[block]
            )
        )
        leaving[-1].start()
    for copy_out in leaving:
        copy_out.wait()


def output_shapes(rows, count, parts):
    return [(rows, count // parts)] * parts + [(rows, count)]


def output_scratch(rows, depth, count, parts, width):
    return [pltpu.VMEM(shape, jnp.bfloat16) for shape in output_shapes(rows, count, parts)] + [
        pltpu.VMEM((2 * count // width, depth, width), jnp.bfloat16),
        pltpu.SemaphoreType.DMA((2 * count // width,)),
        pltpu.SemaphoreType.DMA((2 * count // width,)),
    ]


def output_product(attended, o_weight, layer, starts, count, parts, width=512):
    rows, depth = attended.shape
    n = parts + 1

    def kernel(starts_ref, a_hbm, o_hbm, *refs):
        outs, a_ref, a_sem = refs[:n], refs[n], refs[n + 1]
        ready = fetch([a_hbm], [a_ref], a_sem)
        output_kernel(
            layer,
            width,
            lambda: ready(0),
            starts_ref,
            a_ref,
            o_hbm,
            outs,
            refs[n + 2 : 2 * n + 2],
            *refs[2 * n + 2 :],
        )

    *sent, kept = call(
        kernel,
        [jax.ShapeDtypeStruct(s, jnp.bfloat16) for s in output_shapes(rows, count, parts)],
        4 * rows * depth * count,
        4 * depth * count,
        "output_product",
        vmem=36 * MIB,
        in_specs=[in_smem] + [in_hbm] * 2,
        out_specs=[in_hbm] * n,
        scratch_shapes=buffers_of([attended]) + output_scratch(rows, depth, count, parts, width),
    )(starts, attended, o_weight)
    return sent, kept


def attention_output(features, operands, o_weight, layer, starts, count, width=512):
    rows, depth = operands[0].shape
    n = len(operands)

    def kernel(starts_ref, *refs):
        inputs, o_hbm, out_hbm, outs = refs[:n], refs[n], refs[n + 1], refs[n + 2 : n + 4]
        buffers, in_sem = refs[n + 4 : 2 * n + 4], refs[2 * n + 4]
        out_ref, sem = refs[2 * n + 5 : 2 * n + 7]
        ready = fetch(inputs, buffers, in_sem)

        def attend():
            for i in range(n):
                ready(i)
            attend_kernel(features, n > 6, *buffers, out_ref)
            pltpu.make_async_copy(out_ref, out_hbm, sem.at[0]).start()

        output_kernel(
            layer,
            width,
            attend,
            starts_ref,
            out_ref,
            o_hbm,
            outs,
            refs[2 * n + 7 : 2 * n + 9],
            *refs[2 * n + 9 :],
        )
        pltpu.make_async_copy(out_ref, out_hbm, sem.at[0]).wait()

    attended = jax.ShapeDtypeStruct((rows, depth), jnp.bfloat16)
    attended, sent, kept = call(
        kernel,
        [attended] + [jax.ShapeDtypeStruct((rows, count), jnp.bfloat16)] * 2,
        8 * rows * rows * depth + 4 * rows * depth * count,
        4 * depth * count,
        "attention_output",
        vmem=36 * MIB,
        in_specs=[in_smem] + [in_hbm] * (n + 1),
        out_specs=[in_hbm] * 3,
        scratch_shapes=buffers_of(operands)
        + buffers_of([attended])
        + output_scratch(rows, depth, count, 1, width),
    )(starts, *operands, o_weight)
    return attended, [sent], kept


def add_kernel(n_parts, *refs):
    inputs, out_hbm, buffers = refs[: n_parts + 1], refs[n_parts + 1], refs[n_parts + 2 : -3]
    in_sem, out_ref, out_sem = refs[-3:]
    ready = fetch(inputs, buffers, in_sem)
    ready(n_parts)
    kept_ref = buffers[n_parts]
    leaving = []
    for i in range(n_parts):
        ready(i)
        width = buffers[i].shape[1]
        columns = slice(i * width, (i + 1) * width)
        total = kept_ref[:, columns].astype(jnp.float32) + buffers[i][...].astype(jnp.float32)
        out_ref[:, columns] = total.astype(out_ref.dtype)
        leaving.append(
            pltpu.make_async_copy(out_ref.at[:, columns], out_hbm.at[:, columns], out_sem.at[i])
        )
        leaving[-1].start()
    for copy_out in leaving:
        copy_out.wait()


def add_parts(kept, parts):
    n = len(parts)
    return call(
        lambda *refs: add_kernel(n, *refs),
        jax.ShapeDtypeStruct(kept.shape, kept.dtype),
        kept.size,
        6 * kept.size,
        "chip_sum",
        in_specs=[in_hbm] * (n + 1),
        out_specs=in_hbm,
        scratch_shapes=buffers_of(list(parts) + [kept])
        + [pltpu.VMEM(kept.shape, kept.dtype), pltpu.SemaphoreType.DMA((n,))],
    )(*parts, kept)


def combine_kernel(n_in, n_out, parts, *refs):
    inputs, outs = refs[:n_in], refs[n_in : n_in + n_out]
    in_bufs, out_bufs = refs[n_in + n_out : 2 * n_in + n_out], refs[2 * n_in + n_out : -2]
    in_sem, out_sem = refs[-2:]
    width = outs[0].shape[1] // parts
    columns = [slice(part * width, (part + 1) * width) for part in range(parts)]
    coming = [
        [
            pltpu.make_async_copy(
                inputs[i].at[:, columns[part]], in_bufs[i].at[:, columns[part]], in_sem.at[i, part]
            )
            for i in range(n_in)
        ]
        for part in range(parts)
    ]
    for copies in coming:
        for copy in copies:
            copy.start()
    leaving = []
    for part in range(parts):
        for copy in coming[part]:
            copy.wait()
        values = [buf[:, columns[part]].astype(jnp.float32) for buf in in_bufs]
        total = values[-1]
        for value in values[-2::-1]:
            total = value + total
        for i in range(n_out):
            out_bufs[i][:, columns[part]] = total.astype(out_bufs[i].dtype)
            leaving.append(
                pltpu.make_async_copy(
                    out_bufs[i].at[:, columns[part]], outs[i].at[:, columns[part]], out_sem.at[i, part]
                )
            )
            leaving[-1].start()
    for copy in leaving:
        copy.wait()


def combine(inputs, dtypes, parts=4):
    shape = inputs[0].shape
    return call(
        lambda *refs: combine_kernel(len(inputs), len(dtypes), parts, *refs),
        [jax.ShapeDtypeStruct(shape, dtype) for dtype in dtypes],
        inputs[0].size * len(inputs),
        sum(array.nbytes for array in inputs) + 4 * inputs[0].size,
        "combine",
        in_specs=[in_hbm] * len(inputs),
        out_specs=[in_hbm] * len(dtypes),
        scratch_shapes=[pltpu.VMEM(shape, array.dtype) for array in inputs]
        + [pltpu.VMEM(shape, dtype) for dtype in dtypes]
        + [
            pltpu.SemaphoreType.DMA((len(inputs), parts)),
            pltpu.SemaphoreType.DMA((len(dtypes), parts)),
        ],
    )(*inputs)


def rope_tables(positions):
    half_depth = HEAD_DIM // 2
    inv_freq = rope_base ** (-2.0 * jnp.arange(half_depth, dtype=jnp.float32) / HEAD_DIM)
    angles = positions[:, None] * inv_freq[None, :]
    cosine, sine = jnp.cos(angles), jnp.sin(angles)
    return jnp.concatenate([cosine, cosine], axis=1), jnp.concatenate([-sine, sine], axis=1)


def normalize(rows):
    center = rows - jnp.mean(rows, axis=1, keepdims=True)
    factor = lax.rsqrt(jnp.mean(center * center, axis=1, keepdims=True) + ln_eps)
    return center * factor, factor


def norm_kernel(count_ref, gain_ref, shift_ref, patch_ref, out_ref):
    owners, padded, in_share = out_ref.shape
    slots = patch_ref.shape[0]
    vit = gain_ref.shape[0]
    gain = gain_ref[...].astype(jnp.float32).reshape(1, vit)
    shift = shift_ref[...].astype(jnp.float32).reshape(1, vit)
    counts = jnp.full((padded - slots, vit), count_ref[0].astype(jnp.float32))
    for group in range(patch_ref.shape[1] // vit):
        rows = patch_ref[:, group * vit : (group + 1) * vit].astype(jnp.float32)
        scaled = normalize(rows)[0] * gain + shift
        scaled = jnp.concatenate([scaled, counts], axis=0).astype(out_ref.dtype)
        for i in range(vit // in_share):
            out_ref[group * (vit // in_share) + i] = scaled[:, i * in_share : (i + 1) * in_share]


def norm_back_kernel(patch_ref, grads_ref, gain_ref, out_ref):
    _, _, in_share = grads_ref.shape
    slots = patch_ref.shape[0]
    vit = gain_ref.shape[0]
    gain = gain_ref[...].astype(jnp.float32).reshape(1, vit)
    per_group = vit // in_share
    for group in range(patch_ref.shape[1] // vit):
        rows = patch_ref[:, group * vit : (group + 1) * vit].astype(jnp.float32)
        unit, factor = normalize(rows)
        grads = jnp.concatenate(
            [grads_ref[group * per_group + i].astype(jnp.float32) for i in range(per_group)], axis=1
        )[:slots]
        grads = grads * gain
        along = jnp.mean(grads * unit, axis=1, keepdims=True)
        out_ref[:, group * vit : (group + 1) * vit] = factor * (
            grads - jnp.mean(grads, axis=1, keepdims=True) - unit * along
        )


def split_kernel(core_ref, rows_ref, out_ref):
    owners, part_rows, width = out_ref.shape
    slots = rows_ref.shape[0]
    first = core_ref[0] == 0
    for owner in range(owners):
        rows = rows_ref[:, owner * width : (owner + 1) * width].astype(jnp.float32)
        rest = jnp.zeros((2 * part_rows - slots, width), jnp.float32)
        rows = jnp.concatenate([rows, rest], axis=0)
        rows = jnp.where(first, rows[:part_rows], rows[part_rows:])
        out_ref[owner] = rows.astype(out_ref.dtype)


def pack_kernel(slots, rows_ref, weight_ref, out_ref, pack_ref):
    owners, padded, _ = rows_ref.shape
    packed_rows = out_ref.shape[0]
    row = lax.broadcasted_iota(jnp.int32, (packed_rows, padded), 0).astype(jnp.float32)
    slot = lax.broadcasted_iota(jnp.int32, (packed_rows, padded), 1).astype(jnp.float32)
    offset = jnp.zeros((1, 1), jnp.float32)
    packed = jnp.zeros((packed_rows, rows_ref.shape[2]), jnp.float32)
    for owner in range(owners):
        rows = rows_ref[owner]
        count = rows.astype(jnp.float32)[slots : slots + 1, 0:1]
        chosen = jnp.where((row == offset + slot) & (slot < count), 1.0, 0.0).astype(jnp.bfloat16)
        pack_ref[owner] = chosen
        packed = packed + jnp.dot(chosen, rows, preferred_element_type=jnp.float32)
        offset = offset + count
    out_ref[...] = jnp.dot(
        packed.astype(jnp.bfloat16), weight_ref[...], preferred_element_type=jnp.float32
    ).astype(out_ref.dtype)


def pack_grads_kernel(core_ref, mine_ref, other_ref, pack_ref, weight_ref, out_ref):
    packed = jnp.zeros((out_ref.shape[0], mine_ref.shape[2]), jnp.float32)
    first = core_ref[0] == 0
    padded = pack_ref.shape[2]
    for owner in range(mine_ref.shape[0]):
        mine = mine_ref[owner].astype(jnp.float32)
        other = other_ref[owner].astype(jnp.float32)
        rows = jnp.concatenate(
            [jnp.where(first, mine, other), jnp.where(first, other, mine)], axis=0
        )
        packed = packed + jnp.dot(
            pack_ref[owner],
            rows[:padded].astype(jnp.bfloat16),
            preferred_element_type=jnp.float32,
        )
    out_ref[...] = lax.dot_general(
        packed.astype(jnp.bfloat16),
        weight_ref[...],
        (((1,), (1,)), ((), ())),
        preferred_element_type=jnp.float32,
    ).astype(out_ref.dtype)


def halves_kernel(core_ref, rows_ref, weight_ref, kept_ref, sent_ref):
    product = jnp.dot(rows_ref[...], weight_ref[...], preferred_element_type=jnp.float32)
    half = kept_ref.shape[1]
    first = core_ref[0] == 0
    kept_ref[...] = jnp.where(first, product[:, :half], product[:, half:])
    sent_ref[...] = jnp.where(first, product[:, half:], product[:, :half]).astype(sent_ref.dtype)


def unpack_kernel(first_ref, second_ref, pack_ref, out_ref):
    total = first_ref[...].astype(jnp.float32) + second_ref[...].astype(jnp.float32)
    total = total.astype(jnp.bfloat16)
    for owner in range(pack_ref.shape[0]):
        out_ref[owner] = lax.dot_general(
            pack_ref[owner], total, (((0,), (0,)), ((), ())), preferred_element_type=jnp.float32
        ).astype(out_ref.dtype)


def assemble_kernel(core_ref, shift_ref, mine_hbm, other_hbm, out_ref, mine_ref, other_ref, sem):
    owners, _, half = mine_ref.shape
    first = core_ref[0] == 0
    ready = fetch([mine_hbm, other_hbm], [mine_ref, other_ref], sem)
    ready(0)
    ready(1)
    for owner in range(owners):
        mine = mine_ref[owner].astype(jnp.float32)
        other = other_ref[owner].astype(jnp.float32)
        for i in range(2):
            columns = slice((2 * owner + i) * half, (2 * owner + i + 1) * half)
            part = jnp.where(first, mine, other) if i == 0 else jnp.where(first, other, mine)
            out_ref[:, columns] = (part + shift_ref[:, columns]).astype(out_ref.dtype)


def exchange(values):
    return lax.all_to_all(values, "dp", split_axis=0, concat_axis=0, tiled=True)


def four_chip_local(
    patches,
    ln_gain,
    ln_shift,
    w_in,
    b_in,
    w_out,
    b_out,
    place,
    image_counts,
    text_rows,
    segments,
    norm_gain,
    q_weight,
    kv_weight,
    o_weight,
    grad_rows,
):
    bf16, f32 = jnp.bfloat16, jnp.float32
    shape_of = jax.ShapeDtypeStruct
    me = lax.axis_index("sec")
    core, chip = me & 1, me >> 1
    core_word = core.reshape(1).astype(jnp.int32)
    owners = lax.axis_size("dp")
    slots = patches.shape[0]
    padded = slots + 16 - slots % 16
    tokens, share = text_rows.shape
    features = share * 4
    layers = q_weight.shape[0]
    in_share, hidden_share = w_in.shape
    out_share = w_out.shape[1]
    packed_rows = owners * (tokens // 16)
    chunk = packed_rows // owners

    normed = call(
        norm_kernel,
        shape_of((owners, padded, in_share), bf16),
        slots * owners * in_share * 10,
        slots * owners * in_share * 4,
        "normed_patches",
        in_specs=[in_smem] + in_vmem(3),
    )(image_counts, ln_gain, ln_shift, patches)
    received = exchange(normed)

    text_rows = after(text_rows, normed)
    far = swap(text_rows, "sec", ACROSS)
    gathered_text = [text_rows, swap(text_rows, "sec", CORE)]
    gains = norm_gain.astype(f32)
    starts = jnp.stack([(me ^ r) * share for r in range(4)]).astype(jnp.int32)
    projected = project(gathered_text, starts[:2], gains, q_weight, kv_weight, 0, None)
    received, projected = lax.optimization_barrier((received, projected))
    far = after(far, received)
    gathered_text += [far, swap(far, "sec", CORE)]
    pre_part, pack = call(
        lambda *refs: pack_kernel(slots, *refs),
        [shape_of((packed_rows, hidden_share), bf16), shape_of((owners, packed_rows, padded), bf16)],
        2 * packed_rows * in_share * hidden_share,
        2 * in_share * hidden_share,
        "pre_act",
    )(received, w_in)
    pre_parts = exchange(pre_part.reshape(owners, chunk, hidden_share))

    shift = after(b_out, received).reshape(1, share)
    shift_far = swap(shift, "sec", ACROSS)
    shifts = [shift, swap(shift, "sec", CORE), shift_far, swap(shift_far, "sec", CORE)]
    shifts = jnp.take(jnp.concatenate(shifts, axis=0), jnp.arange(4, dtype=jnp.int32) ^ me, axis=0)
    shifts = shifts.astype(f32).reshape(1, -1)
    allowed, positions = doc_mask(segments[0])
    bias = jnp.where(allowed, 0.0, -1e30).astype(f32)
    cosine, sine = rope_tables(positions)
    projected = project(gathered_text[2:], starts[2:], gains, q_weight, kv_weight, 0, projected)
    pre_act = jnp.sum(pre_parts.astype(f32), axis=0) + b_in.astype(f32)
    hidden_units = gelu_exact(pre_act).astype(bf16)
    hidden_all = exchange(jnp.broadcast_to(hidden_units[None], (owners, chunk, hidden_share)))
    slot_index = jnp.arange(padded, dtype=jnp.int32)
    token_index = jnp.arange(tokens, dtype=jnp.int32)
    places = jnp.pad(place, (0, padded - slots))
    select = (places[None, :] == token_index[:, None]) & (slot_index < image_counts[0])[None, :]
    is_image = jnp.any(select, axis=1)

    hidden_all, projected, cosine, sine, bias, shifts = lax.optimization_barrier(
        (hidden_all, projected, cosine, sine, bias, shifts)
    )
    kept, sent = call(
        halves_kernel,
        [
            shape_of((packed_rows, out_share // 2), f32),
            shape_of((packed_rows, out_share // 2), bf16),
        ],
        2 * packed_rows * out_share * hidden_share,
        2 * out_share * hidden_share,
        "merged",
        in_specs=[in_smem] + in_vmem(2),
    )(core_word, hidden_all.reshape(packed_rows, hidden_share), w_out)
    chip_sum = (kept + swap(sent, "sec", CORE).astype(f32)).astype(bf16)

    def unpack(first, second):
        width = first.shape[1]
        return exchange(
            call(
                unpack_kernel,
                shape_of((owners, padded, width), bf16),
                2 * packed_rows * owners * padded * width,
                2 * owners * padded * width,
                "unpack",
            )(first, second, pack)
        )

    merged_half = unpack(chip_sum, swap(chip_sum, "sec", ACROSS))
    image_rows = call(
        assemble_kernel,
        shape_of((padded, features), bf16),
        padded * features,
        padded * features * 4,
        "image_rows",
        in_specs=[in_smem] + in_vmem(1) + [in_hbm] * 2,
        scratch_shapes=buffers_of([merged_half] * 2),
    )(core_word, shifts, merged_half, swap(merged_half, "sec", CORE))

    def column(chip_index, core_bit):
        return (2 * chip_index + core_bit) * share

    images = project(
        [image_rows], jnp.zeros((1,), jnp.int32), gains, q_weight, kv_weight, 0, None
    )

    def start_rows(r):
        image_part = lax.dynamic_slice_in_dim(image_rows, column(chip ^ r, core), share, 1)
        picked = jnp.dot(select.astype(bf16), image_part, preferred_element_type=f32)
        return jnp.where(is_image[:, None], picked.astype(bf16), gathered_text[2 * r])

    def columns_of(r):
        return jnp.stack([column(chip ^ r, core ^ 1), column(chip ^ r, core)]).astype(
            jnp.int32
        )

    def shared(sent):
        return [swap(part, "sec", CORE) for part in sent]

    grad_rows = after(grad_rows, merged_half)
    grad_parts = call(
        split_kernel,
        shape_of((owners, (padded + 16) // 32 * 16, out_share), bf16),
        slots * owners * out_share,
        slots * owners * out_share * 4,
        "split_grads",
        in_specs=[in_smem] + in_vmem(1),
    )(core_word, grad_rows)
    grads_there = exchange(grad_parts)

    def grads_first():
        grad_part = call(
            pack_grads_kernel,
            shape_of((packed_rows, hidden_share), bf16),
            2 * packed_rows * out_share * hidden_share,
            2 * out_share * hidden_share,
            "hidden_grads",
            in_specs=[in_smem] + in_vmem(4),
        )(core_word, grads_there, swap(grads_there, "sec", CORE), pack, w_out)
        return grad_part.reshape(owners, chunk, hidden_share)

    def grads_second(parts):
        hidden_grads = jnp.sum(parts.astype(f32), axis=0)
        _, pull_gelu = jax.vjp(gelu_exact, pre_act)
        pre_grads = pull_gelu(hidden_grads)[0].astype(bf16)
        return jnp.broadcast_to(pre_grads[None], (owners, chunk, hidden_share))

    def grads_third(pre_grads):
        back = lax.dot_general(
            pre_grads.reshape(packed_rows, hidden_share),
            w_in,
            (((1,), (1,)), ((), ())),
            preferred_element_type=f32,
        )
        return (back + swap(back, "sec", CORE)).astype(bf16)

    operands = list(projected) + [cosine, sine, bias] + list(images) + [select.astype(f32)]

    def partly(old, rows, r, layer):
        here = jnp.stack([column(chip ^ r, core), column(chip ^ r, core ^ 1)])
        return project(
            [rows, swap(rows, "sec", CORE)],
            here.astype(jnp.int32),
            gains,
            q_weight,
            kv_weight,
            layer,
            old,
        )

    grads, held = None, None
    for layer in range(1, layers):
        attended, sent, kept = attention_output(
            features, operands, o_weight, layer - 1, columns_of(1), share
        )
        other_sum = add_parts(kept, shared(sent))
        attended = after(attended, other_sum)
        came_here = swap(other_sum, "sec", ACROSS)
        sent, kept = output_product(attended, o_weight, layer - 1, columns_of(0), share, 4)
        own_sum = add_parts(kept, shared(sent))
        if held is None:
            held = [start_rows(0), start_rows(1)]
        if grads is None:
            grads_there = after(grads_there, own_sum)
            grads = grads_first()
            came_here = after(came_here, grads)
            grads = exchange(grads_second(exchange(grads)))
        came_here = after(came_here, own_sum)
        came_there = swap(own_sum, "sec", ACROSS)
        now = held[0].astype(f32) + (own_sum.astype(f32) + came_here.astype(f32))
        rounded = now.astype(bf16)
        projected = partly(None, rounded, 0, layer)
        if layer == 1:
            grads = grads_third(grads)
        came_there = after(came_there, (projected, held[1]))
        (there,) = combine([held[1], other_sum, came_there], [bf16])
        projected = partly(projected, there, 1, layer)
        held = [now, there]
        operands = list(projected) + [cosine, sine, bias]

    if layers == 1:
        held = [start_rows(0)]
        grads = grads_third(exchange(grads_second(exchange(grads_first()))))
    back = grads
    back_far = swap(back, "sec", ACROSS)
    operands = after(operands, back_far)

    last = layers - 1
    attended, sent, kept = attention_output(
        features, operands, o_weight, last, columns_of(1), share
    )
    other_sum = add_parts(kept, shared(sent))
    attended = after(attended, other_sum)
    back_far = after(back_far, other_sum)
    came = swap(other_sum, "sec", ACROSS)
    normed_grads = unpack(back, back_far)
    sent, kept = output_product(attended, o_weight, last, columns_of(0), share, 4)
    own_sum = add_parts(kept, shared(sent))
    patch_grads = call(
        norm_back_kernel,
        shape_of(patches.shape, f32),
        slots * owners * in_share * 10,
        slots * owners * in_share * 8,
        "patch_grads",
    )(patches, normed_grads, ln_gain)
    came, own_sum, patch_grads = lax.optimization_barrier((came, own_sum, patch_grads))
    return combine([held[0], own_sum, came], [f32])[0], patch_grads


def local(
    patches,
    ln_gain,
    ln_shift,
    w_in,
    b_in,
    w_out,
    b_out,
    place,
    image_counts,
    text_rows,
    segments,
    norm_gain,
    q_weight,
    kv_weight,
    o_weight,
    grad_rows,
):
    slot_count = patches.shape[0]
    tokens, share = text_rows.shape
    slot_index = jnp.arange(slot_count, dtype=jnp.int32)
    live_slot = slot_index < image_counts[0]
    merged, patch_grads = merger_rows(
        patches,
        ln_gain,
        ln_shift,
        w_in,
        b_in,
        w_out,
        live_slot,
        image_counts[0],
        grad_rows,
        lax.axis_size("dp") * (tokens // 16),
    )
    merged_local = lax.dynamic_slice_in_dim(
        merged, lax.axis_index(("sec", "mp")) * share, share, 1
    ).astype(jnp.float32)
    merged_local = (merged_local + b_out.astype(jnp.float32)).astype(jnp.bfloat16)
    token_index = jnp.arange(tokens, dtype=jnp.int32)
    select = (place[:, None] == token_index[None, :]) & live_slot[:, None]
    is_image = jnp.any(select, axis=0)
    picked = lax.dot_general(
        select.astype(jnp.bfloat16),
        merged_local,
        (((0,), (0,)), ((), ())),
        preferred_element_type=jnp.float32,
    )
    start_rows = jnp.where(is_image[:, None], picked, text_rows.astype(jnp.float32)).astype(
        jnp.bfloat16
    )
    allowed, positions = doc_mask(segments[0])
    layer_count = q_weight.shape[0]
    current = start_rows.astype(jnp.float32)
    for layer_index in range(layer_count):
        current = section_features(
            current,
            norm_gain[layer_index],
            allowed,
            positions,
            q_weight[layer_index],
            kv_weight[layer_index],
            o_weight[layer_index],
        )
    return (current, patch_grads)


def solution(mesh):
    in_specs = (
        P("dp", None),
        P(),
        P(),
        P("dp", ("sec", "mp")),
        P(("sec", "mp")),
        P(("sec", "mp"), "dp"),
        P(("sec", "mp")),
        P("dp"),
        P("dp"),
        P("dp", ("sec", "mp")),
        P("dp", None),
        P(),
        P(None, None, ("sec", "mp")),
        P(None, None, ("sec", "mp"), None),
        P(None, ("sec", "mp"), None),
        P("dp", None),
    )
    out_specs = (P("dp", ("sec", "mp")), P("dp", None))
    step = four_chip_local if mesh.shape["sec"] == 4 and mesh.shape["mp"] == 1 else local
    return jax.shard_map(step, mesh=mesh, in_specs=in_specs, out_specs=out_specs, check_vma=False)
```
